32 devices in a mesh: dp: 4 (over y, x), tm: 4 (over z), height: 2 (over core).
Axes of the slice: x: 2, y: 2, z: 4, core: 2. Of those that a mesh axis runs over, the one named last changes fastest.
Arguments:
- video: bfloat16 [4, 8, 8, 64, 256], P('dp', 'tm', 'height'), may hold values from -6 to 6
- lengths: int32 [4], P('dp'), may hold values from 1 to 8
- enc_weight: bfloat16 [3, 3, 3, 256, 256], replicated, may hold values from -0.078125 to 0.078125
- dec_weight: bfloat16 [3, 3, 3, 256, 256], replicated, may hold values from -0.078125 to 0.078125
- cotangent: bfloat16 [4, 8, 8, 64, 256], P('dp', 'tm', 'height'), may hold values from -6 to 6
Outputs:
- output: bfloat16 [4, 8, 8, 64, 256], P('dp', 'tm', 'height')
- enc_grad: float32 [3, 3, 3, 256, 256], replicated
- dec_grad: float32 [3, 3, 3, 256, 256], replicated
The draws below stay inside these ranges and needn't reach their ends.
All inputs are finite; a program needn't handle non-finite values.
Results may differ from the reference program's by a relative error of at most 0.0045.
Values may be sent and summed in bfloat16 or wider, within the bound.
A program may use at most 128 MiB of HBM per device.

```python
import jax
import jax.numpy as jnp
from jax import lax

C = 256
COLS = 64
CLIPS = 4
FRAMES = 8
ROWS = 8


def set_ends(drawn, own_key, low, high):
    place = [jax.random.randint(jax.random.fold_in(own_key, axis), (), 0, length) for axis, length in enumerate(drawn.shape)]
    longest = drawn.shape.index(max(drawn.shape))
    beside = place[:longest] + [(place[longest] + 1) % drawn.shape[longest]] + place[longest + 1:]
    return drawn.at[tuple(place)].set(low).at[tuple(beside)].set(high)


def shard_levels(rng, extent, shards, smallest, largest):
    def one(axis_at, shards_of):
        draws = jax.random.uniform(jax.random.fold_in(jax.random.fold_in(rng, 6), axis_at), (shards_of,), jnp.float32, smallest / len(shards), largest / len(shards))
        return jnp.repeat(jnp.exp(draws), extent[axis_at] // shards_of).reshape((-1,) + (1,) * (len(extent) - axis_at - 1))

    gain = one(*shards[0])
    for cut in shards[1:]:
        gain = gain * one(*cut)
    return gain


def gaussian(key, extent, spread, reach, split=(), kind=jnp.bfloat16):
    array = spread * jax.random.normal(key, extent, jnp.float32)
    if split:
        array = array * shard_levels(key, extent, split, -0.22, 0.18)
    return jnp.clip(array, -reach, reach).astype(kind)


def setup_inputs(seed: int = 0) -> dict:
    seeds = jax.random.split(jax.random.key(seed), 6)
    return {
        "video": gaussian(seeds[0], (CLIPS, FRAMES, ROWS, COLS, C), 1.0, 6.0, ((0, 4), (1, 4), (2, 2))),
        "lengths": set_ends(jax.random.randint(seeds[1], (CLIPS,), 1, FRAMES + 1), jax.random.fold_in(seeds[1], 1), 1, FRAMES).astype(jnp.int32),
        "enc_weight": gaussian(seeds[2], (3, 3, 3, C, C), (27 * C) ** -0.5, 0.078125),
        "dec_weight": gaussian(seeds[3], (3, 3, 3, C, C), (27 * C) ** -0.5, 0.078125),
        "cotangent": gaussian(seeds[4], (CLIPS, FRAMES, ROWS, COLS, C), 1.0, 6.0, ((0, 4), (1, 4), (2, 2))),
    }


def apply_taps(ext, weight):
    count, frame_pad, row_pad, wide, chans = ext.shape
    frames = frame_pad - 2
    rows = row_pad - 2
    outs = weight.shape[-1]
    padded = jnp.pad(ext, ((0, 0), (0, 0), (0, 0), (1, 1), (0, 0)))
    stacked = jnp.concatenate([padded[:, :, :, e:e + wide, :] for e in range(3)], axis=-1)
    total = jnp.zeros((count * frames * rows * wide, outs), jnp.float32)
    for a in range(3):
        for b in range(3):
            slab = stacked[:, a:a + frames, b:b + rows].reshape(-1, 3 * chans)
            total = total + jnp.dot(slab, weight[a, b].reshape(3 * chans, outs), preferred_element_type=jnp.float32)
    return total.reshape(count, frames, rows, wide, outs)


def tap_grads(ext, cot):
    count, frame_pad, row_pad, wide, chans = ext.shape
    frames = frame_pad - 2
    rows = row_pad - 2
    outs = cot.shape[-1]
    padded = jnp.pad(ext, ((0, 0), (0, 0), (0, 0), (1, 1), (0, 0)))
    stacked = jnp.concatenate([padded[:, :, :, e:e + wide, :] for e in range(3)], axis=-1)
    flat = cot.reshape(-1, outs)
    result = []
    for a in range(3):
        for b in range(3):
            slab = stacked[:, a:a + frames, b:b + rows].reshape(-1, 3 * chans)
            result.append(lax.dot_general(slab, flat, (((0,), (0,)), ((), ())), preferred_element_type=jnp.float32))
    return jnp.stack(result).reshape(3, 3, 3, chans, outs)


def dsilu(value):
    sig = jax.nn.sigmoid(value)
    return sig * (1.0 + value * (1.0 - sig))


def reference(video, lengths, enc_weight, dec_weight, cotangent):
    flipped = jnp.transpose(dec_weight[::-1, ::-1, ::-1], (0, 1, 2, 4, 3))

    def one_clip(items):
        frames_in, cot, length = items
        tpos = jnp.arange(FRAMES, dtype=jnp.int32)
        keep = (tpos < length)[:, None, None, None]
        masked = jnp.where(keep, frames_in, jnp.zeros_like(frames_in))[None]
        cot_masked = jnp.where(keep, cot, jnp.zeros_like(cot))[None]
        ext_x = jnp.pad(masked, ((0, 0), (2, 0), (1, 1), (0, 0), (0, 0)))
        pre = apply_taps(ext_x, enc_weight)
        hidden = jax.nn.silu(pre).astype(jnp.bfloat16)
        ext_h = jnp.pad(hidden, ((0, 0), (2, 0), (1, 1), (0, 0), (0, 0)))
        output = (apply_taps(ext_h, dec_weight) + masked.astype(jnp.float32)).astype(jnp.bfloat16)
        ext_g = jnp.pad(cot_masked, ((0, 0), (0, 2), (1, 1), (0, 0), (0, 0)))
        back = apply_taps(ext_g, flipped)
        dpre = (back * dsilu(pre)).astype(jnp.bfloat16)
        return output[0], tap_grads(ext_x, dpre), tap_grads(ext_h, cot_masked)

    output, enc_parts, dec_parts = lax.map(one_clip, (video, cotangent, lengths.astype(jnp.int32)))
    return output, jnp.sum(enc_parts, axis=0), jnp.sum(dec_parts, axis=0)
```

```python
import functools

import jax
import jax.numpy as jnp
from jax import lax
from jax.experimental import pallas as pl
from jax.experimental.pallas import tpu as pltpu
from jax.sharding import PartitionSpec as P

MESH = pl.DeviceIdType.MESH
SLABS = 18
LAG = 2


def extended(shard, sides, width):
    for axis, dim in sides:
        devices, length = (lax.axis_size(axis), shard.shape[dim])
        up = [(i, (i + 1) % devices) for i in range(devices - 1)]
        down = [(j, i) for i, j in up]
        last = lax.slice_in_dim(shard, length - width, length, axis=dim)
        leading = lax.slice_in_dim(shard, 0, width, axis=dim)
        before = lax.ppermute(last, axis, up)
        after = lax.ppermute(leading, axis, down)
        shard = jnp.concatenate([before, shard, after], axis=dim)
    return shard


def from_behind(block, axis, distance):
    devices = range(lax.axis_size(axis))
    route = [(i - distance, i) for i in devices if i - distance in devices]
    return lax.ppermute(block, axis, route)


def apply_taps(ext, weight, transposed=False):
    count, frame_pad, row_pad, wide, chans = ext.shape
    frames = frame_pad - 2
    rows = row_pad - 2
    outs = weight.shape[2] if transposed else weight.shape[-1]
    padded = jnp.pad(ext, ((0, 0), (0, 0), (0, 0), (1, 1), (0, 0)))
    stacked = jnp.concatenate([padded[:, :, :, e : e + wide, :] for e in range(3)], axis=-1)
    total = jnp.zeros((count * frames * rows * wide, outs), jnp.float32)
    for a in range(3):
        for b in range(3):
            slab = stacked[:, a : a + frames, b : b + rows].reshape(-1, 3 * chans)
            if transposed:
                total = total + lax.dot_general(
                    slab, weight[a, b], (((1,), (1,)), ((), ())), preferred_element_type=jnp.float32
                )
                continue
            total = total + jnp.dot(
                slab, weight[a, b].reshape(3 * chans, outs), preferred_element_type=jnp.float32
            )
    return total.reshape(count, frames, rows, wide, outs)


def tap_grads(ext, cot):
    count, frame_pad, row_pad, wide, chans = ext.shape
    frames = frame_pad - 2
    rows = row_pad - 2
    outs = cot.shape[-1]
    padded = jnp.pad(ext, ((0, 0), (0, 0), (0, 0), (1, 1), (0, 0)))
    stacked = jnp.concatenate([padded[:, :, :, e : e + wide, :] for e in range(3)], axis=-1)
    flat = cot.reshape(-1, outs)
    result = []
    for a in range(3):
        for b in range(3):
            slab = stacked[:, a : a + frames, b : b + rows].reshape(-1, 3 * chans)
            result.append(
                lax.dot_general(
                    slab, flat, (((0,), (0,)), ((), ())), preferred_element_type=jnp.float32
                )
            )
    return jnp.stack(result).reshape(3, 3, 3, chans, outs)


def dsilu(value):
    sig = jax.nn.sigmoid(value)
    return sig * (1.0 + value * (1.0 - sig))


def row_edges(block):
    return extended(block, (("height", 2),), 1)


def with_earlier(block):
    before = from_behind(block, "tm", 1)
    return row_edges(jnp.concatenate([before, block], axis=1))


def with_later(block):
    after = from_behind(block, "tm", -1)
    return row_edges(jnp.concatenate([block, after], axis=1))


def index_bits(axis):
    size = lax.axis_size(axis)
    bits = []
    step = 1
    while step < size:
        bits.append((axis, step))
        step *= 2
    return bits


def swap(block, axis, step):
    return lax.ppermute(block, axis, [(i, i ^ step) for i in range(lax.axis_size(axis))])


def sum_part(part, order):
    trail = []
    for dim, (axis, step) in order:
        upper = lax.rem(lax.axis_index(axis) // step, 2) == 1
        low, high = jnp.split(part, 2, axis=dim)
        keep, give = jnp.where(upper, high, low), jnp.where(upper, low, high)
        got = swap(give.astype(jnp.bfloat16), axis, step)
        part = keep + got.astype(jnp.float32)
        trail.append((dim, axis, step, upper))
    part = part.astype(jnp.bfloat16)
    for dim, axis, step, upper in trail[::-1]:
        got = swap(part, axis, step)
        part = jnp.concatenate([jnp.where(upper, got, part), jnp.where(upper, part, got)], axis=dim)
    return part.astype(jnp.float32)


def sum_all(grad):
    height, dp, tm = index_bits("height"), index_bits("dp"), index_bits("tm")
    rest = height[1:]
    flat = grad.reshape(27, -1, grad.shape[-1])
    sums = []
    at = 0
    for count, order in ((10, dp + tm + rest), (10, dp[::-1] + tm + rest), (7, tm + dp + rest)):
        part = flat[at : at + count]
        at += count
        sums.append(sum_part(part, [(2, height[0])] + [(1, bit) for bit in order]))
    return jnp.concatenate(sums, axis=0).reshape(grad.shape)


def sum_kernel(g, out, buf, r0, r1, r2, rz, ssem, rsem):
    d, t, h = lax.axis_index("dp"), lax.axis_index("tm"), lax.axis_index("height")
    xbit, ybit = d % 2, d // 2
    core = (d, t, 1 - h)

    def places(s):
        odd = s % 2
        f1 = jnp.where(odd == 1, ybit, xbit)
        f2 = jnp.where(odd == 1, xbit, ybit)
        xd, yd = d + 1 - 2 * xbit, d + 2 - 4 * ybit
        p1 = (jnp.where(odd == 1, yd, xd), t, h)
        p2 = (jnp.where(odd == 1, xd, yd), t, h)
        return f1, f2, p1, p2

    def zpart(step):
        other = (t + step) % 4
        return other, 16 * (other // 2), 128 * (other % 2)

    def copy(s, slot, src, dst, target):
        return pltpu.make_async_remote_copy(
            src_ref=src,
            dst_ref=dst,
            send_sem=ssem.at[s, slot],
            recv_sem=rsem.at[s, slot],
            device_id=target,
            device_id_type=MESH,
        )

    def rows(ref, s, first, count):
        return ref.at[s, :, pl.ds(pl.multiple_of(first, 16), count)]

    def tile(ref, s, first, col):
        return ref.at[s, :, pl.ds(pl.multiple_of(first, 16), 16), pl.ds(pl.multiple_of(col, 128), 128)]

    def c_core(s):
        return copy(s, 0, rows(g, s, 128 * (1 - h), 128), r0.at[s], core)

    def c_first(s):
        f1, f2, p1, p2 = places(s)
        return copy(s, 1, rows(buf, s, 64 * (1 - f1), 64), r1.at[s], p1)

    def c_second(s):
        f1, f2, p1, p2 = places(s)
        return copy(s, 2, rows(buf, s, 64 * f1 + 32 * (1 - f2), 32), r2.at[s], p2)

    def c_z(s, step):
        f1, f2, p1, p2 = places(s)
        other, row, col = zpart(step)
        return copy(s, 2 + step, tile(buf, s, 64 * f1 + 32 * f2 + row, col), rz.at[s, step - 1], (d, other, h))

    def c_zback(s, step):
        f1, f2, p1, p2 = places(s)
        other, _, _ = zpart(step)
        _, row, col = zpart(0)
        here = tile(out, s, 128 * h + 64 * f1 + 32 * f2 + row, col)
        return copy(s, 5 + step, here, here, (d, other, h))

    def c_secondback(s):
        f1, f2, p1, p2 = places(s)
        here = rows(out, s, 128 * h + 64 * f1 + 32 * f2, 32)
        return copy(s, 9, here, here, p2)

    def c_firstback(s):
        f1, f2, p1, p2 = places(s)
        here = rows(out, s, 128 * h + 64 * f1, 64)
        return copy(s, 10, here, here, p1)

    def c_coreback(s):
        here = rows(out, s, 128 * h, 128)
        return copy(s, 11, here, here, core)

    def s0(s):
        c_core(s).start()

    def s1(s):
        c_core(s).wait_recv()
        mine = g[s, :, pl.ds(pl.multiple_of(128 * h, 128), 128)].astype(jnp.float32)
        buf[s] = (mine + r0[s].astype(jnp.float32)).astype(jnp.bfloat16)
        c_first(s).start()

    def s2(s):
        f1, f2, p1, p2 = places(s)
        c_first(s).wait_recv()
        at = pl.ds(pl.multiple_of(64 * f1, 64), 64)
        buf[s, :, at] = (buf[s, :, at].astype(jnp.float32) + r1[s].astype(jnp.float32)).astype(jnp.bfloat16)
        c_second(s).start()

    def s3(s):
        f1, f2, p1, p2 = places(s)
        c_second(s).wait_recv()
        at = pl.ds(pl.multiple_of(64 * f1 + 32 * f2, 32), 32)
        buf[s, :, at] = (buf[s, :, at].astype(jnp.float32) + r2[s].astype(jnp.float32)).astype(jnp.bfloat16)
        for step in (2, 1, 3):
            c_z(s, step).start()

    def s4(s):
        f1, f2, p1, p2 = places(s)
        _, row, col = zpart(0)
        for step in (1, 2, 3):
            c_z(s, step).wait_recv()
        at = pl.ds(pl.multiple_of(64 * f1 + 32 * f2 + row, 16), 16)
        cols = pl.ds(pl.multiple_of(col, 128), 128)
        total = buf[s, :, at, cols].astype(jnp.float32)
        for k in range(3):
            total = total + rz[s, k].astype(jnp.float32)
        out[s, :, pl.ds(pl.multiple_of(128 * h + 64 * f1 + 32 * f2 + row, 16), 16), cols] = total.astype(jnp.bfloat16)
        for step in (2, 1, 3):
            c_zback(s, step).start()

    def s5(s):
        for step in (1, 2, 3):
            c_zback(s, step).wait_recv()
        c_secondback(s).start()

    def s6(s):
        c_secondback(s).wait_recv()
        c_firstback(s).start()

    def s7(s):
        c_firstback(s).wait_recv()
        c_coreback(s).start()

    def s8(s):
        c_coreback(s).wait_recv()

    barrier = pltpu.get_barrier_semaphore()
    partners = [core, (d + 1 - 2 * xbit, t, h), (d + 2 - 4 * ybit, t, h)] + [(d, (t + k) % 4, h) for k in (1, 2, 3)]
    for partner in partners:
        pl.semaphore_signal(barrier, inc=1, device_id=partner, device_id_type=MESH)
    pl.semaphore_wait(barrier, len(partners))

    stages = [s0, s1, s2, s3, s4, s5, s6, s7, s8]

    def body(i, carry):
        for k in range(len(stages) - 1, -1, -1):
            s = i - LAG * k

            @pl.when((s >= 0) & (s < SLABS))
            def _(k=k, s=s):
                stages[k](s)

        return carry

    lax.fori_loop(0, SLABS + LAG * (len(stages) - 1), body, 0)

    def finish(s, carry):
        c_core(s).wait_send()
        c_first(s).wait_send()
        c_second(s).wait_send()
        for step in (1, 2, 3):
            c_z(s, step).wait_send()
            c_zback(s, step).wait_send()
        c_secondback(s).wait_send()
        c_firstback(s).wait_send()
        c_coreback(s).wait_send()
        return carry

    lax.fori_loop(0, SLABS, finish, 0)


def sum_all_kernel(enc_local, dec_local):
    g = jnp.concatenate([x.reshape(9, 3, 256, 256).astype(jnp.bfloat16) for x in (dec_local, enc_local)])
    bf = jnp.bfloat16
    out = pl.pallas_call(
        sum_kernel,
        out_shape=jax.ShapeDtypeStruct(g.shape, bf),
        in_specs=[pl.BlockSpec(memory_space=pltpu.VMEM)],
        out_specs=pl.BlockSpec(memory_space=pltpu.VMEM),
        scratch_shapes=[
            pltpu.VMEM((SLABS, 3, 128, 256), bf),
            pltpu.VMEM((SLABS, 3, 128, 256), bf),
            pltpu.VMEM((SLABS, 3, 64, 256), bf),
            pltpu.VMEM((SLABS, 3, 32, 256), bf),
            pltpu.VMEM((SLABS, 3, 3, 16, 128), bf),
            pltpu.SemaphoreType.DMA((SLABS, 12)),
            pltpu.SemaphoreType.DMA((SLABS, 12)),
        ],
        compiler_params=pltpu.CompilerParams(
            collective_id=0, has_side_effects=True, vmem_limit_bytes=48 * 2**20
        ),
    )(g)
    full = out.astype(jnp.float32)
    return full[9:].reshape(enc_local.shape), full[:9].reshape(dec_local.shape)


def shards(video, lengths, enc_weight, dec_weight, cotangent):
    frames = video.shape[1]
    first_frame = lax.axis_index("tm") * frames
    tpos = first_frame + jnp.arange(frames, dtype=jnp.int32)
    keep = (tpos[None, :] < lengths[:, None])[:, :, None, None, None]
    masked = jnp.where(keep, video, jnp.zeros_like(video))
    cot_masked = jnp.where(keep, cotangent, jnp.zeros_like(cotangent))
    ext_x = with_earlier(masked)
    pre = apply_taps(ext_x, enc_weight)
    hidden = jax.nn.silu(pre).astype(jnp.bfloat16)
    ext_h = with_earlier(hidden)
    output = (apply_taps(ext_h, dec_weight) + masked.astype(jnp.float32)).astype(jnp.bfloat16)
    ext_g = with_later(cot_masked)
    chans = dec_weight.shape[3]
    flipped = jnp.transpose(dec_weight[::-1, ::-1, ::-1], (0, 1, 3, 2, 4)).reshape(3, 3, chans, -1)
    dec_local = tap_grads(ext_h, cot_masked)
    back = apply_taps(ext_g, flipped, True)
    dpre = (back * dsilu(pre)).astype(jnp.bfloat16)
    enc_local = tap_grads(ext_x, dpre)
    if (lax.axis_size("dp"), lax.axis_size("tm"), lax.axis_size("height")) == (4, 4, 2):
        enc_grad, dec_grad = sum_all_kernel(enc_local, dec_local)
    else:
        enc_grad, dec_grad = sum_all(enc_local), sum_all(dec_local)
    return (output, enc_grad, dec_grad)


def solution(mesh):
    in_specs = (
        P("dp", "tm", "height", None, None),
        P("dp"),
        P(),
        P(),
        P("dp", "tm", "height", None, None),
    )
    out_specs = (P("dp", "tm", "height", None, None), P(), P())
    return jax.shard_map(shards, mesh=mesh, in_specs=in_specs, out_specs=out_specs, check_vma=False)
```

```python
import jax
import jax.numpy as jnp
from jax import lax
from jax.experimental import pallas as pl
from jax.experimental.pallas import tpu as pltpu
from jax.sharding import PartitionSpec as P

MESH = pl.DeviceIdType.MESH
LAG = 1


def extended(shard, sides, width):
    for axis, dim in sides:
        devices, length = (lax.axis_size(axis), shard.shape[dim])
        up = [(i, (i + 1) % devices) for i in range(devices - 1)]
        down = [(j, i) for i, j in up]
        last = lax.slice_in_dim(shard, length - width, length, axis=dim)
        leading = lax.slice_in_dim(shard, 0, width, axis=dim)
        before = lax.ppermute(last, axis, up)
        after = lax.ppermute(leading, axis, down)
        shard = jnp.concatenate([before, shard, after], axis=dim)
    return shard


def from_behind(block, axis, distance):
    devices = range(lax.axis_size(axis))
    route = [(i - distance, i) for i in devices if i - distance in devices]
    return lax.ppermute(block, axis, route)


def apply_taps(ext, weight, transposed=False):
    count, frame_pad, row_pad, wide, chans = ext.shape
    frames = frame_pad - 2
    rows = row_pad - 2
    outs = weight.shape[2] if transposed else weight.shape[-1]
    padded = jnp.pad(ext, ((0, 0), (0, 0), (0, 0), (1, 1), (0, 0)))
    stacked = jnp.concatenate([padded[:, :, :, e : e + wide, :] for e in range(3)], axis=-1)
    total = jnp.zeros((count * frames * rows * wide, outs), jnp.float32)
    for a in range(3):
        for b in range(3):
            slab = stacked[:, a : a + frames, b : b + rows].reshape(-1, 3 * chans)
            if transposed:
                total = total + lax.dot_general(
                    slab, weight[a, b], (((1,), (1,)), ((), ())), preferred_element_type=jnp.float32
                )
                continue
            total = total + jnp.dot(
                slab, weight[a, b].reshape(3 * chans, outs), preferred_element_type=jnp.float32
            )
    return total.reshape(count, frames, rows, wide, outs)


def tap_grads(ext, cot):
    count, frame_pad, row_pad, wide, chans = ext.shape
    frames = frame_pad - 2
    rows = row_pad - 2
    outs = cot.shape[-1]
    padded = jnp.pad(ext, ((0, 0), (0, 0), (0, 0), (1, 1), (0, 0)))
    stacked = jnp.concatenate([padded[:, :, :, e : e + wide, :] for e in range(3)], axis=-1)
    flat = cot.reshape(-1, outs)
    result = []
    for a in range(3):
        for b in range(3):
            slab = stacked[:, a : a + frames, b : b + rows].reshape(-1, 3 * chans)
            result.append(
                lax.dot_general(
                    slab, flat, (((0,), (0,)), ((), ())), preferred_element_type=jnp.float32
                )
            )
    return jnp.stack(result).reshape(3, 3, 3, chans, outs)


def dsilu(value):
    sig = jax.nn.sigmoid(value)
    return sig * (1.0 + value * (1.0 - sig))


def row_edges(block):
    return extended(block, (("height", 2),), 1)


def with_earlier(block):
    before = from_behind(block, "tm", 1)
    return row_edges(jnp.concatenate([before, block], axis=1))


def with_later(block):
    after = from_behind(block, "tm", -1)
    return row_edges(jnp.concatenate([block, after], axis=1))


def index_bits(axis):
    size = lax.axis_size(axis)
    bits = []
    step = 1
    while step < size:
        bits.append((axis, step))
        step *= 2
    return bits


def swap(block, axis, step):
    return lax.ppermute(block, axis, [(i, i ^ step) for i in range(lax.axis_size(axis))])


def sum_part(part, order):
    trail = []
    for dim, (axis, step) in order:
        upper = lax.rem(lax.axis_index(axis) // step, 2) == 1
        low, high = jnp.split(part, 2, axis=dim)
        keep, give = jnp.where(upper, high, low), jnp.where(upper, low, high)
        got = swap(give.astype(jnp.bfloat16), axis, step)
        part = keep + got.astype(jnp.float32)
        trail.append((dim, axis, step, upper))
    part = part.astype(jnp.bfloat16)
    for dim, axis, step, upper in trail[::-1]:
        got = swap(part, axis, step)
        part = jnp.concatenate([jnp.where(upper, got, part), jnp.where(upper, part, got)], axis=dim)
    return part.astype(jnp.float32)


def sum_all(grad):
    height, dp, tm = index_bits("height"), index_bits("dp"), index_bits("tm")
    rest = height[1:]
    flat = grad.reshape(27, -1, grad.shape[-1])
    sums = []
    at = 0
    for count, order in ((10, dp + tm + rest), (10, dp[::-1] + tm + rest), (7, tm + dp + rest)):
        part = flat[at : at + count]
        at += count
        sums.append(sum_part(part, [(2, height[0])] + [(1, bit) for bit in order]))
    return jnp.concatenate(sums, axis=0).reshape(grad.shape)

STEPS = 9
F32 = jnp.float32
BF16 = jnp.bfloat16


def step_kernel(
    lengths, video, cot, enc_hbm, dec_hbm, output, out,
    wenc, wdec, xe, ge, he, de, xp, gp, hp, dp, ht, ds, ys, slope,
    yb, keep, give, r1, zb, rz, wsem, hs, hr, ssem, rsem,
):
    d, t, h = lax.axis_index("dp"), lax.axis_index("tm"), lax.axis_index("height")
    frames, tall, wide, chans = video.shape[1:]
    last = lax.axis_size("tm") - 1
    xbit, ybit = d % 2, d // 2
    core = (d, t, 1 - h)
    xdev = (d + 1 - 2 * xbit, t, h)
    ydev = (d + 2 - 4 * ybit, t, h)
    later = (d, lax.rem(t + 1, last + 1), h)
    earlier = (d, lax.rem(t + last, last + 1), h)
    spots = frames * tall * wide
    base = tall * h

    w_enc = pltpu.make_async_copy(enc_hbm, wenc, wsem.at[0])
    w_dec = pltpu.make_async_copy(dec_hbm, wdec, wsem.at[1])
    w_enc.start()
    w_dec.start()

    barrier = pltpu.get_barrier_semaphore()
    partners = [core, xdev, ydev] + [(d, lax.rem(t + k, last + 1), h) for k in range(1, 4)]
    for partner in partners:
        pl.semaphore_signal(barrier, inc=1, device_id=partner, device_id_type=MESH)

    rows = pl.ds(1 + base, tall)
    own_rows = pl.ds(base, tall)

    def half(first):
        return pl.ds(pl.multiple_of(128 * first, 128), 128)

    for f in range(frames):
        live = t * frames + f < lengths[0]
        xe[2 + f, rows] = jnp.where(live, video[0, f], jnp.zeros_like(video[0, f]))
        ge[f, rows] = jnp.where(live, cot[0, f], jnp.zeros_like(cot[0, f]))
    for ref in (xe, ge, he, xp, gp):
        for edge in (0, 9):
            ref[:, edge] = jnp.zeros((4,) + ref.shape[2:], BF16)

    @pl.when(t == 0)
    def _():
        for ref in (xe, he, xp):
            ref[0:2] = jnp.zeros((2,) + ref.shape[1:], BF16)

    @pl.when(t == last)
    def _():
        for ref in (ge, gp):
            ref[2:4] = jnp.zeros((2,) + ref.shape[1:], BF16)

    pl.semaphore_wait(barrier, len(partners))

    def message(slot, src, dst, target):
        return pltpu.make_async_remote_copy(
            src_ref=src,
            dst_ref=dst,
            send_sem=hs.at[slot],
            recv_sem=hr.at[slot],
            device_id=target,
            device_id_type=MESH,
        )

    def same(slot, ref, target):
        return message(slot, ref, ref, target)

    own, ahead = pl.ds(2, 2), pl.ds(0, 2)
    x_core = same(0, xe.at[own, rows], core)
    g_core = same(1, ge.at[ahead, rows], core)
    x_later = message(2, xe.at[own, rows], xe.at[ahead, rows], later)
    g_earlier = message(3, ge.at[ahead, rows], ge.at[own, rows], earlier)
    x_halo_core = same(4, xe.at[ahead, rows], core)
    g_halo_core = same(5, ge.at[own, rows], core)
    xp_own = message(6, xe.at[own, rows, :, half(1 - ybit)], xp.at[own, rows], ydev)
    xp_own_core = same(7, xp.at[own, rows], core)
    xp_halo = message(8, xe.at[ahead, rows, :, half(1 - ybit)], xp.at[ahead, rows], ydev)
    xp_halo_core = same(9, xp.at[ahead, rows], core)
    gp_own = message(10, ge.at[ahead, rows], gp.at[ahead, rows], xdev)
    gp_own_core = same(11, gp.at[ahead, rows], core)
    gp_halo = message(12, ge.at[own, rows], gp.at[own, rows], xdev)
    gp_halo_core = same(13, gp.at[own, rows], core)
    d_core = same(14, de.at[:, own_rows], core)
    d_pair = message(15, de.at[:, own_rows], dp.at[:, own_rows], ydev)
    d_pair_core = same(16, dp.at[:, own_rows], core)
    h_core = same(17, he.at[own, rows], core)
    h_later = message(18, he.at[own, rows], he.at[ahead, rows], later)
    h_halo_core = same(19, he.at[ahead, rows], core)
    h_pair = message(20, he.at[own, rows, :, half(1 - xbit)], hp.at[:, own_rows], xdev)
    h_pair_core = same(21, hp.at[:, own_rows], core)

    def when(cond, action):
        pl.when(cond)(action)

    inner, outer = t > 0, t < last
    when(outer, lambda: x_later.start())
    when(inner, lambda: g_earlier.start())
    x_core.start()
    g_core.start()
    gp_own.start()
    xp_own.start()

    def shifted(value, by):
        count = value.shape[0]
        column = lax.broadcasted_iota(jnp.int32, value.shape, 0) % wide
        moved = pltpu.roll(value, by % count, axis=0)
        return jnp.where(column == (0 if by == 1 else wide - 1), 0.0, moved)

    def partial_conv(src, weight, taps, transposed, fresh):
        for e in range(3):
            total = None
            for a in taps:
                first = 2 - a if transposed else a
                for b in range(3):
                    down = 2 - b if transposed else b
                    slab = src[first : first + 2, pl.ds(base + down, tall)].reshape(spots, chans)
                    dims = (((1,), (1 if transposed else 0,)), ((), ()))
                    term = lax.dot_general(slab, weight[9 * a + 3 * b + e], dims, preferred_element_type=F32)
                    total = term if total is None else total + term
            if fresh:
                ys[e] = total
            else:
                ys[e] = ys[e] + total

    def joined(transposed):
        one = -1 if transposed else 1
        return ys[1] + shifted(ys[0], one) + shifted(ys[2], -one)

    w_enc.wait()
    x_core.wait_recv()
    partial_conv(xe, wenc, (2,), False, True)

    @pl.when(inner)
    def _():
        x_later.wait_recv()
        x_halo_core.start()
        xp_halo.start()
        x_halo_core.wait_recv()

    partial_conv(xe, wenc, (1, 0), False, False)
    pre = joined(False)
    sig = jax.nn.sigmoid(pre)
    hidden = (pre * sig).astype(BF16)
    slope[...] = sig * (1.0 + pre * (1.0 - sig))
    he[2:4, rows] = hidden.reshape(frames, tall, wide, chans)
    h_pair.start()
    h_core.start()
    when(outer, lambda: h_later.start())

    @pl.when(outer)
    def _():
        g_earlier.wait_recv()
        g_halo_core.start()
        gp_halo.start()

    xp_own.wait_recv()
    xp_own_core.start()
    gp_own.wait_recv()
    gp_own_core.start()
    g_core.wait_recv()
    w_dec.wait()
    when(outer, lambda: g_halo_core.wait_recv())
    partial_conv(ge, wdec, (2, 1, 0), True, True)
    de[:, own_rows] = (joined(True) * slope[...]).astype(BF16).reshape(frames, tall, wide, chans)
    d_pair.start()
    d_core.start()

    chip = 2 * spots

    def turned(value, at):
        value = value.astype(F32)
        for e in range(3):
            moved = value if e == 1 else shifted(value, 1 if e == 0 else -1)
            ht[pl.ds(128 * e, 128), pl.ds(at * chip, chip)] = moved.T.astype(BF16)

    h_core.wait_recv()
    turned(he[2:4, 1:9, :, half(xbit)].reshape(chip, 128), 0)
    h_pair.wait_recv()
    h_pair_core.start()

    def forward_gp():
        gp_halo.wait_recv()
        gp_halo_core.start()

    def forward_xp():
        xp_halo.wait_recv()
        xp_halo_core.start()

    when(outer, forward_gp)
    when(inner, forward_xp)
    h_pair_core.wait_recv()
    turned(hp[...].reshape(chip, 128), 1)
    gp_own_core.wait_recv()
    xp_own_core.wait_recv()
    when(outer, lambda: gp_halo_core.wait_recv())
    when(inner, lambda: xp_halo_core.wait_recv())

    def spread(value, at):
        value = value.astype(F32)
        for e in range(3):
            moved = value if e == 1 else shifted(value, -1 if e == 0 else 1)
            ds[at, :, :, :, pl.ds(chans * e, chans)] = moved.astype(BF16).reshape(frames, 8, wide, chans)

    def kind(i, hh):
        enc = jnp.where((i == 2) | (i == 4) | (i == 6) | (i == 7), 1, 0)
        enc = jnp.where(i == 8, hh, enc)
        before = jnp.where(i > 2, 1, 0) + jnp.where(i > 4, 1, 0) + jnp.where(i > 6, 1, 0) + jnp.where(i > 7, 1, 0)
        tap = jnp.where(enc == 1, before + 4 * hh, i - before + 5 * hh)
        return enc, tap

    def places(i):
        enc, tap = kind(i, h)
        f1 = jnp.where(enc == 1, ybit, xbit)
        f2 = jnp.where(enc == 1, xbit, ybit)
        dx, dy = d + 1 - 2 * xbit, d + 2 - 4 * ybit
        p1 = (jnp.where(enc == 1, dy, dx), t, h)
        p2 = (jnp.where(enc == 1, dx, dy), t, h)
        return 9 * enc + tap, f1, f2, p1, p2

    def copy(i, slot, src, dst, target):
        return pltpu.make_async_remote_copy(
            src_ref=src,
            dst_ref=dst,
            send_sem=ssem.at[i, slot],
            recv_sem=rsem.at[i, slot],
            device_id=target,
            device_id_type=MESH,
        )

    def part(ref, i, first, count):
        return ref.at[i, :, pl.ds(pl.multiple_of(first, 16), count)]

    def zmate(k):
        return lax.rem(t + k, last + 1)

    def c_second(i):
        _, _, _, _, p2 = places(i)
        return copy(i, 0, give.at[i], r1.at[i], p2)

    def c_z(i, k):
        other = zmate(k)
        return copy(i, k, part(zb, i, 16 * other, 16), rz.at[i, k - 1], (d, other, h))

    def c_zback(i, k):
        s, f1, f2, _, _ = places(i)
        here = part(out, s, 128 * f1 + 64 * f2 + 16 * t, 16)
        return copy(i, 3 + k, here, here, (d, zmate(k), h))

    def c_secondback(i):
        s, f1, f2, _, p2 = places(i)
        here = part(out, s, 128 * f1 + 64 * f2, 64)
        return copy(i, 7, here, here, p2)

    def c_firstback(i):
        s, f1, _, p1, _ = places(i)
        here = part(out, s, 128 * f1, 128)
        return copy(i, 8, here, here, p1)

    def c_coreback(i, k):
        s, f1, _, _, _ = places(i)
        here = part(out, s, 128 * (f1 if k == 0 else 1 - f1), 128)
        return copy(i, 9 + k, here, here, core)

    def dec_slab(tap):
        a = tap // 3
        b = tap % 3
        total = None
        for at, ref in ((0, ge), (1, gp)):
            slab = ref[pl.ds(2 - a, 2), pl.ds(2 - b, 8)].reshape(chip, chans)
            term = jnp.dot(ht[:, at * chip : (at + 1) * chip], slab, preferred_element_type=F32)
            total = term if total is None else total + term
        for e in range(3):
            yb[e] = total[128 * e : 128 * (e + 1)]

    def enc_slab(tap):
        a = tap // 3
        b = tap % 3
        total = None
        for at in range(2):
            if at == 0:
                slab = xe[pl.ds(a, 2), pl.ds(b, 8), :, half(ybit)]
            else:
                slab = xp[pl.ds(a, 2), pl.ds(b, 8)]
            term = lax.dot_general(
                slab.reshape(chip, 128),
                ds[at].reshape(chip, 3 * chans),
                (((0,), (0,)), ((), ())),
                preferred_element_type=F32,
            )
            total = term if total is None else total + term
        for e in range(3):
            yb[e] = total[:, chans * e : chans * (e + 1)]

    def s0(i):
        enc, tap = kind(i, h)

        @pl.when(i == 2)
        def _():
            d_core.wait_recv()
            spread(de[...].reshape(chip, chans), 0)
            d_pair.wait_recv()
            d_pair_core.start()
            d_pair_core.wait_recv()
            spread(dp[...].reshape(chip, chans), 1)

        @pl.when(enc == 0)
        def _():
            dec_slab(tap)

        @pl.when(enc == 1)
        def _():
            enc_slab(tap)

        _, _, f2, _, _ = places(i)
        keep[i] = yb[:, pl.ds(pl.multiple_of(64 * f2, 64), 64)]
        give[i] = yb[:, pl.ds(pl.multiple_of(64 * (1 - f2), 64), 64)].astype(BF16)
        c_second(i).start()

        @pl.when(i == 1)
        def _():
            @pl.when(inner)
            def _():
                h_later.wait_recv()
                h_halo_core.start()

        @pl.when(i == 4)
        def _():
            @pl.when(inner)
            def _():
                h_halo_core.wait_recv()

            partial_conv(he, wdec, (0, 1, 2), False, True)
            total = joined(False) + xe[2:4, rows].reshape(spots, chans).astype(F32)
            output[0] = total.astype(BF16).reshape(frames, tall, wide, chans)

    def s1(i):
        c_second(i).wait_recv()
        total = keep[i] + r1[i].astype(F32)
        keep[i] = total
        zb[i] = total.astype(BF16)
        for k in (2, 1, 3):
            c_z(i, k).start()

    def s2(i):
        s, f1, f2, _, _ = places(i)
        for k in (1, 2, 3):
            c_z(i, k).wait_recv()
        total = keep[i, :, pl.ds(pl.multiple_of(16 * t, 16), 16)]
        for k in range(3):
            total = total + rz[i, k].astype(F32)
        out[s, :, pl.ds(pl.multiple_of(128 * f1 + 64 * f2 + 16 * t, 16), 16)] = total.astype(BF16)
        for k in (2, 1, 3):
            c_zback(i, k).start()

    def s3(i):
        for k in (1, 2, 3):
            c_zback(i, k).wait_recv()
        c_secondback(i).start()

    def s4(i):
        c_secondback(i).wait_recv()
        c_firstback(i).start()
        c_coreback(i, 0).start()

    def s5(i):
        c_firstback(i).wait_recv()
        c_coreback(i, 1).start()

    def s6(i):
        c_coreback(i, 0).wait_recv()
        c_coreback(i, 1).wait_recv()

    stages = [s0, s1, s2, s3, s4, s5, s6]

    def body(i, carry):
        for k in (0, 6, 5, 4, 3, 2, 1):
            s = i - LAG * k

            @pl.when((s >= 0) & (s < STEPS))
            def _(k=k, s=s):
                stages[k](s)

        return carry

    lax.fori_loop(0, STEPS + LAG * (len(stages) - 1), body, 0)

    def finish(i, carry):
        c_second(i).wait_send()
        for k in (1, 2, 3):
            c_z(i, k).wait_send()
            c_zback(i, k).wait_send()
        c_secondback(i).wait_send()
        c_firstback(i).wait_send()
        c_coreback(i, 0).wait_send()
        c_coreback(i, 1).wait_send()
        return carry

    lax.fori_loop(0, STEPS, finish, 0)
    for sent in (x_core, g_core, xp_own, xp_own_core, gp_own, gp_own_core, d_core, d_pair, d_pair_core,
                 h_core, h_pair, h_pair_core):
        sent.wait_send()

    @pl.when(inner)
    def _():
        for sent in (g_earlier, x_halo_core, xp_halo, xp_halo_core, h_halo_core):
            sent.wait_send()

    @pl.when(outer)
    def _():
        for sent in (x_later, h_later, g_halo_core, gp_halo, gp_halo_core):
            sent.wait_send()


def whole_step(video, lengths, enc_weight, dec_weight, cotangent):
    vmem, bf = pltpu.VMEM, BF16
    frames, tall, wide, chans = video.shape[1:]
    spots = frames * tall * wide
    ext = (4, 10, wide, chans)
    enc27, dec27 = (w.reshape(27, chans, chans) for w in (enc_weight, dec_weight))
    output, grads = pl.pallas_call(
        step_kernel,
        out_shape=[
            jax.ShapeDtypeStruct(video.shape, bf),
            jax.ShapeDtypeStruct((18, 3, chans, chans), bf),
        ],
        in_specs=[
            pl.BlockSpec(memory_space=pltpu.SMEM),
            pl.BlockSpec(memory_space=vmem),
            pl.BlockSpec(memory_space=vmem),
            pl.BlockSpec(memory_space=pl.ANY),
            pl.BlockSpec(memory_space=pl.ANY),
        ],
        out_specs=[pl.BlockSpec(memory_space=vmem)] * 2,
        scratch_shapes=[
            vmem((27, chans, chans), bf),
            vmem((27, chans, chans), bf),
            vmem(ext, bf),
            vmem(ext, bf),
            vmem(ext, bf),
            vmem((frames, 8, wide, chans), bf),
            vmem((4, 10, wide, 128), bf),
            vmem(ext, bf),
            vmem((frames, 8, wide, 128), bf),
            vmem((frames, 8, wide, chans), bf),
            vmem((384, 4 * spots), bf),
            vmem((2, frames, 8, wide, 3 * chans), bf),
            vmem((3, spots, chans), F32),
            vmem((spots, chans), F32),
            vmem((3, 128, chans), F32),
            vmem((STEPS, 3, 64, chans), F32),
            vmem((STEPS, 3, 64, chans), bf),
            vmem((STEPS, 3, 64, chans), bf),
            vmem((STEPS, 3, 64, chans), bf),
            vmem((STEPS, 3, 3, 16, chans), bf),
            pltpu.SemaphoreType.DMA((2,)),
            pltpu.SemaphoreType.DMA((22,)),
            pltpu.SemaphoreType.DMA((22,)),
            pltpu.SemaphoreType.DMA((STEPS, 11)),
            pltpu.SemaphoreType.DMA((STEPS, 11)),
        ],
        compiler_params=pltpu.CompilerParams(
            collective_id=0, has_side_effects=True, vmem_limit_bytes=56 * 2**20
        ),
    )(lengths, video, cotangent, enc27, dec27)
    dec_grad = grads[:9].astype(F32).reshape(dec_weight.shape)
    enc_grad = grads[9:].astype(F32).reshape(enc_weight.shape)
    return output, enc_grad, dec_grad


def shards(video, lengths, enc_weight, dec_weight, cotangent):
    sizes = tuple(lax.axis_size(axis) for axis in ("dp", "tm", "height"))
    if sizes == (4, 4, 2) and video.shape[:3] == (1, 2, 4) and video.shape[-1] == 256:
        return whole_step(video, lengths, enc_weight, dec_weight, cotangent)
    frames = video.shape[1]
    first_frame = lax.axis_index("tm") * frames
    tpos = first_frame + jnp.arange(frames, dtype=jnp.int32)
    keep = (tpos[None, :] < lengths[:, None])[:, :, None, None, None]
    masked = jnp.where(keep, video, jnp.zeros_like(video))
    cot_masked = jnp.where(keep, cotangent, jnp.zeros_like(cotangent))
    ext_x = with_earlier(masked)
    pre = apply_taps(ext_x, enc_weight)
    hidden = jax.nn.silu(pre).astype(jnp.bfloat16)
    ext_h = with_earlier(hidden)
    output = (apply_taps(ext_h, dec_weight) + masked.astype(jnp.float32)).astype(jnp.bfloat16)
    ext_g = with_later(cot_masked)
    chans = dec_weight.shape[3]
    flipped = jnp.transpose(dec_weight[::-1, ::-1, ::-1], (0, 1, 3, 2, 4)).reshape(3, 3, chans, -1)
    dec_local = tap_grads(ext_h, cot_masked)
    back = apply_taps(ext_g, flipped, True)
    dpre = (back * dsilu(pre)).astype(jnp.bfloat16)
    enc_local = tap_grads(ext_x, dpre)
    enc_grad, dec_grad = sum_all(enc_local), sum_all(dec_local)
    return (output, enc_grad, dec_grad)


def solution(mesh):
    in_specs = (
        P("dp", "tm", "height", None, None),
        P("dp"),
        P(),
        P(),
        P("dp", "tm", "height", None, None),
    )
    out_specs = (P("dp", "tm", "height", None, None), P(), P())
    return jax.shard_map(shards, mesh=mesh, in_specs=in_specs, out_specs=out_specs, check_vma=False)
```

```python
import jax
import jax.numpy as jnp
from jax import lax
from jax.experimental import pallas as pl
from jax.experimental.pallas import tpu as pltpu
from jax.sharding import PartitionSpec as P

MESH = pl.DeviceIdType.MESH
LAG = 3


def extended(shard, sides, width):
    for axis, dim in sides:
        devices, length = (lax.axis_size(axis), shard.shape[dim])
        up = [(i, (i + 1) % devices) for i in range(devices - 1)]
        down = [(j, i) for i, j in up]
        last = lax.slice_in_dim(shard, length - width, length, axis=dim)
        leading = lax.slice_in_dim(shard, 0, width, axis=dim)
        before = lax.ppermute(last, axis, up)
        after = lax.ppermute(leading, axis, down)
        shard = jnp.concatenate([before, shard, after], axis=dim)
    return shard


def from_behind(block, axis, distance):
    devices = range(lax.axis_size(axis))
    route = [(i - distance, i) for i in devices if i - distance in devices]
    return lax.ppermute(block, axis, route)


def apply_taps(ext, weight, transposed=False):
    count, frame_pad, row_pad, wide, chans = ext.shape
    frames = frame_pad - 2
    rows = row_pad - 2
    outs = weight.shape[2] if transposed else weight.shape[-1]
    padded = jnp.pad(ext, ((0, 0), (0, 0), (0, 0), (1, 1), (0, 0)))
    stacked = jnp.concatenate([padded[:, :, :, e : e + wide, :] for e in range(3)], axis=-1)
    total = jnp.zeros((count * frames * rows * wide, outs), jnp.float32)
    for a in range(3):
        for b in range(3):
            slab = stacked[:, a : a + frames, b : b + rows].reshape(-1, 3 * chans)
            if transposed:
                total = total + lax.dot_general(
                    slab, weight[a, b], (((1,), (1,)), ((), ())), preferred_element_type=jnp.float32
                )
                continue
            total = total + jnp.dot(
                slab, weight[a, b].reshape(3 * chans, outs), preferred_element_type=jnp.float32
            )
    return total.reshape(count, frames, rows, wide, outs)


def tap_grads(ext, cot):
    count, frame_pad, row_pad, wide, chans = ext.shape
    frames = frame_pad - 2
    rows = row_pad - 2
    outs = cot.shape[-1]
    padded = jnp.pad(ext, ((0, 0), (0, 0), (0, 0), (1, 1), (0, 0)))
    stacked = jnp.concatenate([padded[:, :, :, e : e + wide, :] for e in range(3)], axis=-1)
    flat = cot.reshape(-1, outs)
    result = []
    for a in range(3):
        for b in range(3):
            slab = stacked[:, a : a + frames, b : b + rows].reshape(-1, 3 * chans)
            result.append(
                lax.dot_general(
                    slab, flat, (((0,), (0,)), ((), ())), preferred_element_type=jnp.float32
                )
            )
    return jnp.stack(result).reshape(3, 3, 3, chans, outs)


def dsilu(value):
    sig = jax.nn.sigmoid(value)
    return sig * (1.0 + value * (1.0 - sig))


def row_edges(block):
    return extended(block, (("height", 2),), 1)


def with_earlier(block):
    before = from_behind(block, "tm", 1)
    return row_edges(jnp.concatenate([before, block], axis=1))


def with_later(block):
    after = from_behind(block, "tm", -1)
    return row_edges(jnp.concatenate([block, after], axis=1))


def index_bits(axis):
    size = lax.axis_size(axis)
    bits = []
    step = 1
    while step < size:
        bits.append((axis, step))
        step *= 2
    return bits


def swap(block, axis, step):
    return lax.ppermute(block, axis, [(i, i ^ step) for i in range(lax.axis_size(axis))])


def sum_part(part, order):
    trail = []
    for dim, (axis, step) in order:
        upper = lax.rem(lax.axis_index(axis) // step, 2) == 1
        low, high = jnp.split(part, 2, axis=dim)
        keep, give = jnp.where(upper, high, low), jnp.where(upper, low, high)
        got = swap(give.astype(jnp.bfloat16), axis, step)
        part = keep + got.astype(jnp.float32)
        trail.append((dim, axis, step, upper))
    part = part.astype(jnp.bfloat16)
    for dim, axis, step, upper in trail[::-1]:
        got = swap(part, axis, step)
        part = jnp.concatenate([jnp.where(upper, got, part), jnp.where(upper, part, got)], axis=dim)
    return part.astype(jnp.float32)


def sum_all(grad):
    height, dp, tm = index_bits("height"), index_bits("dp"), index_bits("tm")
    rest = height[1:]
    flat = grad.reshape(27, -1, grad.shape[-1])
    sums = []
    at = 0
    for count, order in ((10, dp + tm + rest), (10, dp[::-1] + tm + rest), (7, tm + dp + rest)):
        part = flat[at : at + count]
        at += count
        sums.append(sum_part(part, [(2, height[0])] + [(1, bit) for bit in order]))
    return jnp.concatenate(sums, axis=0).reshape(grad.shape)

ITEMS = 9
STEPS = 2 * ITEMS
F32 = jnp.float32
BF16 = jnp.bfloat16


def step_kernel(
    lengths, video, cot, enc_hbm, dec_hbm, output, enc_out, dec_out,
    wenc, wdec, xe, ge, he, de, xp, gp, hp, dp, ht, ds, ys, yg, slope,
    yb, keep, give, r1, zb, rz, out, wsem, hs, hr, ssem, rsem, lsem,
):
    d, t, h = lax.axis_index("dp"), lax.axis_index("tm"), lax.axis_index("height")
    frames, tall, wide, chans = video.shape[1:]
    last = lax.axis_size("tm") - 1
    xbit, ybit = d % 2, d // 2
    core = (d, t, 1 - h)
    xdev = (d + 1 - 2 * xbit, t, h)
    ydev = (d + 2 - 4 * ybit, t, h)
    later = (d, lax.rem(t + 1, last + 1), h)
    earlier = (d, lax.rem(t + last, last + 1), h)
    spots = frames * tall * wide
    base = tall * h

    w_enc = pltpu.make_async_copy(enc_hbm, wenc, wsem.at[0])
    w_dec = pltpu.make_async_copy(dec_hbm, wdec, wsem.at[1])
    w_enc.start()
    w_dec.start()

    barrier = pltpu.get_barrier_semaphore()
    partners = [core, xdev, ydev] + [(d, lax.rem(t + k, last + 1), h) for k in range(1, 4)]
    for partner in partners:
        pl.semaphore_signal(barrier, inc=1, device_id=partner, device_id_type=MESH)

    rows = pl.ds(1 + base, tall)
    own_rows = pl.ds(base, tall)

    def half(first):
        return pl.ds(pl.multiple_of(128 * first, 128), 128)

    for f in range(frames):
        live = t * frames + f < lengths[0]
        xe[2 + f, rows] = jnp.where(live, video[0, f], jnp.zeros_like(video[0, f]))
        ge[f, rows] = jnp.where(live, cot[0, f], jnp.zeros_like(cot[0, f]))
    for ref in (xe, ge, he, xp, gp):
        for edge in (0, 9):
            ref[:, edge] = jnp.zeros((4,) + ref.shape[2:], BF16)

    @pl.when(t == 0)
    def _():
        for ref in (xe, he, xp):
            ref[0:2] = jnp.zeros((2,) + ref.shape[1:], BF16)

    @pl.when(t == last)
    def _():
        for ref in (ge, gp):
            ref[2:4] = jnp.zeros((2,) + ref.shape[1:], BF16)

    pl.semaphore_wait(barrier, len(partners))

    def message(slot, src, dst, target):
        return pltpu.make_async_remote_copy(
            src_ref=src,
            dst_ref=dst,
            send_sem=hs.at[slot],
            recv_sem=hr.at[slot],
            device_id=target,
            device_id_type=MESH,
        )

    def same(slot, ref, target):
        return message(slot, ref, ref, target)

    own, ahead = pl.ds(2, 2), pl.ds(0, 2)
    x_core = same(0, xe.at[own, rows], core)
    g_core = same(1, ge.at[ahead, rows], core)
    x_later = message(2, xe.at[own, rows], xe.at[ahead, rows], later)
    g_earlier = message(3, ge.at[ahead, rows], ge.at[own, rows], earlier)
    x_halo_core = same(4, xe.at[ahead, rows], core)
    g_halo_core = same(5, ge.at[own, rows], core)
    xp_own = message(6, xe.at[own, rows, :, half(1 - ybit)], xp.at[own, rows], ydev)
    xp_own_core = same(7, xp.at[own, rows], core)
    xp_halo = message(8, xe.at[ahead, rows, :, half(1 - ybit)], xp.at[ahead, rows], ydev)
    xp_halo_core = same(9, xp.at[ahead, rows], core)
    gp_own = message(10, ge.at[ahead, rows], gp.at[ahead, rows], xdev)
    gp_own_core = same(11, gp.at[ahead, rows], core)
    gp_halo = message(12, gp.at[ahead, rows], gp.at[own, rows], earlier)
    gp_halo_core = same(13, gp.at[own, rows], core)
    d_core = same(14, de.at[:, own_rows], core)
    d_pair = message(15, de.at[:, own_rows], dp.at[:, own_rows], ydev)
    d_pair_core = same(16, dp.at[:, own_rows], core)
    h_core = same(17, he.at[own, rows], core)
    h_later = message(18, he.at[own, rows], he.at[ahead, rows], later)
    h_halo_core = same(19, he.at[ahead, rows], core)
    h_pair = message(20, he.at[own, rows, :, half(1 - xbit)], hp.at[:, own_rows], xdev)
    h_pair_core = same(21, hp.at[:, own_rows], core)

    def when(cond, action):
        pl.when(cond)(action)

    inner, outer = t > 0, t < last
    when(outer, lambda: x_later.start())
    when(inner, lambda: g_earlier.start())
    x_core.start()
    g_core.start()
    gp_own.start()
    xp_own.start()

    def shifted(value, by):
        count = value.shape[0]
        column = lax.broadcasted_iota(jnp.int32, value.shape, 0) % wide
        moved = pltpu.roll(value, by % count, axis=0)
        return jnp.where(column == (0 if by == 1 else wide - 1), 0.0, moved)

    def partial_conv(acc, src, weight, taps, transposed, fresh):
        for e in range(3):
            total = None
            for a in taps:
                first = 2 - a if transposed else a
                for b in range(3):
                    down = 2 - b if transposed else b
                    slab = src[first : first + 2, pl.ds(base + down, tall)].reshape(spots, chans)
                    dims = (((1,), (1 if transposed else 0,)), ((), ()))
                    term = lax.dot_general(slab, weight[9 * a + 3 * b + e], dims, preferred_element_type=F32)
                    total = term if total is None else total + term
            if fresh:
                acc[e] = total
            else:
                acc[e] = acc[e] + total

    def joined(acc, transposed):
        one = -1 if transposed else 1
        return acc[1] + shifted(acc[0], one) + shifted(acc[2], -one)

    w_enc.wait()
    x_core.wait_recv()
    partial_conv(ys, xe, wenc, (2,), False, True)
    w_dec.wait()
    g_core.wait_recv()
    partial_conv(yg, ge, wdec, (2,), True, True)

    @pl.when(inner)
    def _():
        x_later.wait_recv()
        x_halo_core.start()
        xp_halo.start()
        x_halo_core.wait_recv()

    partial_conv(ys, xe, wenc, (1, 0), False, False)
    pre = joined(ys, False)
    sig = jax.nn.sigmoid(pre)
    hidden = (pre * sig).astype(BF16)
    slope[...] = sig * (1.0 + pre * (1.0 - sig))
    he[2:4, rows] = hidden.reshape(frames, tall, wide, chans)
    h_pair.start()
    h_core.start()
    when(outer, lambda: h_later.start())

    gp_own.wait_recv()
    gp_own_core.start()
    when(inner, lambda: gp_halo.start())
    xp_own.wait_recv()
    xp_own_core.start()

    @pl.when(outer)
    def _():
        g_earlier.wait_recv()
        g_halo_core.start()
        g_halo_core.wait_recv()

    partial_conv(yg, ge, wdec, (1, 0), True, False)
    de[:, own_rows] = (joined(yg, True) * slope[...]).astype(BF16).reshape(frames, tall, wide, chans)
    d_pair.start()
    d_core.start()

    chip = 2 * spots

    def turned(value, at):
        value = value.astype(F32)
        for e in range(3):
            moved = value if e == 1 else shifted(value, 1 if e == 0 else -1)
            ht[pl.ds(128 * e, 128), pl.ds(at * chip, chip)] = moved.T.astype(BF16)

    h_core.wait_recv()
    turned(he[2:4, 1:9, :, half(xbit)].reshape(chip, 128), 0)
    h_pair.wait_recv()
    h_pair_core.start()

    @pl.when(inner)
    def _():
        xp_halo.wait_recv()
        xp_halo_core.start()

    h_pair_core.wait_recv()
    turned(hp[...].reshape(chip, 128), 1)
    gp_own_core.wait_recv()

    def spread(value, at):
        value = value.astype(F32)
        for e in range(3):
            moved = value if e == 1 else shifted(value, -1 if e == 0 else 1)
            ds[at, :, :, :, pl.ds(chans * e, chans)] = moved.astype(BF16).reshape(frames, 8, wide, chans)

    def kind(i, hh):
        enc = jnp.where((i == ITEMS - 1) | ((i > 0) & ((i + hh) % 2 == 0)), 1, 0)
        before = jnp.where(hh == 1, i, jnp.maximum(i - 1, 0)) // 2
        tap = jnp.where(enc == 1, 7 + hh - 2 * before, 8 - hh - 2 * (i - before))
        return enc, tap

    def places(i):
        enc, tap = kind(i // 2, h)
        f1 = jnp.where(enc == 1, ybit, xbit)
        f2 = jnp.where(enc == 1, xbit, ybit)
        dx, dy = d + 1 - 2 * xbit, d + 2 - 4 * ybit
        p1 = (jnp.where(enc == 1, dy, dx), t, h)
        p2 = (jnp.where(enc == 1, dx, dy), t, h)
        return 18 * enc + 2 * tap + i % 2, f1, f2, p1, p2

    def copy(i, slot, src, dst, target):
        return pltpu.make_async_remote_copy(
            src_ref=src,
            dst_ref=dst,
            send_sem=ssem.at[i, slot],
            recv_sem=rsem.at[i, slot],
            device_id=target,
            device_id_type=MESH,
        )

    def part(ref, i, first, count):
        return ref.at[i, :, pl.ds(pl.multiple_of(first, 16), count)]

    def zmate(k):
        return lax.rem(t + k, last + 1)

    def c_second(i):
        _, _, _, _, p2 = places(i)
        return copy(i, 0, give.at[i], r1.at[i], p2)

    def c_z(i, k):
        other = zmate(k)
        return copy(i, k, part(zb, i, 16 * other, 16), rz.at[i, k - 1], (d, other, h))

    def c_zback(i, k):
        s, f1, f2, _, _ = places(i)
        here = part(out, s, 128 * f1 + 64 * f2 + 16 * t, 16)
        return copy(i, 3 + k, here, here, (d, zmate(k), h))

    def c_secondback(i):
        s, f1, f2, _, p2 = places(i)
        here = part(out, s, 128 * f1 + 64 * f2, 64)
        return copy(i, 7, here, here, p2)

    def c_firstback(i):
        s, f1, _, p1, _ = places(i)
        here = part(out, s, 128 * f1, 128)
        return copy(i, 8, here, here, p1)

    def c_coreback(i, k):
        s, f1, _, _, _ = places(i)
        here = part(out, s, 128 * (f1 if k == 0 else 1 - f1), 128)
        return copy(i, 9 + k, here, here, core)

    def dec_slab(tap):
        a = tap // 3
        b = tap % 3
        total = None
        for at, ref in ((0, ge), (1, gp)):
            slab = ref[pl.ds(2 - a, 2), pl.ds(2 - b, 8)].reshape(chip, chans)
            term = jnp.dot(ht[:, at * chip : (at + 1) * chip], slab, preferred_element_type=F32)
            total = term if total is None else total + term
        for e in range(3):
            for side in range(2):
                yb[side, e] = total[128 * e : 128 * (e + 1), 128 * side : 128 * (side + 1)]

    def enc_slab(tap):
        a = tap // 3
        b = tap % 3
        total = None
        for at in range(2):
            if at == 0:
                slab = xe[pl.ds(a, 2), pl.ds(b, 8), :, half(ybit)]
            else:
                slab = xp[pl.ds(a, 2), pl.ds(b, 8)]
            term = lax.dot_general(
                slab.reshape(chip, 128),
                ds[at].reshape(chip, 3 * chans),
                (((0,), (0,)), ((), ())),
                preferred_element_type=F32,
            )
            total = term if total is None else total + term
        for e in range(3):
            for side in range(2):
                at = chans * e + 128 * side
                yb[side, e] = total[:, at : at + 128]

    def items(i):
        enc, tap = kind(i, h)

        @pl.when(i == 1)
        def _():
            @pl.when(outer)
            def _():
                gp_halo.wait_recv()
                gp_halo_core.start()
                gp_halo_core.wait_recv()

        @pl.when(i == 1)
        def _():
            d_core.wait_recv()
            spread(de[...].reshape(chip, chans), 0)
            d_pair.wait_recv()
            d_pair_core.start()
            xp_own_core.wait_recv()
            when(inner, lambda: xp_halo_core.wait_recv())
            d_pair_core.wait_recv()
            spread(dp[...].reshape(chip, chans), 1)

        @pl.when(enc == 0)
        def _():
            dec_slab(tap)

        @pl.when(enc == 1)
        def _():
            enc_slab(tap)

        @pl.when(i == 1)
        def _():
            @pl.when(inner)
            def _():
                h_later.wait_recv()
                h_halo_core.start()

        @pl.when(i == 4)
        def _():
            @pl.when(inner)
            def _():
                h_halo_core.wait_recv()

            partial_conv(ys, he, wdec, (0, 1, 2), False, True)
            total = joined(ys, False) + xe[2:4, rows].reshape(spots, chans).astype(F32)
            output[0] = total.astype(BF16).reshape(frames, tall, wide, chans)

    def s0(i):
        @pl.when(i % 2 == 0)
        def _():
            items(i // 2)

        _, _, f2, _, _ = places(i)
        side = i % 2
        keep[i] = yb[side, :, pl.ds(pl.multiple_of(64 * f2, 64), 64)]
        give[i] = yb[side, :, pl.ds(pl.multiple_of(64 * (1 - f2), 64), 64)].astype(BF16)
        c_second(i).start()

    def s1(i):
        c_second(i).wait_recv()
        total = keep[i] + r1[i].astype(F32)
        keep[i] = total
        zb[i] = total.astype(BF16)
        for k in (2, 1, 3):
            c_z(i, k).start()

    def s2(i):
        s, f1, f2, _, _ = places(i)
        for k in (1, 2, 3):
            c_z(i, k).wait_recv()
        total = keep[i, :, pl.ds(pl.multiple_of(16 * t, 16), 16)]
        for k in range(3):
            total = total + rz[i, k].astype(F32)
        out[s, :, pl.ds(pl.multiple_of(128 * f1 + 64 * f2 + 16 * t, 16), 16)] = total.astype(BF16)
        for k in (2, 1, 3):
            c_zback(i, k).start()

    def s3(i):
        for k in (1, 2, 3):
            c_zback(i, k).wait_recv()
        c_secondback(i).start()

    def s4(i):
        c_secondback(i).wait_recv()
        c_firstback(i).start()
        c_coreback(i, 0).start()

    def s5(i):
        c_firstback(i).wait_recv()
        c_coreback(i, 1).start()

    def leave(i, hh, action):
        enc, tap = kind(i // 2, hh)
        side = i % 2
        s = 18 * enc + 2 * tap + side
        slot = jnp.where(hh == h, 0, 1)

        def to(dst):
            return pltpu.make_async_copy(
                out.at[s], dst.at[pl.ds(3 * tap, 3), :, pl.ds(pl.multiple_of(128 * side, 128), 128)], lsem.at[i, slot]
            )

        @pl.when(enc == 1)
        def _():
            action(to(enc_out))

        @pl.when(enc == 0)
        def _():
            action(to(dec_out))

    def s6(i):
        c_coreback(i, 0).wait_recv()
        c_coreback(i, 1).wait_recv()
        leave(i, h, lambda c: c.start())
        leave(i, 1 - h, lambda c: c.start())

    stages = [s0, s1, s2, s3, s4, s5, s6]

    def body(i, carry):
        for k in (6, 5, 4, 3, 2, 1, 0):
            s = i - LAG * k

            @pl.when((s >= 0) & (s < STEPS))
            def _(k=k, s=s):
                stages[k](s)

        return carry

    lax.fori_loop(0, STEPS + LAG * (len(stages) - 1), body, 0)

    def finish(i, carry):
        c_second(i).wait_send()
        for k in (1, 2, 3):
            c_z(i, k).wait_send()
            c_zback(i, k).wait_send()
        c_secondback(i).wait_send()
        c_firstback(i).wait_send()
        c_coreback(i, 0).wait_send()
        c_coreback(i, 1).wait_send()
        leave(i, h, lambda c: c.wait())
        leave(i, 1 - h, lambda c: c.wait())
        return carry

    lax.fori_loop(0, STEPS, finish, 0)
    for sent in (x_core, g_core, xp_own, xp_own_core, gp_own, gp_own_core, d_core, d_pair, d_pair_core,
                 h_core, h_pair, h_pair_core):
        sent.wait_send()

    @pl.when(inner)
    def _():
        for sent in (g_earlier, x_halo_core, xp_halo, xp_halo_core, gp_halo, h_halo_core):
            sent.wait_send()

    @pl.when(outer)
    def _():
        for sent in (x_later, h_later, g_halo_core, gp_halo_core):
            sent.wait_send()


def whole_step(video, lengths, enc_weight, dec_weight, cotangent):
    vmem, bf = pltpu.VMEM, BF16
    frames, tall, wide, chans = video.shape[1:]
    spots = frames * tall * wide
    ext = (4, 10, wide, chans)
    enc27, dec27 = (w.reshape(27, chans, chans) for w in (enc_weight, dec_weight))
    output, enc_grad, dec_grad = pl.pallas_call(
        step_kernel,
        out_shape=[
            jax.ShapeDtypeStruct(video.shape, bf),
            jax.ShapeDtypeStruct((27, chans, chans), bf),
            jax.ShapeDtypeStruct((27, chans, chans), bf),
        ],
        in_specs=[
            pl.BlockSpec(memory_space=pltpu.SMEM),
            pl.BlockSpec(memory_space=vmem),
            pl.BlockSpec(memory_space=vmem),
            pl.BlockSpec(memory_space=pl.ANY),
            pl.BlockSpec(memory_space=pl.ANY),
        ],
        out_specs=[pl.BlockSpec(memory_space=vmem)] + [pl.BlockSpec(memory_space=pl.ANY)] * 2,
        scratch_shapes=[
            vmem((27, chans, chans), bf),
            vmem((27, chans, chans), bf),
            vmem(ext, bf),
            vmem(ext, bf),
            vmem(ext, bf),
            vmem((frames, 8, wide, chans), bf),
            vmem((4, 10, wide, 128), bf),
            vmem(ext, bf),
            vmem((frames, 8, wide, 128), bf),
            vmem((frames, 8, wide, chans), bf),
            vmem((384, 4 * spots), bf),
            vmem((2, frames, 8, wide, 3 * chans), bf),
            vmem((3, spots, chans), F32),
            vmem((3, spots, chans), F32),
            vmem((spots, chans), F32),
            vmem((2, 3, 128, 128), F32),
            vmem((STEPS, 3, 64, 128), F32),
            vmem((STEPS, 3, 64, 128), bf),
            vmem((STEPS, 3, 64, 128), bf),
            vmem((STEPS, 3, 64, 128), bf),
            vmem((STEPS, 3, 3, 16, 128), bf),
            vmem((36, 3, chans, 128), bf),
            pltpu.SemaphoreType.DMA((2,)),
            pltpu.SemaphoreType.DMA((22,)),
            pltpu.SemaphoreType.DMA((22,)),
            pltpu.SemaphoreType.DMA((STEPS, 11)),
            pltpu.SemaphoreType.DMA((STEPS, 11)),
            pltpu.SemaphoreType.DMA((STEPS, 2)),
        ],
        compiler_params=pltpu.CompilerParams(
            collective_id=0, has_side_effects=True, vmem_limit_bytes=56 * 2**20
        ),
    )(lengths, video, cotangent, enc27, dec27)
    enc_grad, dec_grad = (g.astype(F32).reshape(enc_weight.shape) for g in (enc_grad, dec_grad))
    return output, enc_grad, dec_grad


def shards(video, lengths, enc_weight, dec_weight, cotangent):
    sizes = tuple(lax.axis_size(axis) for axis in ("dp", "tm", "height"))
    if sizes == (4, 4, 2) and video.shape[:3] == (1, 2, 4) and video.shape[-1] == 256:
        return whole_step(video, lengths, enc_weight, dec_weight, cotangent)
    frames = video.shape[1]
    first_frame = lax.axis_index("tm") * frames
    tpos = first_frame + jnp.arange(frames, dtype=jnp.int32)
    keep = (tpos[None, :] < lengths[:, None])[:, :, None, None, None]
    masked = jnp.where(keep, video, jnp.zeros_like(video))
    cot_masked = jnp.where(keep, cotangent, jnp.zeros_like(cotangent))
    ext_x = with_earlier(masked)
    pre = apply_taps(ext_x, enc_weight)
    hidden = jax.nn.silu(pre).astype(jnp.bfloat16)
    ext_h = with_earlier(hidden)
    output = (apply_taps(ext_h, dec_weight) + masked.astype(jnp.float32)).astype(jnp.bfloat16)
    ext_g = with_later(cot_masked)
    chans = dec_weight.shape[3]
    flipped = jnp.transpose(dec_weight[::-1, ::-1, ::-1], (0, 1, 3, 2, 4)).reshape(3, 3, chans, -1)
    dec_local = tap_grads(ext_h, cot_masked)
    back = apply_taps(ext_g, flipped, True)
    dpre = (back * dsilu(pre)).astype(jnp.bfloat16)
    enc_local = tap_grads(ext_x, dpre)
    enc_grad, dec_grad = sum_all(enc_local), sum_all(dec_local)
    return (output, enc_grad, dec_grad)


def solution(mesh):
    in_specs = (
        P("dp", "tm", "height", None, None),
        P("dp"),
        P(),
        P(),
        P("dp", "tm", "height", None, None),
    )
    out_specs = (P("dp", "tm", "height", None, None), P(), P())
    return jax.shard_map(shards, mesh=mesh, in_specs=in_specs, out_specs=out_specs, check_vma=False)
```

```python
import jax
import jax.numpy as jnp
from jax import lax
from jax.experimental import pallas as pl
from jax.experimental.pallas import tpu as pltpu
from jax.sharding import PartitionSpec as P

MESH = pl.DeviceIdType.MESH
ORDER = (8, 7, 6, 5, 4, 3, 2, 1, 0)
LAGS = (0, 5, 8, 12, 15, 17, 21, 25, 28)


def extended(shard, sides, width):
    for axis, dim in sides:
        devices, length = (lax.axis_size(axis), shard.shape[dim])
        up = [(i, (i + 1) % devices) for i in range(devices - 1)]
        down = [(j, i) for i, j in up]
        last = lax.slice_in_dim(shard, length - width, length, axis=dim)
        leading = lax.slice_in_dim(shard, 0, width, axis=dim)
        before = lax.ppermute(last, axis, up)
        after = lax.ppermute(leading, axis, down)
        shard = jnp.concatenate([before, shard, after], axis=dim)
    return shard


def from_behind(block, axis, distance):
    devices = range(lax.axis_size(axis))
    route = [(i - distance, i) for i in devices if i - distance in devices]
    return lax.ppermute(block, axis, route)


def apply_taps(ext, weight, transposed=False):
    count, frame_pad, row_pad, wide, chans = ext.shape
    frames = frame_pad - 2
    rows = row_pad - 2
    outs = weight.shape[2] if transposed else weight.shape[-1]
    padded = jnp.pad(ext, ((0, 0), (0, 0), (0, 0), (1, 1), (0, 0)))
    stacked = jnp.concatenate([padded[:, :, :, e : e + wide, :] for e in range(3)], axis=-1)
    total = jnp.zeros((count * frames * rows * wide, outs), jnp.float32)
    for a in range(3):
        for b in range(3):
            slab = stacked[:, a : a + frames, b : b + rows].reshape(-1, 3 * chans)
            if transposed:
                total = total + lax.dot_general(
                    slab, weight[a, b], (((1,), (1,)), ((), ())), preferred_element_type=jnp.float32
                )
                continue
            total = total + jnp.dot(
                slab, weight[a, b].reshape(3 * chans, outs), preferred_element_type=jnp.float32
            )
    return total.reshape(count, frames, rows, wide, outs)


def tap_grads(ext, cot):
    count, frame_pad, row_pad, wide, chans = ext.shape
    frames = frame_pad - 2
    rows = row_pad - 2
    outs = cot.shape[-1]
    padded = jnp.pad(ext, ((0, 0), (0, 0), (0, 0), (1, 1), (0, 0)))
    stacked = jnp.concatenate([padded[:, :, :, e : e + wide, :] for e in range(3)], axis=-1)
    flat = cot.reshape(-1, outs)
    result = []
    for a in range(3):
        for b in range(3):
            slab = stacked[:, a : a + frames, b : b + rows].reshape(-1, 3 * chans)
            result.append(
                lax.dot_general(
                    slab, flat, (((0,), (0,)), ((), ())), preferred_element_type=jnp.float32
                )
            )
    return jnp.stack(result).reshape(3, 3, 3, chans, outs)


def dsilu(value):
    sig = jax.nn.sigmoid(value)
    return sig * (1.0 + value * (1.0 - sig))


def row_edges(block):
    return extended(block, (("height", 2),), 1)


def with_earlier(block):
    before = from_behind(block, "tm", 1)
    return row_edges(jnp.concatenate([before, block], axis=1))


def with_later(block):
    after = from_behind(block, "tm", -1)
    return row_edges(jnp.concatenate([block, after], axis=1))


def index_bits(axis):
    size = lax.axis_size(axis)
    bits = []
    step = 1
    while step < size:
        bits.append((axis, step))
        step *= 2
    return bits


def swap(block, axis, step):
    return lax.ppermute(block, axis, [(i, i ^ step) for i in range(lax.axis_size(axis))])


def sum_part(part, order):
    trail = []
    for dim, (axis, step) in order:
        upper = lax.rem(lax.axis_index(axis) // step, 2) == 1
        low, high = jnp.split(part, 2, axis=dim)
        keep, give = jnp.where(upper, high, low), jnp.where(upper, low, high)
        got = swap(give.astype(jnp.bfloat16), axis, step)
        part = keep + got.astype(jnp.float32)
        trail.append((dim, axis, step, upper))
    part = part.astype(jnp.bfloat16)
    for dim, axis, step, upper in trail[::-1]:
        got = swap(part, axis, step)
        part = jnp.concatenate([jnp.where(upper, got, part), jnp.where(upper, part, got)], axis=dim)
    return part.astype(jnp.float32)


def sum_all(grad):
    height, dp, tm = index_bits("height"), index_bits("dp"), index_bits("tm")
    rest = height[1:]
    flat = grad.reshape(27, -1, grad.shape[-1])
    sums = []
    at = 0
    for count, order in ((10, dp + tm + rest), (10, dp[::-1] + tm + rest), (7, tm + dp + rest)):
        part = flat[at : at + count]
        at += count
        sums.append(sum_part(part, [(2, height[0])] + [(1, bit) for bit in order]))
    return jnp.concatenate(sums, axis=0).reshape(grad.shape)

ITEMS = 9
STEPS = 2 * ITEMS
F32 = jnp.float32
BF16 = jnp.bfloat16


def step_kernel(
    lengths, video, cot, enc_hbm, dec_hbm, output, enc_out, dec_out,
    wenc, wdec, xe, ge, he, de, xp, gp, hp, dp, ht, ds, ys, yg, slope,
    yb, keep, give, r1, zb, zc, ra, rn, rc, out, wsem, hs, hr, ssem, rsem, lsem,
):
    d, t, h = lax.axis_index("dp"), lax.axis_index("tm"), lax.axis_index("height")
    frames, tall, wide, chans = video.shape[1:]
    last = lax.axis_size("tm") - 1
    xbit, ybit = d % 2, d // 2
    core = (d, t, 1 - h)
    xdev = (d + 1 - 2 * xbit, t, h)
    ydev = (d + 2 - 4 * ybit, t, h)
    later = (d, lax.rem(t + 1, last + 1), h)
    earlier = (d, lax.rem(t + last, last + 1), h)
    spots = frames * tall * wide
    base = tall * h

    w_enc = pltpu.make_async_copy(enc_hbm, wenc, wsem.at[0])
    w_dec = pltpu.make_async_copy(dec_hbm, wdec, wsem.at[1])
    w_enc.start()
    w_dec.start()

    barrier = pltpu.get_barrier_semaphore()
    partners = [core, xdev, ydev] + [(d, lax.rem(t + k, last + 1), h) for k in range(1, 4)]
    for partner in partners:
        pl.semaphore_signal(barrier, inc=1, device_id=partner, device_id_type=MESH)

    rows = pl.ds(1 + base, tall)
    own_rows = pl.ds(base, tall)

    def half(first):
        return pl.ds(pl.multiple_of(128 * first, 128), 128)

    for f in range(frames):
        live = t * frames + f < lengths[0]
        xe[2 + f, rows] = jnp.where(live, video[0, f], jnp.zeros_like(video[0, f]))
        ge[f, rows] = jnp.where(live, cot[0, f], jnp.zeros_like(cot[0, f]))
    pl.semaphore_wait(barrier, len(partners))

    def message(slot, src, dst, target):
        return pltpu.make_async_remote_copy(
            src_ref=src,
            dst_ref=dst,
            send_sem=hs.at[slot],
            recv_sem=hr.at[slot],
            device_id=target,
            device_id_type=MESH,
        )

    def same(slot, ref, target):
        return message(slot, ref, ref, target)

    own, ahead = pl.ds(2, 2), pl.ds(0, 2)
    x_core = same(0, xe.at[own, rows], core)
    g_core = same(1, ge.at[ahead, rows], core)
    x_later = message(2, xe.at[own, rows], xe.at[ahead, rows], later)
    g_earlier = message(3, ge.at[ahead, rows], ge.at[own, rows], earlier)
    x_halo_core = same(4, xe.at[ahead, rows], core)
    g_halo_core = same(5, ge.at[own, rows], core)
    xp_own = message(6, xe.at[own, rows, :, half(1 - ybit)], xp.at[own, rows], ydev)
    xp_own_core = same(7, xp.at[own, rows], core)
    xp_halo = message(8, xe.at[ahead, rows, :, half(1 - ybit)], xp.at[ahead, rows], ydev)
    xp_halo_core = same(9, xp.at[ahead, rows], core)
    gp_own = message(10, ge.at[ahead, rows], gp.at[ahead, rows], xdev)
    gp_own_core = same(11, gp.at[ahead, rows], core)
    gp_halo = message(12, gp.at[ahead, rows], gp.at[own, rows], earlier)
    gp_halo_core = same(13, gp.at[own, rows], core)
    d_core = same(14, de.at[:, own_rows], core)
    d_pair = message(15, de.at[:, own_rows], dp.at[:, own_rows], ydev)
    d_pair_core = same(16, dp.at[:, own_rows], core)
    h_core = same(17, he.at[own, rows], core)
    h_later = message(18, he.at[own, rows], he.at[ahead, rows], later)
    h_halo_core = same(19, he.at[ahead, rows], core)
    h_pair = message(20, he.at[own, rows, :, half(1 - xbit)], hp.at[:, own_rows], xdev)
    h_pair_core = same(21, hp.at[:, own_rows], core)

    def when(cond, action):
        pl.when(cond)(action)

    inner, outer = t > 0, t < last
    when(outer, lambda: x_later.start())
    when(inner, lambda: g_earlier.start())
    x_core.start()
    g_core.start()
    gp_own.start()
    xp_own.start()

    for ref in (xe, ge, he, xp, gp):
        for edge in (0, 9):
            ref[:, edge] = jnp.zeros((4,) + ref.shape[2:], BF16)

    @pl.when(t == 0)
    def _():
        for ref in (xe, he, xp):
            ref[0:2] = jnp.zeros((2,) + ref.shape[1:], BF16)

    @pl.when(t == last)
    def _():
        for ref in (ge, gp):
            ref[2:4] = jnp.zeros((2,) + ref.shape[1:], BF16)

    def shifted(value, by):
        count = value.shape[0]
        column = lax.broadcasted_iota(jnp.int32, value.shape, 0) % wide
        moved = pltpu.roll(value, by % count, axis=0)
        return jnp.where(column == (0 if by == 1 else wide - 1), 0.0, moved)

    def partial_conv(acc, src, weight, taps, transposed, fresh):
        for e in range(3):
            total = None
            for a in taps:
                first = 2 - a if transposed else a
                for b in range(3):
                    down = 2 - b if transposed else b
                    slab = src[first : first + 2, pl.ds(base + down, tall)].reshape(spots, chans)
                    dims = (((1,), (1 if transposed else 0,)), ((), ()))
                    term = lax.dot_general(slab, weight[9 * a + 3 * b + e], dims, preferred_element_type=F32)
                    total = term if total is None else total + term
            if fresh:
                acc[e] = total
            else:
                acc[e] = acc[e] + total

    def joined(acc, transposed):
        one = -1 if transposed else 1
        return acc[1] + shifted(acc[0], one) + shifted(acc[2], -one)

    w_enc.wait()
    x_core.wait_recv()
    partial_conv(ys, xe, wenc, (2,), False, True)
    w_dec.wait()
    g_core.wait_recv()
    partial_conv(yg, ge, wdec, (2,), True, True)

    @pl.when(inner)
    def _():
        x_later.wait_recv()
        x_halo_core.start()
        xp_halo.start()
        x_halo_core.wait_recv()

    partial_conv(ys, xe, wenc, (1, 0), False, False)
    pre = joined(ys, False)
    sig = jax.nn.sigmoid(pre)
    hidden = (pre * sig).astype(BF16)
    slope[...] = sig * (1.0 + pre * (1.0 - sig))
    he[2:4, rows] = hidden.reshape(frames, tall, wide, chans)
    h_pair.start()
    h_core.start()
    when(outer, lambda: h_later.start())

    gp_own.wait_recv()
    gp_own_core.start()
    when(inner, lambda: gp_halo.start())
    xp_own.wait_recv()
    xp_own_core.start()

    @pl.when(outer)
    def _():
        g_earlier.wait_recv()
        g_halo_core.start()
        g_halo_core.wait_recv()

    partial_conv(yg, ge, wdec, (1, 0), True, False)
    de[:, own_rows] = (joined(yg, True) * slope[...]).astype(BF16).reshape(frames, tall, wide, chans)
    d_pair.start()
    d_core.start()

    chip = 2 * spots

    def turned(value, at):
        value = value.astype(F32)
        for e in range(3):
            moved = value if e == 1 else shifted(value, 1 if e == 0 else -1)
            ht[pl.ds(128 * e, 128), pl.ds(at * chip, chip)] = moved.T.astype(BF16)

    h_core.wait_recv()
    turned(he[2:4, 1:9, :, half(xbit)].reshape(chip, 128), 0)
    h_pair.wait_recv()
    h_pair_core.start()

    @pl.when(inner)
    def _():
        xp_halo.wait_recv()
        xp_halo_core.start()

    h_pair_core.wait_recv()
    turned(hp[...].reshape(chip, 128), 1)
    gp_own_core.wait_recv()

    def spread(value, at):
        value = value.astype(F32)
        for e in range(3):
            moved = value if e == 1 else shifted(value, -1 if e == 0 else 1)
            ds[at, :, :, :, pl.ds(chans * e, chans)] = moved.astype(BF16).reshape(frames, 8, wide, chans)

    def kind(i, hh):
        start = ITEMS // 2 + 1 - hh
        enc = jnp.where(i >= start, 1, 0)
        before = jnp.maximum(i - start, 0)
        tap = jnp.where(enc == 1, 7 + hh - 2 * before, 8 - hh - 2 * (i - before))
        return enc, tap

    def places(i):
        enc, tap = kind(i // 2, h)
        f1 = jnp.where(enc == 1, ybit, xbit)
        f2 = jnp.where(enc == 1, xbit, ybit)
        dx, dy = d + 1 - 2 * xbit, d + 2 - 4 * ybit
        p1 = (jnp.where(enc == 1, dy, dx), t, h)
        p2 = (jnp.where(enc == 1, dx, dy), t, h)
        return 18 * enc + 2 * tap + i % 2, f1, f2, p1, p2

    def copy(i, slot, src, dst, target):
        return pltpu.make_async_remote_copy(
            src_ref=src,
            dst_ref=dst,
            send_sem=ssem.at[i, slot],
            recv_sem=rsem.at[i, slot],
            device_id=target,
            device_id_type=MESH,
        )

    def part(ref, i, first, count):
        return ref.at[i, :, pl.ds(pl.multiple_of(first, 16), count)]

    edge = (t == 0) | (t == last)
    near = jnp.where(t == 0, 1, 2)
    side_edge = jnp.where(t == 1, 0, last)

    def along(other):
        return (d, other, h)

    def c_second(i):
        _, _, _, _, p2 = places(i)
        return copy(i, 0, give.at[i], r1.at[i], p2)

    def c_hand(i):
        return copy(i, 1, part(zb, i, jnp.where(t == 0, 16, 0), 48), ra.at[i], along(near))

    def c_near(i):
        return copy(i, 1, part(zb, i, 16 * side_edge, 16), rn.at[i], along(side_edge))

    def c_cross(i):
        return copy(i, 2, part(zc, i, jnp.where(t == 1, 0, 16), 16), rc.at[i], along(last - t))

    def c_far(i):
        return copy(i, 3, part(zc, i, jnp.where(t == 1, 16, 0), 16), rc.at[i], along(last - side_edge))

    def shard(i, owner, count=1):
        s, f1, f2, _, _ = places(i)
        return part(out, s, 128 * f1 + 64 * f2 + 16 * owner, 16 * count)

    def c_shard(i, slot, other):
        return copy(i, slot, shard(i, t), shard(i, t), along(other))

    def c_arrive(i, slot, owner, count=1):
        return copy(i, slot, shard(i, owner, count), shard(i, owner, count), along(owner))

    def c_pass(i):
        here = shard(i, jnp.where(t == 1, 2, 0), 2)
        return copy(i, 5, here, here, along(side_edge))

    def piece(i, flip1, flip2, first, count):
        s, f1, f2, _, _ = places(i)
        g1, g2 = (1 - f1 if flip1 else f1), (1 - f2 if flip2 else f2)
        return part(out, s, 128 * g1 + 64 * g2 + first, count)

    def gather(i, slot, here, which):
        return copy(i, slot, here, here, places(i)[which])

    def c_own2(i):
        return gather(i, 7, piece(i, False, False, 0, 64), 4)

    def c_own1(i):
        return gather(i, 8, piece(i, False, False, 0, 64), 3)

    def c_on1(i):
        return gather(i, 9, piece(i, False, True, 0, 32), 3)

    def c_on2(i):
        return gather(i, 10, piece(i, True, False, 32, 32), 4)

    def c_coreback(i):
        s = places(i)[0]
        return copy(i, 11, out.at[s], out.at[s], core)

    def dec_slab(tap):
        a = tap // 3
        b = tap % 3
        total = None
        for at, ref in ((0, ge), (1, gp)):
            slab = ref[pl.ds(2 - a, 2), pl.ds(2 - b, 8)].reshape(chip, chans)
            term = jnp.dot(ht[:, at * chip : (at + 1) * chip], slab, preferred_element_type=F32)
            total = term if total is None else total + term
        for e in range(3):
            for side in range(2):
                yb[side, e] = total[128 * e : 128 * (e + 1), 128 * side : 128 * (side + 1)]

    def enc_slab(tap):
        a = tap // 3
        b = tap % 3
        total = None
        for at in range(2):
            if at == 0:
                slab = xe[pl.ds(a, 2), pl.ds(b, 8), :, half(ybit)]
            else:
                slab = xp[pl.ds(a, 2), pl.ds(b, 8)]
            term = lax.dot_general(
                slab.reshape(chip, 128),
                ds[at].reshape(chip, 3 * chans),
                (((0,), (0,)), ((), ())),
                preferred_element_type=F32,
            )
            total = term if total is None else total + term
        for e in range(3):
            for side in range(2):
                at = chans * e + 128 * side
                yb[side, e] = total[:, at : at + 128]

    def items(i):
        enc, tap = kind(i, h)

        @pl.when(i == 1)
        def _():
            @pl.when(outer)
            def _():
                gp_halo.wait_recv()
                gp_halo_core.start()
                gp_halo_core.wait_recv()

        @pl.when((i == 2) & inner)
        def _():
            h_later.wait_recv()
            h_halo_core.start()

        @pl.when(i == 2)
        def _():
            d_core.wait_recv()
            spread(de[...].reshape(chip, chans), 0)
            d_pair.wait_recv()
            d_pair_core.start()

        @pl.when(i == 4)
        def _():
            xp_own_core.wait_recv()
            when(inner, lambda: xp_halo_core.wait_recv())
            d_pair_core.wait_recv()
            spread(dp[...].reshape(chip, chans), 1)

        @pl.when(enc == 0)
        def _():
            dec_slab(tap)

        @pl.when(enc == 1)
        def _():
            enc_slab(tap)

    def finish_output():
        @pl.when(inner)
        def _():
            h_halo_core.wait_recv()

        partial_conv(ys, he, wdec, (0, 1, 2), False, True)
        total = joined(ys, False) + xe[2:4, rows].reshape(spots, chans).astype(F32)
        output[0] = total.astype(BF16).reshape(frames, tall, wide, chans)

    def s0(i):
        @pl.when(i % 2 == 0)
        def _():
            items(i // 2)

        _, _, f2, _, _ = places(i)
        side = i % 2
        keep[i] = yb[side, :, pl.ds(pl.multiple_of(64 * f2, 64), 64)]
        give[i] = yb[side, :, pl.ds(pl.multiple_of(64 * (1 - f2), 64), 64)].astype(BF16)
        c_second(i).start()

    def s1(i):
        c_second(i).wait_recv()
        total = keep[i] + r1[i].astype(F32)
        keep[i] = total
        zb[i] = total.astype(BF16)
        when(edge, lambda: c_hand(i).start())
        when(~edge, lambda: c_near(i).start())

    def s2(i):
        @pl.when(~edge)
        def _():
            copy(i, 1, ra.at[i], ra.at[i], along(side_edge)).wait_recv()
            low = jnp.where(t == 1, 16, 0)
            at = pl.ds(pl.multiple_of(low, 16), 48)
            keep[i, :, at] = keep[i, :, at] + ra[i].astype(F32)
            zc[i] = keep[i, :, pl.ds(pl.multiple_of(2 * low, 16), 32)].astype(BF16)
            c_cross(i).start()
            c_far(i).start()

    def s3(i):
        s, f1, f2, _, _ = places(i)
        mine = pl.ds(pl.multiple_of(16 * t, 16), 16)

        @pl.when(edge)
        def _():
            copy(i, 1, rn.at[i], rn.at[i], along(near)).wait_recv()
            copy(i, 3, rc.at[i], rc.at[i], along(last - near)).wait_recv()
            keep[i, :, mine] = keep[i, :, mine] + rn[i].astype(F32)

        @pl.when(~edge)
        def _():
            copy(i, 2, rc.at[i], rc.at[i], along(last - t)).wait_recv()

        total = keep[i, :, mine] + rc[i].astype(F32)
        out[s, :, pl.ds(pl.multiple_of(128 * f1 + 64 * f2 + 16 * t, 16), 16)] = total.astype(BF16)

        @pl.when(edge)
        def _():
            c_shard(i, 5, last - near).start()
            c_shard(i, 4, near).start()

        @pl.when(~edge)
        def _():
            c_shard(i, 6, last - t).start()
            c_shard(i, 4, side_edge).start()

    def s3b(i):
        @pl.when(~edge)
        def _():
            c_arrive(i, 6, last - t).wait_recv()
            c_arrive(i, 5, last - side_edge).wait_recv()
            c_pass(i).start()
            c_arrive(i, 4, side_edge).wait_recv()
            c_own1(i).start()
            c_own2(i).start()

    def s3c(i):
        @pl.when(edge)
        def _():
            c_arrive(i, 4, near).wait_recv()
            c_arrive(i, 5, jnp.where(t == 0, 2, 0), 2).wait_recv()
            c_own1(i).start()
            c_own2(i).start()

    def s4(i):
        c_own2(i).wait_recv()
        c_on1(i).start()
        c_own1(i).wait_recv()
        c_on2(i).start()

    def s5(i):
        c_on1(i).wait_recv()
        c_on2(i).wait_recv()
        c_coreback(i).start()
        leave(i, h, lambda c: c.start())

    def leave(i, hh, action):
        enc, tap = kind(i // 2, hh)
        side = i % 2
        s = 18 * enc + 2 * tap + side
        slot = jnp.where(hh == h, 0, 1)

        def to(dst):
            return pltpu.make_async_copy(
                out.at[s], dst.at[pl.ds(3 * tap, 3), :, pl.ds(pl.multiple_of(128 * side, 128), 128)], lsem.at[i, slot]
            )

        @pl.when(enc == 1)
        def _():
            action(to(enc_out))

        @pl.when(enc == 0)
        def _():
            action(to(dec_out))

    def s6(i):
        c_coreback(i).wait_recv()
        leave(i, 1 - h, lambda c: c.start())

    stages = [s0, s1, s2, s3, s3b, s3c, s4, s5, s6]

    def body(i, carry):
        for k in ORDER:
            s = i - LAGS[k]

            @pl.when((s >= 0) & (s < STEPS))
            def _(k=k, s=s):
                stages[k](s)

        pl.when(i == STEPS + 1)(finish_output)
        return carry

    lax.fori_loop(0, STEPS + max(LAGS), body, 0)

    def finish(i, carry):
        c_second(i).wait_send()

        @pl.when(edge)
        def _():
            c_hand(i).wait_send()
            c_shard(i, 5, last - near).wait_send()
            c_shard(i, 4, near).wait_send()

        @pl.when(~edge)
        def _():
            c_near(i).wait_send()
            c_cross(i).wait_send()
            c_far(i).wait_send()
            c_shard(i, 6, last - t).wait_send()
            c_shard(i, 4, side_edge).wait_send()
            c_pass(i).wait_send()

        for sent in (c_own1(i), c_own2(i), c_on1(i), c_on2(i), c_coreback(i)):
            sent.wait_send()
        leave(i, h, lambda c: c.wait())
        leave(i, 1 - h, lambda c: c.wait())
        return carry

    lax.fori_loop(0, STEPS, finish, 0)
    for sent in (x_core, g_core, xp_own, xp_own_core, gp_own, gp_own_core, d_core, d_pair, d_pair_core,
                 h_core, h_pair, h_pair_core):
        sent.wait_send()

    @pl.when(inner)
    def _():
        for sent in (g_earlier, x_halo_core, xp_halo, xp_halo_core, gp_halo, h_halo_core):
            sent.wait_send()

    @pl.when(outer)
    def _():
        for sent in (x_later, h_later, g_halo_core, gp_halo_core):
            sent.wait_send()


def whole_step(video, lengths, enc_weight, dec_weight, cotangent):
    vmem, bf = pltpu.VMEM, BF16
    frames, tall, wide, chans = video.shape[1:]
    spots = frames * tall * wide
    ext = (4, 10, wide, chans)
    enc27, dec27 = (w.reshape(27, chans, chans) for w in (enc_weight, dec_weight))
    output, enc_grad, dec_grad = pl.pallas_call(
        step_kernel,
        out_shape=[
            jax.ShapeDtypeStruct(video.shape, bf),
            jax.ShapeDtypeStruct((27, chans, chans), bf),
            jax.ShapeDtypeStruct((27, chans, chans), bf),
        ],
        in_specs=[
            pl.BlockSpec(memory_space=pltpu.SMEM),
            pl.BlockSpec(memory_space=vmem),
            pl.BlockSpec(memory_space=vmem),
            pl.BlockSpec(memory_space=pl.ANY),
            pl.BlockSpec(memory_space=pl.ANY),
        ],
        out_specs=[pl.BlockSpec(memory_space=vmem)] + [pl.BlockSpec(memory_space=pl.ANY)] * 2,
        scratch_shapes=[
            vmem((27, chans, chans), bf),
            vmem((27, chans, chans), bf),
            vmem(ext, bf),
            vmem(ext, bf),
            vmem(ext, bf),
            vmem((frames, 8, wide, chans), bf),
            vmem((4, 10, wide, 128), bf),
            vmem(ext, bf),
            vmem((frames, 8, wide, 128), bf),
            vmem((frames, 8, wide, chans), bf),
            vmem((384, 4 * spots), bf),
            vmem((2, frames, 8, wide, 3 * chans), bf),
            vmem((3, spots, chans), F32),
            vmem((3, spots, chans), F32),
            vmem((spots, chans), F32),
            vmem((2, 3, 128, 128), F32),
            vmem((STEPS, 3, 64, 128), F32),
            vmem((STEPS, 3, 64, 128), bf),
            vmem((STEPS, 3, 64, 128), bf),
            vmem((STEPS, 3, 64, 128), bf),
            vmem((STEPS, 3, 32, 128), bf),
            vmem((STEPS, 3, 48, 128), bf),
            vmem((STEPS, 3, 16, 128), bf),
            vmem((STEPS, 3, 16, 128), bf),
            vmem((36, 3, chans, 128), bf),
            pltpu.SemaphoreType.DMA((2,)),
            pltpu.SemaphoreType.DMA((22,)),
            pltpu.SemaphoreType.DMA((22,)),
            pltpu.SemaphoreType.DMA((STEPS, 12)),
            pltpu.SemaphoreType.DMA((STEPS, 12)),
            pltpu.SemaphoreType.DMA((STEPS, 2)),
        ],
        compiler_params=pltpu.CompilerParams(
            collective_id=0, has_side_effects=True, vmem_limit_bytes=56 * 2**20
        ),
    )(lengths, video, cotangent, enc27, dec27)
    enc_grad, dec_grad = (g.astype(F32).reshape(enc_weight.shape) for g in (enc_grad, dec_grad))
    return output, enc_grad, dec_grad


def shards(video, lengths, enc_weight, dec_weight, cotangent):
    sizes = tuple(lax.axis_size(axis) for axis in ("dp", "tm", "height"))
    if sizes == (4, 4, 2) and video.shape[:3] == (1, 2, 4) and video.shape[-1] == 256:
        return whole_step(video, lengths, enc_weight, dec_weight, cotangent)
    frames = video.shape[1]
    first_frame = lax.axis_index("tm") * frames
    tpos = first_frame + jnp.arange(frames, dtype=jnp.int32)
    keep = (tpos[None, :] < lengths[:, None])[:, :, None, None, None]
    masked = jnp.where(keep, video, jnp.zeros_like(video))
    cot_masked = jnp.where(keep, cotangent, jnp.zeros_like(cotangent))
    ext_x = with_earlier(masked)
    pre = apply_taps(ext_x, enc_weight)
    hidden = jax.nn.silu(pre).astype(jnp.bfloat16)
    ext_h = with_earlier(hidden)
    output = (apply_taps(ext_h, dec_weight) + masked.astype(jnp.float32)).astype(jnp.bfloat16)
    ext_g = with_later(cot_masked)
    chans = dec_weight.shape[3]
    flipped = jnp.transpose(dec_weight[::-1, ::-1, ::-1], (0, 1, 3, 2, 4)).reshape(3, 3, chans, -1)
    dec_local = tap_grads(ext_h, cot_masked)
    back = apply_taps(ext_g, flipped, True)
    dpre = (back * dsilu(pre)).astype(jnp.bfloat16)
    enc_local = tap_grads(ext_x, dpre)
    enc_grad, dec_grad = sum_all(enc_local), sum_all(dec_local)
    return (output, enc_grad, dec_grad)


def solution(mesh):
    in_specs = (
        P("dp", "tm", "height", None, None),
        P("dp"),
        P(),
        P(),
        P("dp", "tm", "height", None, None),
    )
    out_specs = (P("dp", "tm", "height", None, None), P(), P())
    return jax.shard_map(shards, mesh=mesh, in_specs=in_specs, out_specs=out_specs, check_vma=False)
```

```python
import jax
import jax.numpy as jnp
from jax import lax
from jax.experimental import pallas as pl
from jax.experimental.pallas import tpu as pltpu
from jax.sharding import PartitionSpec as P

MESH = pl.DeviceIdType.MESH
ORDER = (8, 7, 6, 5, 4, 3, 2, 1, 0)
LAGS = (0, 5, 8, 12, 15, 17, 21, 25, 28)


def extended(shard, sides, width):
    for axis, dim in sides:
        devices, length = (lax.axis_size(axis), shard.shape[dim])
        up = [(i, (i + 1) % devices) for i in range(devices - 1)]
        down = [(j, i) for i, j in up]
        last = lax.slice_in_dim(shard, length - width, length, axis=dim)
        leading = lax.slice_in_dim(shard, 0, width, axis=dim)
        before = lax.ppermute(last, axis, up)
        after = lax.ppermute(leading, axis, down)
        shard = jnp.concatenate([before, shard, after], axis=dim)
    return shard


def from_behind(block, axis, distance):
    devices = range(lax.axis_size(axis))
    route = [(i - distance, i) for i in devices if i - distance in devices]
    return lax.ppermute(block, axis, route)


def apply_taps(ext, weight, transposed=False):
    count, frame_pad, row_pad, wide, chans = ext.shape
    frames = frame_pad - 2
    rows = row_pad - 2
    outs = weight.shape[2] if transposed else weight.shape[-1]
    padded = jnp.pad(ext, ((0, 0), (0, 0), (0, 0), (1, 1), (0, 0)))
    stacked = jnp.concatenate([padded[:, :, :, e : e + wide, :] for e in range(3)], axis=-1)
    total = jnp.zeros((count * frames * rows * wide, outs), jnp.float32)
    for a in range(3):
        for b in range(3):
            slab = stacked[:, a : a + frames, b : b + rows].reshape(-1, 3 * chans)
            if transposed:
                total = total + lax.dot_general(
                    slab, weight[a, b], (((1,), (1,)), ((), ())), preferred_element_type=jnp.float32
                )
                continue
            total = total + jnp.dot(
                slab, weight[a, b].reshape(3 * chans, outs), preferred_element_type=jnp.float32
            )
    return total.reshape(count, frames, rows, wide, outs)


def tap_grads(ext, cot):
    count, frame_pad, row_pad, wide, chans = ext.shape
    frames = frame_pad - 2
    rows = row_pad - 2
    outs = cot.shape[-1]
    padded = jnp.pad(ext, ((0, 0), (0, 0), (0, 0), (1, 1), (0, 0)))
    stacked = jnp.concatenate([padded[:, :, :, e : e + wide, :] for e in range(3)], axis=-1)
    flat = cot.reshape(-1, outs)
    result = []
    for a in range(3):
        for b in range(3):
            slab = stacked[:, a : a + frames, b : b + rows].reshape(-1, 3 * chans)
            result.append(
                lax.dot_general(
                    slab, flat, (((0,), (0,)), ((), ())), preferred_element_type=jnp.float32
                )
            )
    return jnp.stack(result).reshape(3, 3, 3, chans, outs)


def dsilu(value):
    sig = jax.nn.sigmoid(value)
    return sig * (1.0 + value * (1.0 - sig))


def row_edges(block):
    return extended(block, (("height", 2),), 1)


def with_earlier(block):
    before = from_behind(block, "tm", 1)
    return row_edges(jnp.concatenate([before, block], axis=1))


def with_later(block):
    after = from_behind(block, "tm", -1)
    return row_edges(jnp.concatenate([block, after], axis=1))


def index_bits(axis):
    size = lax.axis_size(axis)
    bits = []
    step = 1
    while step < size:
        bits.append((axis, step))
        step *= 2
    return bits


def swap(block, axis, step):
    return lax.ppermute(block, axis, [(i, i ^ step) for i in range(lax.axis_size(axis))])


def sum_part(part, order):
    trail = []
    for dim, (axis, step) in order:
        upper = lax.rem(lax.axis_index(axis) // step, 2) == 1
        low, high = jnp.split(part, 2, axis=dim)
        keep, give = jnp.where(upper, high, low), jnp.where(upper, low, high)
        got = swap(give.astype(jnp.bfloat16), axis, step)
        part = keep + got.astype(jnp.float32)
        trail.append((dim, axis, step, upper))
    part = part.astype(jnp.bfloat16)
    for dim, axis, step, upper in trail[::-1]:
        got = swap(part, axis, step)
        part = jnp.concatenate([jnp.where(upper, got, part), jnp.where(upper, part, got)], axis=dim)
    return part.astype(jnp.float32)


def sum_all(grad):
    height, dp, tm = index_bits("height"), index_bits("dp"), index_bits("tm")
    rest = height[1:]
    flat = grad.reshape(27, -1, grad.shape[-1])
    sums = []
    at = 0
    for count, order in ((10, dp + tm + rest), (10, dp[::-1] + tm + rest), (7, tm + dp + rest)):
        part = flat[at : at + count]
        at += count
        sums.append(sum_part(part, [(2, height[0])] + [(1, bit) for bit in order]))
    return jnp.concatenate(sums, axis=0).reshape(grad.shape)

ITEMS = 9
STEPS = 2 * ITEMS
F32 = jnp.float32
BF16 = jnp.bfloat16


def step_kernel(
    lengths, video, cot, enc_hbm, dec_hbm, output, enc_out, dec_out,
    wenc, wdec, xe, ge, he, de, xp, gp, hp, dp, ht, ds, ys, yg, slope,
    yb, keep, give, r1, zb, zc, ra, rn, rc, out, wsem, hs, hr, ssem, rsem, lsem,
):
    d, t, h = lax.axis_index("dp"), lax.axis_index("tm"), lax.axis_index("height")
    frames, tall, wide, chans = video.shape[1:]
    last = lax.axis_size("tm") - 1
    xbit, ybit = d % 2, d // 2
    core = (d, t, 1 - h)
    xdev = (d + 1 - 2 * xbit, t, h)
    ydev = (d + 2 - 4 * ybit, t, h)
    later = (d, lax.rem(t + 1, last + 1), h)
    earlier = (d, lax.rem(t + last, last + 1), h)
    spots = frames * tall * wide
    base = tall * h

    w_enc = pltpu.make_async_copy(enc_hbm, wenc, wsem.at[0])
    w_dec = pltpu.make_async_copy(dec_hbm, wdec, wsem.at[1])
    w_enc.start()
    w_dec.start()

    barrier = pltpu.get_barrier_semaphore()
    partners = [core, xdev, ydev] + [(d, lax.rem(t + k, last + 1), h) for k in range(1, 4)]
    for partner in partners:
        pl.semaphore_signal(barrier, inc=1, device_id=partner, device_id_type=MESH)

    rows = pl.ds(1 + base, tall)
    own_rows = pl.ds(base, tall)

    def half(first):
        return pl.ds(pl.multiple_of(128 * first, 128), 128)

    for f in range(frames):
        live = t * frames + f < lengths[0]
        xe[2 + f, rows] = jnp.where(live, video[0, f], jnp.zeros_like(video[0, f]))
        ge[f, rows] = jnp.where(live, cot[0, f], jnp.zeros_like(cot[0, f]))
    pl.semaphore_wait(barrier, len(partners))

    def message(slot, src, dst, target):
        return pltpu.make_async_remote_copy(
            src_ref=src,
            dst_ref=dst,
            send_sem=hs.at[slot],
            recv_sem=hr.at[slot],
            device_id=target,
            device_id_type=MESH,
        )

    def same(slot, ref, target):
        return message(slot, ref, ref, target)

    own, ahead = pl.ds(2, 2), pl.ds(0, 2)
    x_core = same(0, xe.at[own, rows], core)
    g_core = same(1, ge.at[ahead, rows], core)
    x_later = message(2, xe.at[own, rows], xe.at[ahead, rows], later)
    g_earlier = message(3, ge.at[ahead, rows], ge.at[own, rows], earlier)
    x_halo_core = same(4, xe.at[ahead, rows], core)
    g_halo_core = same(5, ge.at[own, rows], core)
    xp_own = message(6, xe.at[own, rows, :, half(1 - ybit)], xp.at[own, rows], ydev)
    xp_own_core = same(7, xp.at[own, rows], core)
    xp_halo = message(8, xe.at[ahead, rows, :, half(1 - ybit)], xp.at[ahead, rows], ydev)
    xp_halo_core = same(9, xp.at[ahead, rows], core)
    gp_own = message(10, ge.at[ahead, rows], gp.at[ahead, rows], xdev)
    gp_own_core = same(11, gp.at[ahead, rows], core)
    gp_halo = message(12, gp.at[ahead, rows], gp.at[own, rows], earlier)
    gp_halo_core = same(13, gp.at[own, rows], core)
    d_core = same(14, de.at[:, own_rows], core)
    d_pair = message(15, de.at[:, own_rows], dp.at[:, own_rows], ydev)
    d_pair_core = same(16, dp.at[:, own_rows], core)
    h_core = same(17, he.at[own, rows], core)
    h_later = message(18, he.at[own, rows], he.at[ahead, rows], later)
    h_halo_core = same(19, he.at[ahead, rows], core)
    h_pair = message(20, he.at[own, rows, :, half(1 - xbit)], hp.at[:, own_rows], xdev)
    h_pair_core = same(21, hp.at[:, own_rows], core)

    def when(cond, action):
        pl.when(cond)(action)

    inner, outer = t > 0, t < last
    when(outer, lambda: x_later.start())
    when(inner, lambda: g_earlier.start())
    x_core.start()
    g_core.start()
    gp_own.start()
    xp_own.start()

    for ref in (xe, ge, he, xp, gp):
        for edge in (0, 9):
            ref[:, edge] = jnp.zeros((4,) + ref.shape[2:], BF16)

    @pl.when(t == 0)
    def _():
        for ref in (xe, he, xp):
            ref[0:2] = jnp.zeros((2,) + ref.shape[1:], BF16)

    @pl.when(t == last)
    def _():
        for ref in (ge, gp):
            ref[2:4] = jnp.zeros((2,) + ref.shape[1:], BF16)

    def shifted(value, by):
        count = value.shape[0]
        column = lax.broadcasted_iota(jnp.int32, value.shape, 0) % wide
        moved = pltpu.roll(value, by % count, axis=0)
        return jnp.where(column == (0 if by == 1 else wide - 1), 0.0, moved)

    def partial_conv(acc, src, weight, taps, transposed, fresh):
        for e in range(3):
            total = None
            for a in taps:
                first = 2 - a if transposed else a
                for b in range(3):
                    down = 2 - b if transposed else b
                    slab = src[first : first + 2, pl.ds(base + down, tall)].reshape(spots, chans)
                    dims = (((1,), (1 if transposed else 0,)), ((), ()))
                    term = lax.dot_general(slab, weight[9 * a + 3 * b + e], dims, preferred_element_type=F32)
                    total = term if total is None else total + term
            if fresh:
                acc[e] = total
            else:
                acc[e] = acc[e] + total

    def joined(acc, transposed):
        one = -1 if transposed else 1
        return acc[1] + shifted(acc[0], one) + shifted(acc[2], -one)

    w_enc.wait()
    x_core.wait_recv()
    partial_conv(ys, xe, wenc, (2,), False, True)
    w_dec.wait()
    g_core.wait_recv()
    partial_conv(yg, ge, wdec, (2,), True, True)

    @pl.when(inner)
    def _():
        x_later.wait_recv()
        x_halo_core.start()
        xp_halo.start()
        x_halo_core.wait_recv()

    partial_conv(ys, xe, wenc, (1, 0), False, False)
    pre = joined(ys, False)
    sig = jax.nn.sigmoid(pre)
    hidden = (pre * sig).astype(BF16)
    slope[...] = sig * (1.0 + pre * (1.0 - sig))
    he[2:4, rows] = hidden.reshape(frames, tall, wide, chans)
    h_pair.start()
    h_core.start()
    when(outer, lambda: h_later.start())

    gp_own.wait_recv()
    gp_own_core.start()
    when(inner, lambda: gp_halo.start())
    xp_own.wait_recv()
    xp_own_core.start()

    @pl.when(outer)
    def _():
        g_earlier.wait_recv()
        g_halo_core.start()
        g_halo_core.wait_recv()

    partial_conv(yg, ge, wdec, (1, 0), True, False)
    de[:, own_rows] = (joined(yg, True) * slope[...]).astype(BF16).reshape(frames, tall, wide, chans)
    d_pair.start()
    d_core.start()

    chip = 2 * spots

    def turned(value, at):
        value = value.astype(F32)
        for e in range(3):
            moved = value if e == 1 else shifted(value, 1 if e == 0 else -1)
            ht[pl.ds(128 * e, 128), pl.ds(at * chip, chip)] = moved.T.astype(BF16)

    h_core.wait_recv()
    turned(he[2:4, 1:9, :, half(xbit)].reshape(chip, 128), 0)
    h_pair.wait_recv()
    h_pair_core.start()

    @pl.when(inner)
    def _():
        xp_halo.wait_recv()
        xp_halo_core.start()

    h_pair_core.wait_recv()
    turned(hp[...].reshape(chip, 128), 1)
    gp_own_core.wait_recv()

    def spread(value, at):
        value = value.astype(F32)
        for e in range(3):
            moved = value if e == 1 else shifted(value, -1 if e == 0 else 1)
            ds[at, :, :, :, pl.ds(chans * e, chans)] = moved.astype(BF16).reshape(frames, 8, wide, chans)

    def kind(i, hh):
        start = ITEMS // 2 + 1 - hh
        enc = jnp.where(i >= start, 1, 0)
        before = jnp.maximum(i - start, 0)
        tap = jnp.where(enc == 1, 7 + hh - 2 * before, 8 - hh - 2 * (i - before))
        return enc, tap

    def places(i):
        enc, tap = kind(i // 2, h)
        f1 = jnp.where(enc == 1, ybit, xbit)
        f2 = jnp.where(enc == 1, xbit, ybit)
        dx, dy = d + 1 - 2 * xbit, d + 2 - 4 * ybit
        p1 = (jnp.where(enc == 1, dy, dx), t, h)
        p2 = (jnp.where(enc == 1, dx, dy), t, h)
        return 18 * enc + 2 * tap + i % 2, f1, f2, p1, p2

    def copy(i, slot, src, dst, target):
        return pltpu.make_async_remote_copy(
            src_ref=src,
            dst_ref=dst,
            send_sem=ssem.at[slot],
            recv_sem=rsem.at[i, slot],
            device_id=target,
            device_id_type=MESH,
        )

    def part(ref, i, first, count):
        return ref.at[i, :, pl.ds(pl.multiple_of(first, 16), count)]

    edge = (t == 0) | (t == last)
    near = jnp.where(t == 0, 1, 2)
    side_edge = jnp.where(t == 1, 0, last)

    def along(other):
        return (d, other, h)

    def c_second(i):
        _, _, _, _, p2 = places(i)
        return copy(i, 0, give.at[i], r1.at[i], p2)

    def c_hand(i):
        return copy(i, 1, part(zb, i, jnp.where(t == 0, 16, 0), 48), ra.at[i], along(near))

    def c_near(i):
        return copy(i, 1, part(zb, i, 16 * side_edge, 16), rn.at[i], along(side_edge))

    def c_cross(i):
        return copy(i, 2, part(zc, i, jnp.where(t == 1, 0, 16), 16), rc.at[i], along(last - t))

    def c_far(i):
        return copy(i, 3, part(zc, i, jnp.where(t == 1, 16, 0), 16), rc.at[i], along(last - side_edge))

    def shard(i, owner, count=1):
        s, f1, f2, _, _ = places(i)
        return part(out, s, 128 * f1 + 64 * f2 + 16 * owner, 16 * count)

    def c_shard(i, slot, other):
        return copy(i, slot, shard(i, t), shard(i, t), along(other))

    def c_arrive(i, slot, owner, count=1):
        return copy(i, slot, shard(i, owner, count), shard(i, owner, count), along(owner))

    def c_pass(i):
        here = shard(i, jnp.where(t == 1, 2, 0), 2)
        return copy(i, 5, here, here, along(side_edge))

    def piece(i, flip1, flip2, first, count):
        s, f1, f2, _, _ = places(i)
        g1, g2 = (1 - f1 if flip1 else f1), (1 - f2 if flip2 else f2)
        return part(out, s, 128 * g1 + 64 * g2 + first, count)

    def gather(i, slot, here, which):
        return copy(i, slot, here, here, places(i)[which])

    def c_own2(i):
        return gather(i, 7, piece(i, False, False, 0, 64), 4)

    def c_own1(i):
        return gather(i, 8, piece(i, False, False, 0, 64), 3)

    def c_on1(i):
        return gather(i, 9, piece(i, False, True, 0, 32), 3)

    def c_on2(i):
        return gather(i, 10, piece(i, True, False, 32, 32), 4)

    def c_coreback(i):
        s = places(i)[0]
        return copy(i, 11, out.at[s], out.at[s], core)

    def dec_slab(tap):
        a = tap // 3
        b = tap % 3
        total = None
        for at, ref in ((0, ge), (1, gp)):
            slab = ref[pl.ds(2 - a, 2), pl.ds(2 - b, 8)].reshape(chip, chans)
            term = jnp.dot(ht[:, at * chip : (at + 1) * chip], slab, preferred_element_type=F32)
            total = term if total is None else total + term
        for e in range(3):
            for side in range(2):
                yb[side, e] = total[128 * e : 128 * (e + 1), 128 * side : 128 * (side + 1)]

    def enc_slab(tap):
        a = tap // 3
        b = tap % 3
        total = None
        for at in range(2):
            if at == 0:
                slab = xe[pl.ds(a, 2), pl.ds(b, 8), :, half(ybit)]
            else:
                slab = xp[pl.ds(a, 2), pl.ds(b, 8)]
            term = lax.dot_general(
                slab.reshape(chip, 128),
                ds[at].reshape(chip, 3 * chans),
                (((0,), (0,)), ((), ())),
                preferred_element_type=F32,
            )
            total = term if total is None else total + term
        for e in range(3):
            for side in range(2):
                at = chans * e + 128 * side
                yb[side, e] = total[:, at : at + 128]

    def items(i):
        enc, tap = kind(i, h)

        @pl.when(i == 1)
        def _():
            @pl.when(outer)
            def _():
                gp_halo.wait_recv()
                gp_halo_core.start()
                gp_halo_core.wait_recv()

        @pl.when((i == 2) & inner)
        def _():
            h_later.wait_recv()
            h_halo_core.start()

        @pl.when(i == 2)
        def _():
            d_core.wait_recv()
            spread(de[...].reshape(chip, chans), 0)
            d_pair.wait_recv()
            d_pair_core.start()

        @pl.when(i == 4)
        def _():
            xp_own_core.wait_recv()
            when(inner, lambda: xp_halo_core.wait_recv())
            d_pair_core.wait_recv()
            spread(dp[...].reshape(chip, chans), 1)

        @pl.when(enc == 0)
        def _():
            dec_slab(tap)

        @pl.when(enc == 1)
        def _():
            enc_slab(tap)

    def finish_output():
        @pl.when(inner)
        def _():
            h_halo_core.wait_recv()

        partial_conv(ys, he, wdec, (0, 1, 2), False, True)
        total = joined(ys, False) + xe[2:4, rows].reshape(spots, chans).astype(F32)
        output[0] = total.astype(BF16).reshape(frames, tall, wide, chans)

    def s0(i):
        @pl.when(i % 2 == 0)
        def _():
            items(i // 2)

        _, _, f2, _, _ = places(i)
        side = i % 2
        keep[i] = yb[side, :, pl.ds(pl.multiple_of(64 * f2, 64), 64)]
        give[i] = yb[side, :, pl.ds(pl.multiple_of(64 * (1 - f2), 64), 64)].astype(BF16)
        c_second(i).start()

    def s1(i):
        c_second(i).wait_recv()
        total = keep[i] + r1[i].astype(F32)
        keep[i] = total
        zb[i] = total.astype(BF16)
        when(edge, lambda: c_hand(i).start())
        when(~edge, lambda: c_near(i).start())

    def s2(i):
        @pl.when(~edge)
        def _():
            copy(i, 1, ra.at[i], ra.at[i], along(side_edge)).wait_recv()
            low = jnp.where(t == 1, 16, 0)
            at = pl.ds(pl.multiple_of(low, 16), 48)
            keep[i, :, at] = keep[i, :, at] + ra[i].astype(F32)
            zc[i] = keep[i, :, pl.ds(pl.multiple_of(2 * low, 16), 32)].astype(BF16)
            c_cross(i).start()
            c_far(i).start()

    def s3(i):
        s, f1, f2, _, _ = places(i)
        mine = pl.ds(pl.multiple_of(16 * t, 16), 16)

        @pl.when(edge)
        def _():
            copy(i, 1, rn.at[i], rn.at[i], along(near)).wait_recv()
            copy(i, 3, rc.at[i], rc.at[i], along(last - near)).wait_recv()
            keep[i, :, mine] = keep[i, :, mine] + rn[i].astype(F32)

        @pl.when(~edge)
        def _():
            copy(i, 2, rc.at[i], rc.at[i], along(last - t)).wait_recv()

        total = keep[i, :, mine] + rc[i].astype(F32)
        out[s, :, pl.ds(pl.multiple_of(128 * f1 + 64 * f2 + 16 * t, 16), 16)] = total.astype(BF16)

        @pl.when(edge)
        def _():
            c_shard(i, 5, last - near).start()
            c_shard(i, 4, near).start()

        @pl.when(~edge)
        def _():
            c_shard(i, 6, last - t).start()
            c_shard(i, 4, side_edge).start()

    def s3b(i):
        @pl.when(~edge)
        def _():
            c_arrive(i, 6, last - t).wait_recv()
            c_arrive(i, 5, last - side_edge).wait_recv()
            c_pass(i).start()
            c_arrive(i, 4, side_edge).wait_recv()
            c_own1(i).start()
            c_own2(i).start()

    def s3c(i):
        @pl.when(edge)
        def _():
            c_arrive(i, 4, near).wait_recv()
            c_arrive(i, 5, jnp.where(t == 0, 2, 0), 2).wait_recv()
            c_own1(i).start()
            c_own2(i).start()

    def s4(i):
        c_own2(i).wait_recv()
        c_on1(i).start()
        c_own1(i).wait_recv()
        c_on2(i).start()

    def s5(i):
        c_on1(i).wait_recv()
        c_on2(i).wait_recv()
        c_coreback(i).start()
        leave(i, h, lambda c: c.start())

    def leave(i, hh, action):
        enc, tap = kind(i // 2, hh)
        side = i % 2
        s = 18 * enc + 2 * tap + side
        slot = jnp.where(hh == h, 0, 1)

        def to(dst):
            return pltpu.make_async_copy(
                out.at[s], dst.at[pl.ds(3 * tap, 3), :, pl.ds(pl.multiple_of(128 * side, 128), 128)], lsem.at[i, slot]
            )

        @pl.when(enc == 1)
        def _():
            action(to(enc_out))

        @pl.when(enc == 0)
        def _():
            action(to(dec_out))

    def s6(i):
        c_coreback(i).wait_recv()
        leave(i, 1 - h, lambda c: c.start())

    stages = [s0, s1, s2, s3, s3b, s3c, s4, s5, s6]

    def body(i, carry):
        for k in ORDER:
            s = i - LAGS[k]

            @pl.when((s >= 0) & (s < STEPS))
            def _(k=k, s=s):
                stages[k](s)

        pl.when(i == STEPS + 1)(finish_output)
        return carry

    lax.fori_loop(0, STEPS + max(LAGS), body, 0)

    def sent_all(slot, ref):
        copy(0, slot, ref, ref, core).wait_send()

    halves = out.at[pl.ds(0, STEPS)]
    sent_all(0, give)
    sent_all(7, give)
    sent_all(8, give)
    sent_all(9, zc)
    sent_all(10, zc)
    sent_all(11, halves)

    @pl.when(edge)
    def _():
        sent_all(1, ra)
        sent_all(4, rn)
        sent_all(5, rn)

    @pl.when(~edge)
    def _():
        sent_all(1, rn)
        sent_all(2, rn)
        sent_all(3, rn)
        sent_all(4, rn)
        sent_all(5, zc)
        sent_all(6, rn)


    def left(i, carry):
        leave(i, h, lambda c: c.wait())
        leave(i, 1 - h, lambda c: c.wait())
        return carry

    lax.fori_loop(0, STEPS, left, 0)
    for sent in (x_core, g_core, xp_own, xp_own_core, gp_own, gp_own_core, d_core, d_pair, d_pair_core,
                 h_core, h_pair, h_pair_core):
        sent.wait_send()

    @pl.when(inner)
    def _():
        for sent in (g_earlier, x_halo_core, xp_halo, xp_halo_core, gp_halo, h_halo_core):
            sent.wait_send()

    @pl.when(outer)
    def _():
        for sent in (x_later, h_later, g_halo_core, gp_halo_core):
            sent.wait_send()


def widen_kernel(output, enc_sum, dec_sum, output_out, enc_out, dec_out):
    @pl.when(pl.program_id(0) == 0)
    def _():
        output_out[...] = output[...]

    enc_out[...] = enc_sum[...].astype(F32)
    dec_out[...] = dec_sum[...].astype(F32)


def whole_step(video, lengths, enc_weight, dec_weight, cotangent):
    vmem, bf = pltpu.VMEM, BF16
    frames, tall, wide, chans = video.shape[1:]
    spots = frames * tall * wide
    ext = (4, 10, wide, chans)
    enc27, dec27 = (w.reshape(27, chans, chans) for w in (enc_weight, dec_weight))
    output, enc_grad, dec_grad = pl.pallas_call(
        step_kernel,
        out_shape=[
            jax.ShapeDtypeStruct(video.shape, bf),
            jax.ShapeDtypeStruct((27, chans, chans), bf),
            jax.ShapeDtypeStruct((27, chans, chans), bf),
        ],
        in_specs=[
            pl.BlockSpec(memory_space=pltpu.SMEM),
            pl.BlockSpec(memory_space=vmem),
            pl.BlockSpec(memory_space=vmem),
            pl.BlockSpec(memory_space=pl.ANY),
            pl.BlockSpec(memory_space=pl.ANY),
        ],
        out_specs=[pl.BlockSpec(memory_space=vmem)] + [pl.BlockSpec(memory_space=pl.ANY)] * 2,
        scratch_shapes=[
            vmem((27, chans, chans), bf),
            vmem((27, chans, chans), bf),
            vmem(ext, bf),
            vmem(ext, bf),
            vmem(ext, bf),
            vmem((frames, 8, wide, chans), bf),
            vmem((4, 10, wide, 128), bf),
            vmem(ext, bf),
            vmem((frames, 8, wide, 128), bf),
            vmem((frames, 8, wide, chans), bf),
            vmem((384, 4 * spots), bf),
            vmem((2, frames, 8, wide, 3 * chans), bf),
            vmem((3, spots, chans), F32),
            vmem((3, spots, chans), F32),
            vmem((spots, chans), F32),
            vmem((2, 3, 128, 128), F32),
            vmem((STEPS, 3, 64, 128), F32),
            vmem((STEPS, 3, 64, 128), bf),
            vmem((STEPS, 3, 64, 128), bf),
            vmem((STEPS, 3, 64, 128), bf),
            vmem((STEPS, 3, 32, 128), bf),
            vmem((STEPS, 3, 48, 128), bf),
            vmem((STEPS, 3, 16, 128), bf),
            vmem((STEPS, 3, 16, 128), bf),
            vmem((36, 3, chans, 128), bf),
            pltpu.SemaphoreType.DMA((2,)),
            pltpu.SemaphoreType.DMA((22,)),
            pltpu.SemaphoreType.DMA((22,)),
            pltpu.SemaphoreType.DMA((12,)),
            pltpu.SemaphoreType.DMA((STEPS, 12)),
            pltpu.SemaphoreType.DMA((STEPS, 2)),
        ],
        compiler_params=pltpu.CompilerParams(
            collective_id=0, has_side_effects=True, vmem_limit_bytes=56 * 2**20
        ),
    )(lengths, video, cotangent, enc27, dec27)
    taps = pl.BlockSpec((9, chans, chans), lambda i: (i, 0, 0))
    whole = pl.BlockSpec(video.shape, lambda i: (0,) * 5)
    output, enc_grad, dec_grad = pl.pallas_call(
        widen_kernel,
        grid=(3,),
        in_specs=[whole, taps, taps],
        out_specs=[whole, taps, taps],
        out_shape=[jax.ShapeDtypeStruct(video.shape, bf)] + [jax.ShapeDtypeStruct(enc27.shape, F32)] * 2,
        compiler_params=pltpu.CompilerParams(vmem_limit_bytes=56 * 2**20),
    )(output, enc_grad, dec_grad)
    return output, enc_grad.reshape(enc_weight.shape), dec_grad.reshape(dec_weight.shape)


def shards(video, lengths, enc_weight, dec_weight, cotangent):
    sizes = tuple(lax.axis_size(axis) for axis in ("dp", "tm", "height"))
    if sizes == (4, 4, 2) and video.shape[:3] == (1, 2, 4) and video.shape[-1] == 256:
        return whole_step(video, lengths, enc_weight, dec_weight, cotangent)
    frames = video.shape[1]
    first_frame = lax.axis_index("tm") * frames
    tpos = first_frame + jnp.arange(frames, dtype=jnp.int32)
    keep = (tpos[None, :] < lengths[:, None])[:, :, None, None, None]
    masked = jnp.where(keep, video, jnp.zeros_like(video))
    cot_masked = jnp.where(keep, cotangent, jnp.zeros_like(cotangent))
    ext_x = with_earlier(masked)
    pre = apply_taps(ext_x, enc_weight)
    hidden = jax.nn.silu(pre).astype(jnp.bfloat16)
    ext_h = with_earlier(hidden)
    output = (apply_taps(ext_h, dec_weight) + masked.astype(jnp.float32)).astype(jnp.bfloat16)
    ext_g = with_later(cot_masked)
    chans = dec_weight.shape[3]
    flipped = jnp.transpose(dec_weight[::-1, ::-1, ::-1], (0, 1, 3, 2, 4)).reshape(3, 3, chans, -1)
    dec_local = tap_grads(ext_h, cot_masked)
    back = apply_taps(ext_g, flipped, True)
    dpre = (back * dsilu(pre)).astype(jnp.bfloat16)
    enc_local = tap_grads(ext_x, dpre)
    enc_grad, dec_grad = sum_all(enc_local), sum_all(dec_local)
    return (output, enc_grad, dec_grad)


def solution(mesh):
    in_specs = (
        P("dp", "tm", "height", None, None),
        P("dp"),
        P(),
        P(),
        P("dp", "tm", "height", None, None),
    )
    out_specs = (P("dp", "tm", "height", None, None), P(), P())
    return jax.shard_map(shards, mesh=mesh, in_specs=in_specs, out_specs=out_specs, check_vma=False)
```

```python
import jax
import jax.numpy as jnp
from jax import lax
from jax.experimental import pallas as pl
from jax.experimental.pallas import tpu as pltpu
from jax.sharding import PartitionSpec as P

MESH = pl.DeviceIdType.MESH
WIDE = 9
ORDER = (8, 7, 6, 5, 4, 3, 2, 1, 0)
LAGS = (0, 5, 8, 12, 15, 17, 21, 25, 28)


def extended(shard, sides, width):
    for axis, dim in sides:
        devices, length = (lax.axis_size(axis), shard.shape[dim])
        up = [(i, (i + 1) % devices) for i in range(devices - 1)]
        down = [(j, i) for i, j in up]
        last = lax.slice_in_dim(shard, length - width, length, axis=dim)
        leading = lax.slice_in_dim(shard, 0, width, axis=dim)
        before = lax.ppermute(last, axis, up)
        after = lax.ppermute(leading, axis, down)
        shard = jnp.concatenate([before, shard, after], axis=dim)
    return shard


def from_behind(block, axis, distance):
    devices = range(lax.axis_size(axis))
    route = [(i - distance, i) for i in devices if i - distance in devices]
    return lax.ppermute(block, axis, route)


def apply_taps(ext, weight, transposed=False):
    count, frame_pad, row_pad, wide, chans = ext.shape
    frames = frame_pad - 2
    rows = row_pad - 2
    outs = weight.shape[2] if transposed else weight.shape[-1]
    padded = jnp.pad(ext, ((0, 0), (0, 0), (0, 0), (1, 1), (0, 0)))
    stacked = jnp.concatenate([padded[:, :, :, e : e + wide, :] for e in range(3)], axis=-1)
    total = jnp.zeros((count * frames * rows * wide, outs), jnp.float32)
    for a in range(3):
        for b in range(3):
            slab = stacked[:, a : a + frames, b : b + rows].reshape(-1, 3 * chans)
            if transposed:
                total = total + lax.dot_general(
                    slab, weight[a, b], (((1,), (1,)), ((), ())), preferred_element_type=jnp.float32
                )
                continue
            total = total + jnp.dot(
                slab, weight[a, b].reshape(3 * chans, outs), preferred_element_type=jnp.float32
            )
    return total.reshape(count, frames, rows, wide, outs)


def tap_grads(ext, cot):
    count, frame_pad, row_pad, wide, chans = ext.shape
    frames = frame_pad - 2
    rows = row_pad - 2
    outs = cot.shape[-1]
    padded = jnp.pad(ext, ((0, 0), (0, 0), (0, 0), (1, 1), (0, 0)))
    stacked = jnp.concatenate([padded[:, :, :, e : e + wide, :] for e in range(3)], axis=-1)
    flat = cot.reshape(-1, outs)
    result = []
    for a in range(3):
        for b in range(3):
            slab = stacked[:, a : a + frames, b : b + rows].reshape(-1, 3 * chans)
            result.append(
                lax.dot_general(
                    slab, flat, (((0,), (0,)), ((), ())), preferred_element_type=jnp.float32
                )
            )
    return jnp.stack(result).reshape(3, 3, 3, chans, outs)


def dsilu(value):
    sig = jax.nn.sigmoid(value)
    return sig * (1.0 + value * (1.0 - sig))


def row_edges(block):
    return extended(block, (("height", 2),), 1)


def with_earlier(block):
    before = from_behind(block, "tm", 1)
    return row_edges(jnp.concatenate([before, block], axis=1))


def with_later(block):
    after = from_behind(block, "tm", -1)
    return row_edges(jnp.concatenate([block, after], axis=1))


def index_bits(axis):
    size = lax.axis_size(axis)
    bits = []
    step = 1
    while step < size:
        bits.append((axis, step))
        step *= 2
    return bits


def swap(block, axis, step):
    return lax.ppermute(block, axis, [(i, i ^ step) for i in range(lax.axis_size(axis))])


def sum_part(part, order):
    trail = []
    for dim, (axis, step) in order:
        upper = lax.rem(lax.axis_index(axis) // step, 2) == 1
        low, high = jnp.split(part, 2, axis=dim)
        keep, give = jnp.where(upper, high, low), jnp.where(upper, low, high)
        got = swap(give.astype(jnp.bfloat16), axis, step)
        part = keep + got.astype(jnp.float32)
        trail.append((dim, axis, step, upper))
    part = part.astype(jnp.bfloat16)
    for dim, axis, step, upper in trail[::-1]:
        got = swap(part, axis, step)
        part = jnp.concatenate([jnp.where(upper, got, part), jnp.where(upper, part, got)], axis=dim)
    return part.astype(jnp.float32)


def sum_all(grad):
    height, dp, tm = index_bits("height"), index_bits("dp"), index_bits("tm")
    rest = height[1:]
    flat = grad.reshape(27, -1, grad.shape[-1])
    sums = []
    at = 0
    for count, order in ((10, dp + tm + rest), (10, dp[::-1] + tm + rest), (7, tm + dp + rest)):
        part = flat[at : at + count]
        at += count
        sums.append(sum_part(part, [(2, height[0])] + [(1, bit) for bit in order]))
    return jnp.concatenate(sums, axis=0).reshape(grad.shape)

ITEMS = 9
STEPS = 2 * ITEMS
F32 = jnp.float32
BF16 = jnp.bfloat16


def step_kernel(
    lengths, video, cot, enc_hbm, dec_hbm, output, out,
    wenc, wdec, xe, ge, he, de, xp, gp, hp, dp, ht, ds, ys, yg, slope,
    yb, keep, give, r1, zb, zc, ra, rn, rc, wsem, hs, hr, ssem, rsem,
):
    d, t, h = lax.axis_index("dp"), lax.axis_index("tm"), lax.axis_index("height")
    frames, tall, wide, chans = video.shape[1:]
    last = lax.axis_size("tm") - 1
    xbit, ybit = d % 2, d // 2
    core = (d, t, 1 - h)
    xdev = (d + 1 - 2 * xbit, t, h)
    ydev = (d + 2 - 4 * ybit, t, h)
    later = (d, lax.rem(t + 1, last + 1), h)
    earlier = (d, lax.rem(t + last, last + 1), h)
    spots = frames * tall * wide
    base = tall * h

    w_enc = pltpu.make_async_copy(enc_hbm, wenc, wsem.at[0])
    w_dec = pltpu.make_async_copy(dec_hbm, wdec, wsem.at[1])
    w_enc.start()
    w_dec.start()

    barrier = pltpu.get_barrier_semaphore()
    partners = [core, xdev, ydev] + [(d, lax.rem(t + k, last + 1), h) for k in range(1, 4)]
    for partner in partners:
        pl.semaphore_signal(barrier, inc=1, device_id=partner, device_id_type=MESH)

    rows = pl.ds(1 + base, tall)
    own_rows = pl.ds(base, tall)

    def half(first):
        return pl.ds(pl.multiple_of(128 * first, 128), 128)

    for f in range(frames):
        live = t * frames + f < lengths[0]
        xe[2 + f, rows] = jnp.where(live, video[0, f], jnp.zeros_like(video[0, f]))
        ge[f, rows] = jnp.where(live, cot[0, f], jnp.zeros_like(cot[0, f]))
    pl.semaphore_wait(barrier, len(partners))

    def message(slot, src, dst, target):
        return pltpu.make_async_remote_copy(
            src_ref=src,
            dst_ref=dst,
            send_sem=hs.at[slot],
            recv_sem=hr.at[slot],
            device_id=target,
            device_id_type=MESH,
        )

    def same(slot, ref, target):
        return message(slot, ref, ref, target)

    own, ahead = pl.ds(2, 2), pl.ds(0, 2)
    x_core = same(0, xe.at[own, rows], core)
    g_core = same(1, ge.at[ahead, rows], core)
    x_later = message(2, xe.at[own, rows], xe.at[ahead, rows], later)
    g_earlier = message(3, ge.at[ahead, rows], ge.at[own, rows], earlier)
    x_halo_core = same(4, xe.at[ahead, rows], core)
    g_halo_core = same(5, ge.at[own, rows], core)
    xp_own = message(6, xe.at[own, rows, :, half(1 - ybit)], xp.at[own, rows], ydev)
    xp_own_core = same(7, xp.at[own, rows], core)
    xp_halo = message(8, xe.at[ahead, rows, :, half(1 - ybit)], xp.at[ahead, rows], ydev)
    xp_halo_core = same(9, xp.at[ahead, rows], core)
    gp_own = message(10, ge.at[ahead, rows], gp.at[ahead, rows], xdev)
    gp_own_core = same(11, gp.at[ahead, rows], core)
    gp_halo = message(12, gp.at[ahead, rows], gp.at[own, rows], earlier)
    gp_halo_core = same(13, gp.at[own, rows], core)
    d_core = same(14, de.at[:, own_rows], core)
    d_pair = message(15, de.at[:, own_rows], dp.at[:, own_rows], ydev)
    d_pair_core = same(16, dp.at[:, own_rows], core)
    h_core = same(17, he.at[own, rows], core)
    h_later = message(18, he.at[own, rows], he.at[ahead, rows], later)
    h_halo_core = same(19, he.at[ahead, rows], core)
    h_pair = message(20, he.at[own, rows, :, half(1 - xbit)], hp.at[:, own_rows], xdev)
    h_pair_core = same(21, hp.at[:, own_rows], core)

    def when(cond, action):
        pl.when(cond)(action)

    inner, outer = t > 0, t < last
    when(outer, lambda: x_later.start())
    when(inner, lambda: g_earlier.start())
    x_core.start()
    g_core.start()
    gp_own.start()
    xp_own.start()

    for ref in (xe, ge, he, xp, gp):
        for edge in (0, 9):
            ref[:, edge] = jnp.zeros((4,) + ref.shape[2:], BF16)

    @pl.when(t == 0)
    def _():
        for ref in (xe, he, xp):
            ref[0:2] = jnp.zeros((2,) + ref.shape[1:], BF16)

    @pl.when(t == last)
    def _():
        for ref in (ge, gp):
            ref[2:4] = jnp.zeros((2,) + ref.shape[1:], BF16)

    def shifted(value, by):
        count = value.shape[0]
        column = lax.broadcasted_iota(jnp.int32, value.shape, 0) % wide
        moved = pltpu.roll(value, by % count, axis=0)
        return jnp.where(column == (0 if by == 1 else wide - 1), 0.0, moved)

    def partial_conv(acc, src, weight, taps, transposed, fresh):
        for e in range(3):
            total = None
            for a in taps:
                first = 2 - a if transposed else a
                for b in range(3):
                    down = 2 - b if transposed else b
                    slab = src[first : first + 2, pl.ds(base + down, tall)].reshape(spots, chans)
                    dims = (((1,), (1 if transposed else 0,)), ((), ()))
                    term = lax.dot_general(slab, weight[9 * a + 3 * b + e], dims, preferred_element_type=F32)
                    total = term if total is None else total + term
            if fresh:
                acc[e] = total
            else:
                acc[e] = acc[e] + total

    def joined(acc, transposed):
        one = -1 if transposed else 1
        return acc[1] + shifted(acc[0], one) + shifted(acc[2], -one)

    w_enc.wait()
    x_core.wait_recv()
    partial_conv(ys, xe, wenc, (2,), False, True)
    w_dec.wait()
    g_core.wait_recv()
    partial_conv(yg, ge, wdec, (2,), True, True)

    @pl.when(inner)
    def _():
        x_later.wait_recv()
        x_halo_core.start()
        xp_halo.start()
        x_halo_core.wait_recv()

    partial_conv(ys, xe, wenc, (1, 0), False, False)
    pre = joined(ys, False)
    sig = jax.nn.sigmoid(pre)
    hidden = (pre * sig).astype(BF16)
    slope[...] = sig * (1.0 + pre * (1.0 - sig))
    he[2:4, rows] = hidden.reshape(frames, tall, wide, chans)
    h_pair.start()
    h_core.start()
    when(outer, lambda: h_later.start())

    gp_own.wait_recv()
    gp_own_core.start()
    when(inner, lambda: gp_halo.start())
    xp_own.wait_recv()
    xp_own_core.start()

    @pl.when(outer)
    def _():
        g_earlier.wait_recv()
        g_halo_core.start()
        g_halo_core.wait_recv()

    partial_conv(yg, ge, wdec, (1, 0), True, False)
    de[:, own_rows] = (joined(yg, True) * slope[...]).astype(BF16).reshape(frames, tall, wide, chans)
    d_pair.start()
    d_core.start()

    chip = 2 * spots

    def turned(value, at):
        value = value.astype(F32)
        for e in range(3):
            moved = value if e == 1 else shifted(value, 1 if e == 0 else -1)
            ht[pl.ds(128 * e, 128), pl.ds(at * chip, chip)] = moved.T.astype(BF16)

    h_core.wait_recv()
    turned(he[2:4, 1:9, :, half(xbit)].reshape(chip, 128), 0)
    h_pair.wait_recv()
    h_pair_core.start()

    @pl.when(inner)
    def _():
        xp_halo.wait_recv()
        xp_halo_core.start()

    h_pair_core.wait_recv()
    turned(hp[...].reshape(chip, 128), 1)
    gp_own_core.wait_recv()

    def spread(value, at):
        value = value.astype(F32)
        for e in range(3):
            moved = value if e == 1 else shifted(value, -1 if e == 0 else 1)
            ds[at, :, :, :, pl.ds(chans * e, chans)] = moved.astype(BF16).reshape(frames, 8, wide, chans)

    def kind(i, hh):
        start = ITEMS // 2 + 1 - hh
        enc = jnp.where(i >= start, 1, 0)
        before = jnp.maximum(i - start, 0)
        tap = jnp.where(enc == 1, 7 + hh - 2 * before, 8 - hh - 2 * (i - before))
        return enc, tap

    def places(i):
        enc, tap = kind(i // 2, h)
        f1 = jnp.where(enc == 1, ybit, xbit)
        f2 = jnp.where(enc == 1, xbit, ybit)
        dx, dy = d + 1 - 2 * xbit, d + 2 - 4 * ybit
        p1 = (jnp.where(enc == 1, dy, dx), t, h)
        p2 = (jnp.where(enc == 1, dx, dy), t, h)
        return 18 * enc + 2 * tap + i % 2, f1, f2, p1, p2

    def copy(i, slot, src, dst, target):
        return pltpu.make_async_remote_copy(
            src_ref=src,
            dst_ref=dst,
            send_sem=ssem.at[slot],
            recv_sem=rsem.at[i, slot],
            device_id=target,
            device_id_type=MESH,
        )

    def part(ref, i, first, count):
        return ref.at[i, :, pl.ds(pl.multiple_of(first, 16), count)]

    edge = (t == 0) | (t == last)
    near = jnp.where(t == 0, 1, 2)
    side_edge = jnp.where(t == 1, 0, last)

    def along(other):
        return (d, other, h)

    def c_second(i):
        _, _, _, _, p2 = places(i)
        return copy(i, 0, give.at[i], r1.at[i], p2)

    def c_hand(i):
        return copy(i, 1, part(zb, i, jnp.where(t == 0, 16, 0), 48), ra.at[i], along(near))

    def c_near(i):
        return copy(i, 1, part(zb, i, 16 * side_edge, 16), rn.at[i], along(side_edge))

    def c_cross(i):
        return copy(i, 2, part(zc, i, jnp.where(t == 1, 0, 16), 16), rc.at[i], along(last - t))

    def c_far(i):
        return copy(i, 3, part(zc, i, jnp.where(t == 1, 16, 0), 16), rc.at[i], along(last - side_edge))

    def shard(i, owner, count=1):
        s, f1, f2, _, _ = places(i)
        return part(out, s, 128 * f1 + 64 * f2 + 16 * owner, 16 * count)

    def c_shard(i, slot, other):
        return copy(i, slot, shard(i, t), shard(i, t), along(other))

    def c_arrive(i, slot, owner, count=1):
        return copy(i, slot, shard(i, owner, count), shard(i, owner, count), along(owner))

    def c_pass(i):
        here = shard(i, jnp.where(t == 1, 2, 0), 2)
        return copy(i, 5, here, here, along(side_edge))

    def piece(i, flip1, flip2, first, count):
        s, f1, f2, _, _ = places(i)
        g1, g2 = (1 - f1 if flip1 else f1), (1 - f2 if flip2 else f2)
        return part(out, s, 128 * g1 + 64 * g2 + first, count)

    def gather(i, slot, here, which):
        return copy(i, slot, here, here, places(i)[which])

    def c_own2(i):
        return gather(i, 7, piece(i, False, False, 0, 64), 4)

    def c_own1(i):
        return gather(i, 8, piece(i, False, False, 0, 64), 3)

    def c_on1(i):
        return gather(i, 9, piece(i, False, True, 0, 32), 3)

    def c_on2(i):
        return gather(i, 10, piece(i, True, False, 32, 32), 4)

    def c_coreback(i):
        s = places(i)[0]
        return copy(i, 11, out.at[s], out.at[s], core)

    def dec_slab(tap):
        a = tap // 3
        b = tap % 3
        total = None
        for at, ref in ((0, ge), (1, gp)):
            slab = ref[pl.ds(2 - a, 2), pl.ds(2 - b, 8)].reshape(chip, chans)
            term = jnp.dot(ht[:, at * chip : (at + 1) * chip], slab, preferred_element_type=F32)
            total = term if total is None else total + term
        for e in range(3):
            for side in range(2):
                yb[side, e] = total[128 * e : 128 * (e + 1), 128 * side : 128 * (side + 1)]

    def enc_slab(tap):
        a = tap // 3
        b = tap % 3
        total = None
        for at in range(2):
            if at == 0:
                slab = xe[pl.ds(a, 2), pl.ds(b, 8), :, half(ybit)]
            else:
                slab = xp[pl.ds(a, 2), pl.ds(b, 8)]
            term = lax.dot_general(
                slab.reshape(chip, 128),
                ds[at].reshape(chip, 3 * chans),
                (((0,), (0,)), ((), ())),
                preferred_element_type=F32,
            )
            total = term if total is None else total + term
        for e in range(3):
            for side in range(2):
                at = chans * e + 128 * side
                yb[side, e] = total[:, at : at + 128]

    def items(i):
        enc, tap = kind(i, h)

        @pl.when(i == 1)
        def _():
            @pl.when(outer)
            def _():
                gp_halo.wait_recv()
                gp_halo_core.start()
                gp_halo_core.wait_recv()

        @pl.when((i == 2) & inner)
        def _():
            h_later.wait_recv()
            h_halo_core.start()

        @pl.when(i == 2)
        def _():
            d_core.wait_recv()
            spread(de[...].reshape(chip, chans), 0)
            d_pair.wait_recv()
            d_pair_core.start()

        @pl.when(i == 4)
        def _():
            xp_own_core.wait_recv()
            when(inner, lambda: xp_halo_core.wait_recv())
            d_pair_core.wait_recv()
            spread(dp[...].reshape(chip, chans), 1)

        @pl.when(enc == 0)
        def _():
            dec_slab(tap)

        @pl.when(enc == 1)
        def _():
            enc_slab(tap)

    def finish_output():
        @pl.when(inner)
        def _():
            h_halo_core.wait_recv()

        partial_conv(ys, he, wdec, (0, 1, 2), False, True)
        total = joined(ys, False) + xe[2:4, rows].reshape(spots, chans).astype(F32)
        output[0] = total.astype(BF16).reshape(frames, tall, wide, chans)

    def s0(i):
        @pl.when(i % 2 == 0)
        def _():
            items(i // 2)

        _, _, f2, _, _ = places(i)
        side = i % 2
        keep[i] = yb[side, :, pl.ds(pl.multiple_of(64 * f2, 64), 64)]
        give[i] = yb[side, :, pl.ds(pl.multiple_of(64 * (1 - f2), 64), 64)].astype(BF16)
        c_second(i).start()

    def s1(i):
        c_second(i).wait_recv()
        total = keep[i] + r1[i].astype(F32)
        keep[i] = total
        zb[i] = total.astype(BF16)
        when(edge, lambda: c_hand(i).start())
        when(~edge, lambda: c_near(i).start())

    def s2(i):
        @pl.when(~edge)
        def _():
            copy(i, 1, ra.at[i], ra.at[i], along(side_edge)).wait_recv()
            low = jnp.where(t == 1, 16, 0)
            at = pl.ds(pl.multiple_of(low, 16), 48)
            keep[i, :, at] = keep[i, :, at] + ra[i].astype(F32)
            zc[i] = keep[i, :, pl.ds(pl.multiple_of(2 * low, 16), 32)].astype(BF16)
            c_cross(i).start()
            c_far(i).start()

    def s3(i):
        s, f1, f2, _, _ = places(i)
        mine = pl.ds(pl.multiple_of(16 * t, 16), 16)

        @pl.when(edge)
        def _():
            copy(i, 1, rn.at[i], rn.at[i], along(near)).wait_recv()
            copy(i, 3, rc.at[i], rc.at[i], along(last - near)).wait_recv()
            keep[i, :, mine] = keep[i, :, mine] + rn[i].astype(F32)

        @pl.when(~edge)
        def _():
            copy(i, 2, rc.at[i], rc.at[i], along(last - t)).wait_recv()

        total = keep[i, :, mine] + rc[i].astype(F32)
        out[s, :, pl.ds(pl.multiple_of(128 * f1 + 64 * f2 + 16 * t, 16), 16)] = total.astype(BF16)

        @pl.when(edge)
        def _():
            c_shard(i, 5, last - near).start()
            c_shard(i, 4, near).start()

        @pl.when(~edge)
        def _():
            c_shard(i, 6, last - t).start()
            c_shard(i, 4, side_edge).start()

    def s3b(i):
        @pl.when(~edge)
        def _():
            c_arrive(i, 6, last - t).wait_recv()
            c_arrive(i, 5, last - side_edge).wait_recv()
            c_pass(i).start()
            c_arrive(i, 4, side_edge).wait_recv()
            c_own1(i).start()
            c_own2(i).start()

    def s3c(i):
        @pl.when(edge)
        def _():
            c_arrive(i, 4, near).wait_recv()
            c_arrive(i, 5, jnp.where(t == 0, 2, 0), 2).wait_recv()
            c_own1(i).start()
            c_own2(i).start()

    def s4(i):
        c_own2(i).wait_recv()
        c_on1(i).start()
        c_own1(i).wait_recv()
        c_on2(i).start()

    def s5(i):
        c_on1(i).wait_recv()
        c_on2(i).wait_recv()
        c_coreback(i).start()

    def s6(i):
        c_coreback(i).wait_recv()

    stages = [s0, s1, s2, s3, s3b, s3c, s4, s5, s6]

    def body(i, carry):
        for k in ORDER:
            s = i - LAGS[k]

            @pl.when((s >= 0) & (s < STEPS))
            def _(k=k, s=s):
                stages[k](s)

        pl.when(i == STEPS + 1)(finish_output)
        return carry

    lax.fori_loop(0, STEPS + max(LAGS), body, 0)

    def sent_all(slot, ref):
        copy(0, slot, ref, ref, core).wait_send()

    halves = out.at[pl.ds(0, STEPS)]
    sent_all(0, give)
    sent_all(7, give)
    sent_all(8, give)
    sent_all(9, zc)
    sent_all(10, zc)
    sent_all(11, halves)

    @pl.when(edge)
    def _():
        sent_all(1, ra)
        sent_all(4, rn)
        sent_all(5, rn)

    @pl.when(~edge)
    def _():
        sent_all(1, rn)
        sent_all(2, rn)
        sent_all(3, rn)
        sent_all(4, rn)
        sent_all(5, zc)
        sent_all(6, rn)


    for sent in (x_core, g_core, xp_own, xp_own_core, gp_own, gp_own_core, d_core, d_pair, d_pair_core,
                 h_core, h_pair, h_pair_core):
        sent.wait_send()

    @pl.when(inner)
    def _():
        for sent in (g_earlier, x_halo_core, xp_halo, xp_halo_core, gp_halo, h_halo_core):
            sent.wait_send()

    @pl.when(outer)
    def _():
        for sent in (x_later, h_later, g_halo_core, gp_halo_core):
            sent.wait_send()


def widen_kernel(output, sums, output_out, enc_out, dec_out):
    step = pl.program_id(0)

    @pl.when(step == 0)
    def _():
        output_out[...] = output[...]

    taps = enc_out.shape[0] // 3
    for ref, first in ((dec_out, 0), (enc_out, STEPS)):
        for k in range(taps):
            for side in range(2):
                part = sums[first + 2 * (taps * step + k) + side]
                ref[3 * k : 3 * k + 3, :, 128 * side : 128 * (side + 1)] = part.astype(F32)


def whole_step(video, lengths, enc_weight, dec_weight, cotangent):
    vmem, bf = pltpu.VMEM, BF16
    frames, tall, wide, chans = video.shape[1:]
    spots = frames * tall * wide
    ext = (4, 10, wide, chans)
    enc27, dec27 = (w.reshape(27, chans, chans) for w in (enc_weight, dec_weight))
    output, sums = pl.pallas_call(
        step_kernel,
        out_shape=[
            jax.ShapeDtypeStruct(video.shape, bf),
            vmem((2 * STEPS, 3, chans, 128), bf),
        ],
        in_specs=[
            pl.BlockSpec(memory_space=pltpu.SMEM),
            pl.BlockSpec(memory_space=vmem),
            pl.BlockSpec(memory_space=vmem),
            pl.BlockSpec(memory_space=pl.ANY),
            pl.BlockSpec(memory_space=pl.ANY),
        ],
        out_specs=[pl.BlockSpec(memory_space=vmem)] * 2,
        scratch_shapes=[
            vmem((27, chans, chans), bf),
            vmem((27, chans, chans), bf),
            vmem(ext, bf),
            vmem(ext, bf),
            vmem(ext, bf),
            vmem((frames, 8, wide, chans), bf),
            vmem((4, 10, wide, 128), bf),
            vmem(ext, bf),
            vmem((frames, 8, wide, 128), bf),
            vmem((frames, 8, wide, chans), bf),
            vmem((384, 4 * spots), bf),
            vmem((2, frames, 8, wide, 3 * chans), bf),
            vmem((3, spots, chans), F32),
            vmem((3, spots, chans), F32),
            vmem((spots, chans), F32),
            vmem((2, 3, 128, 128), F32),
            vmem((STEPS, 3, 64, 128), F32),
            vmem((STEPS, 3, 64, 128), bf),
            vmem((STEPS, 3, 64, 128), bf),
            vmem((STEPS, 3, 64, 128), bf),
            vmem((STEPS, 3, 32, 128), bf),
            vmem((STEPS, 3, 48, 128), bf),
            vmem((STEPS, 3, 16, 128), bf),
            vmem((STEPS, 3, 16, 128), bf),
            pltpu.SemaphoreType.DMA((2,)),
            pltpu.SemaphoreType.DMA((22,)),
            pltpu.SemaphoreType.DMA((22,)),
            pltpu.SemaphoreType.DMA((12,)),
            pltpu.SemaphoreType.DMA((STEPS, 12)),
        ],
        compiler_params=pltpu.CompilerParams(
            collective_id=0, has_side_effects=True, vmem_limit_bytes=48 * 2**20
        ),
    )(lengths, video, cotangent, enc27, dec27)
    taps = pl.BlockSpec((WIDE, chans, chans), lambda i: (i, 0, 0))
    whole = pl.BlockSpec(video.shape, lambda i: (0,) * 5)
    output, enc_grad, dec_grad = pl.pallas_call(
        widen_kernel,
        grid=(27 // WIDE,),
        in_specs=[whole, pl.BlockSpec(memory_space=vmem)],
        out_specs=[whole, taps, taps],
        out_shape=[jax.ShapeDtypeStruct(video.shape, bf)] + [jax.ShapeDtypeStruct(enc27.shape, F32)] * 2,
        compiler_params=pltpu.CompilerParams(vmem_limit_bytes=40 * 2**20),
    )(output, sums)
    return output, enc_grad.reshape(enc_weight.shape), dec_grad.reshape(dec_weight.shape)


def shards(video, lengths, enc_weight, dec_weight, cotangent):
    sizes = tuple(lax.axis_size(axis) for axis in ("dp", "tm", "height"))
    if sizes == (4, 4, 2) and video.shape[:3] == (1, 2, 4) and video.shape[-1] == 256:
        return whole_step(video, lengths, enc_weight, dec_weight, cotangent)
    frames = video.shape[1]
    first_frame = lax.axis_index("tm") * frames
    tpos = first_frame + jnp.arange(frames, dtype=jnp.int32)
    keep = (tpos[None, :] < lengths[:, None])[:, :, None, None, None]
    masked = jnp.where(keep, video, jnp.zeros_like(video))
    cot_masked = jnp.where(keep, cotangent, jnp.zeros_like(cotangent))
    ext_x = with_earlier(masked)
    pre = apply_taps(ext_x, enc_weight)
    hidden = jax.nn.silu(pre).astype(jnp.bfloat16)
    ext_h = with_earlier(hidden)
    output = (apply_taps(ext_h, dec_weight) + masked.astype(jnp.float32)).astype(jnp.bfloat16)
    ext_g = with_later(cot_masked)
    chans = dec_weight.shape[3]
    flipped = jnp.transpose(dec_weight[::-1, ::-1, ::-1], (0, 1, 3, 2, 4)).reshape(3, 3, chans, -1)
    dec_local = tap_grads(ext_h, cot_masked)
    back = apply_taps(ext_g, flipped, True)
    dpre = (back * dsilu(pre)).astype(jnp.bfloat16)
    enc_local = tap_grads(ext_x, dpre)
    enc_grad, dec_grad = sum_all(enc_local), sum_all(dec_local)
    return (output, enc_grad, dec_grad)


def solution(mesh):
    in_specs = (
        P("dp", "tm", "height", None, None),
        P("dp"),
        P(),
        P(),
        P("dp", "tm", "height", None, None),
    )
    out_specs = (P("dp", "tm", "height", None, None), P(), P())
    return jax.shard_map(shards, mesh=mesh, in_specs=in_specs, out_specs=out_specs, check_vma=False)
```

```python
import jax
import jax.numpy as jnp
from jax import lax
from jax.experimental import pallas as pl
from jax.experimental.pallas import tpu as pltpu
from jax.sharding import PartitionSpec as P

MESH = pl.DeviceIdType.MESH
WIDE = 9
ORDER = (8, 7, 6, 5, 4, 3, 2, 1, 0)
LAGS = (0, 5, 8, 12, 15, 18, 22, 26, 29)


def extended(shard, sides, width):
    for axis, dim in sides:
        devices, length = (lax.axis_size(axis), shard.shape[dim])
        up = [(i, (i + 1) % devices) for i in range(devices - 1)]
        down = [(j, i) for i, j in up]
        last = lax.slice_in_dim(shard, length - width, length, axis=dim)
        leading = lax.slice_in_dim(shard, 0, width, axis=dim)
        before = lax.ppermute(last, axis, up)
        after = lax.ppermute(leading, axis, down)
        shard = jnp.concatenate([before, shard, after], axis=dim)
    return shard


def from_behind(block, axis, distance):
    devices = range(lax.axis_size(axis))
    route = [(i - distance, i) for i in devices if i - distance in devices]
    return lax.ppermute(block, axis, route)


def apply_taps(ext, weight, transposed=False):
    count, frame_pad, row_pad, wide, chans = ext.shape
    frames = frame_pad - 2
    rows = row_pad - 2
    outs = weight.shape[2] if transposed else weight.shape[-1]
    padded = jnp.pad(ext, ((0, 0), (0, 0), (0, 0), (1, 1), (0, 0)))
    stacked = jnp.concatenate([padded[:, :, :, e : e + wide, :] for e in range(3)], axis=-1)
    total = jnp.zeros((count * frames * rows * wide, outs), jnp.float32)
    for a in range(3):
        for b in range(3):
            slab = stacked[:, a : a + frames, b : b + rows].reshape(-1, 3 * chans)
            if transposed:
                total = total + lax.dot_general(
                    slab, weight[a, b], (((1,), (1,)), ((), ())), preferred_element_type=jnp.float32
                )
                continue
            total = total + jnp.dot(
                slab, weight[a, b].reshape(3 * chans, outs), preferred_element_type=jnp.float32
            )
    return total.reshape(count, frames, rows, wide, outs)


def tap_grads(ext, cot):
    count, frame_pad, row_pad, wide, chans = ext.shape
    frames = frame_pad - 2
    rows = row_pad - 2
    outs = cot.shape[-1]
    padded = jnp.pad(ext, ((0, 0), (0, 0), (0, 0), (1, 1), (0, 0)))
    stacked = jnp.concatenate([padded[:, :, :, e : e + wide, :] for e in range(3)], axis=-1)
    flat = cot.reshape(-1, outs)
    result = []
    for a in range(3):
        for b in range(3):
            slab = stacked[:, a : a + frames, b : b + rows].reshape(-1, 3 * chans)
            result.append(
                lax.dot_general(
                    slab, flat, (((0,), (0,)), ((), ())), preferred_element_type=jnp.float32
                )
            )
    return jnp.stack(result).reshape(3, 3, 3, chans, outs)


def dsilu(value):
    sig = jax.nn.sigmoid(value)
    return sig * (1.0 + value * (1.0 - sig))


def row_edges(block):
    return extended(block, (("height", 2),), 1)


def with_earlier(block):
    before = from_behind(block, "tm", 1)
    return row_edges(jnp.concatenate([before, block], axis=1))


def with_later(block):
    after = from_behind(block, "tm", -1)
    return row_edges(jnp.concatenate([block, after], axis=1))


def index_bits(axis):
    size = lax.axis_size(axis)
    bits = []
    step = 1
    while step < size:
        bits.append((axis, step))
        step *= 2
    return bits


def swap(block, axis, step):
    return lax.ppermute(block, axis, [(i, i ^ step) for i in range(lax.axis_size(axis))])


def sum_part(part, order):
    trail = []
    for dim, (axis, step) in order:
        upper = lax.rem(lax.axis_index(axis) // step, 2) == 1
        low, high = jnp.split(part, 2, axis=dim)
        keep, give = jnp.where(upper, high, low), jnp.where(upper, low, high)
        got = swap(give.astype(jnp.bfloat16), axis, step)
        part = keep + got.astype(jnp.float32)
        trail.append((dim, axis, step, upper))
    part = part.astype(jnp.bfloat16)
    for dim, axis, step, upper in trail[::-1]:
        got = swap(part, axis, step)
        part = jnp.concatenate([jnp.where(upper, got, part), jnp.where(upper, part, got)], axis=dim)
    return part.astype(jnp.float32)


def sum_all(grad):
    height, dp, tm = index_bits("height"), index_bits("dp"), index_bits("tm")
    rest = height[1:]
    flat = grad.reshape(27, -1, grad.shape[-1])
    sums = []
    at = 0
    for count, order in ((10, dp + tm + rest), (10, dp[::-1] + tm + rest), (7, tm + dp + rest)):
        part = flat[at : at + count]
        at += count
        sums.append(sum_part(part, [(2, height[0])] + [(1, bit) for bit in order]))
    return jnp.concatenate(sums, axis=0).reshape(grad.shape)

ITEMS = 9
STEPS = 2 * ITEMS
F32 = jnp.float32
BF16 = jnp.bfloat16


def step_kernel(
    lengths, video, cot, enc_hbm, dec_hbm, output, out,
    wenc, wdec, xe, ge, he, de, xp, gp, hp, dp, ht, ds, ys, yg, slope,
    yb, keep, give, r1, zb, zc, ra, rn, rc, wsem, hs, hr, ssem, rsem,
):
    d, t, h = lax.axis_index("dp"), lax.axis_index("tm"), lax.axis_index("height")
    frames, tall, wide, chans = video.shape[1:]
    last = lax.axis_size("tm") - 1
    xbit, ybit = d % 2, d // 2
    core = (d, t, 1 - h)
    xdev = (d + 1 - 2 * xbit, t, h)
    ydev = (d + 2 - 4 * ybit, t, h)
    later = (d, lax.rem(t + 1, last + 1), h)
    earlier = (d, lax.rem(t + last, last + 1), h)
    spots = frames * tall * wide
    base = tall * h

    w_enc = pltpu.make_async_copy(enc_hbm, wenc, wsem.at[0])
    w_dec = pltpu.make_async_copy(dec_hbm, wdec, wsem.at[1])
    w_enc.start()
    w_dec.start()

    barrier = pltpu.get_barrier_semaphore()
    partners = [core, xdev, ydev] + [(d, lax.rem(t + k, last + 1), h) for k in range(1, 4)]
    for partner in partners:
        pl.semaphore_signal(barrier, inc=1, device_id=partner, device_id_type=MESH)

    rows = pl.ds(1 + base, tall)
    own_rows = pl.ds(base, tall)

    def half(first):
        return pl.ds(pl.multiple_of(128 * first, 128), 128)

    for f in range(frames):
        live = t * frames + f < lengths[0]
        xe[2 + f, rows] = jnp.where(live, video[0, f], jnp.zeros_like(video[0, f]))
        ge[f, rows] = jnp.where(live, cot[0, f], jnp.zeros_like(cot[0, f]))
    pl.semaphore_wait(barrier, len(partners))

    def message(slot, src, dst, target):
        return pltpu.make_async_remote_copy(
            src_ref=src,
            dst_ref=dst,
            send_sem=hs.at[slot],
            recv_sem=hr.at[slot],
            device_id=target,
            device_id_type=MESH,
        )

    def same(slot, ref, target):
        return message(slot, ref, ref, target)

    own, ahead = pl.ds(2, 2), pl.ds(0, 2)
    x_core = same(0, xe.at[own, rows], core)
    g_core = same(1, ge.at[ahead, rows], core)
    x_later = message(2, xe.at[own, rows], xe.at[ahead, rows], later)
    g_earlier = message(3, ge.at[ahead, rows], ge.at[own, rows], earlier)
    x_halo_core = same(4, xe.at[ahead, rows], core)
    g_halo_core = same(5, ge.at[own, rows], core)
    xp_own = message(6, xe.at[own, rows, :, half(1 - ybit)], xp.at[own, rows], ydev)
    xp_own_core = same(7, xp.at[own, rows], core)
    xp_halo = message(8, xe.at[ahead, rows, :, half(1 - ybit)], xp.at[ahead, rows], ydev)
    xp_halo_core = same(9, xp.at[ahead, rows], core)
    gp_own = message(10, ge.at[ahead, rows], gp.at[ahead, rows], xdev)
    gp_own_core = same(11, gp.at[ahead, rows], core)
    gp_halo = message(12, gp.at[ahead, rows], gp.at[own, rows], earlier)
    gp_halo_core = same(13, gp.at[own, rows], core)
    d_core = same(14, de.at[:, own_rows], core)
    d_pair = message(15, de.at[:, own_rows], dp.at[:, own_rows], ydev)
    d_pair_core = same(16, dp.at[:, own_rows], core)
    h_core = same(17, he.at[own, rows], core)
    h_later = message(18, he.at[own, rows], he.at[ahead, rows], later)
    h_halo_core = same(19, he.at[ahead, rows], core)
    h_pair = message(20, he.at[own, rows, :, half(1 - xbit)], hp.at[:, own_rows], xdev)
    h_pair_core = same(21, hp.at[:, own_rows], core)

    def when(cond, action):
        pl.when(cond)(action)

    inner, outer = t > 0, t < last
    when(outer, lambda: x_later.start())
    when(inner, lambda: g_earlier.start())
    x_core.start()
    g_core.start()
    gp_own.start()
    xp_own.start()

    for ref in (xe, ge, he, xp, gp):
        for edge in (0, 9):
            ref[:, edge] = jnp.zeros((4,) + ref.shape[2:], BF16)

    @pl.when(t == 0)
    def _():
        for ref in (xe, he, xp):
            ref[0:2] = jnp.zeros((2,) + ref.shape[1:], BF16)

    @pl.when(t == last)
    def _():
        for ref in (ge, gp):
            ref[2:4] = jnp.zeros((2,) + ref.shape[1:], BF16)

    def shifted(value, by):
        count = value.shape[0]
        column = lax.broadcasted_iota(jnp.int32, value.shape, 0) % wide
        moved = pltpu.roll(value, by % count, axis=0)
        return jnp.where(column == (0 if by == 1 else wide - 1), 0.0, moved)

    def partial_conv(acc, src, weight, taps, transposed, fresh):
        for e in range(3):
            total = None
            for a in taps:
                first = 2 - a if transposed else a
                for b in range(3):
                    down = 2 - b if transposed else b
                    slab = src[first : first + 2, pl.ds(base + down, tall)].reshape(spots, chans)
                    dims = (((1,), (1 if transposed else 0,)), ((), ()))
                    term = lax.dot_general(slab, weight[9 * a + 3 * b + e], dims, preferred_element_type=F32)
                    total = term if total is None else total + term
            if fresh:
                acc[e] = total
            else:
                acc[e] = acc[e] + total

    def joined(acc, transposed):
        one = -1 if transposed else 1
        return acc[1] + shifted(acc[0], one) + shifted(acc[2], -one)

    w_enc.wait()
    x_core.wait_recv()
    partial_conv(ys, xe, wenc, (2,), False, True)
    w_dec.wait()
    g_core.wait_recv()
    partial_conv(yg, ge, wdec, (2,), True, True)

    @pl.when(inner)
    def _():
        x_later.wait_recv()
        x_halo_core.start()
        xp_halo.start()
        x_halo_core.wait_recv()

    partial_conv(ys, xe, wenc, (1, 0), False, False)
    pre = joined(ys, False)
    sig = jax.nn.sigmoid(pre)
    hidden = (pre * sig).astype(BF16)
    slope[...] = sig * (1.0 + pre * (1.0 - sig))
    he[2:4, rows] = hidden.reshape(frames, tall, wide, chans)
    h_pair.start()
    h_core.start()
    when(outer, lambda: h_later.start())

    gp_own.wait_recv()
    gp_own_core.start()
    when(inner, lambda: gp_halo.start())
    xp_own.wait_recv()
    xp_own_core.start()

    @pl.when(outer)
    def _():
        g_earlier.wait_recv()
        g_halo_core.start()
        g_halo_core.wait_recv()

    partial_conv(yg, ge, wdec, (1, 0), True, False)
    de[:, own_rows] = (joined(yg, True) * slope[...]).astype(BF16).reshape(frames, tall, wide, chans)
    d_pair.start()
    d_core.start()

    chip = 2 * spots

    def turned(value, at):
        value = value.astype(F32)
        for e in range(3):
            moved = value if e == 1 else shifted(value, 1 if e == 0 else -1)
            ht[pl.ds(128 * e, 128), pl.ds(at * chip, chip)] = moved.T.astype(BF16)

    h_core.wait_recv()
    turned(he[2:4, 1:9, :, half(xbit)].reshape(chip, 128), 0)
    h_pair.wait_recv()
    h_pair_core.start()

    @pl.when(inner)
    def _():
        xp_halo.wait_recv()
        xp_halo_core.start()

    h_pair_core.wait_recv()
    turned(hp[...].reshape(chip, 128), 1)
    gp_own_core.wait_recv()

    def spread(value, at):
        value = value.astype(F32)
        for e in range(3):
            moved = value if e == 1 else shifted(value, -1 if e == 0 else 1)
            ds[at, :, :, :, pl.ds(chans * e, chans)] = moved.astype(BF16).reshape(frames, 8, wide, chans)

    def kind(i, hh):
        start = ITEMS // 2 + 1 - hh
        enc = jnp.where(i >= start, 1, 0)
        before = jnp.maximum(i - start, 0)
        tap = jnp.where(enc == 1, 7 + hh - 2 * before, 8 - hh - 2 * (i - before))
        return enc, tap

    def places(i):
        enc, tap = kind(i // 2, h)
        f1 = jnp.where(enc == 1, ybit, xbit)
        f2 = jnp.where(enc == 1, xbit, ybit)
        dx, dy = d + 1 - 2 * xbit, d + 2 - 4 * ybit
        p1 = (jnp.where(enc == 1, dy, dx), t, h)
        p2 = (jnp.where(enc == 1, dx, dy), t, h)
        return 18 * enc + 2 * tap + i % 2, f1, f2, p1, p2

    def copy(i, slot, src, dst, target):
        return pltpu.make_async_remote_copy(
            src_ref=src,
            dst_ref=dst,
            send_sem=ssem.at[slot],
            recv_sem=rsem.at[i, slot],
            device_id=target,
            device_id_type=MESH,
        )

    def part(ref, i, first, count):
        return ref.at[i, :, pl.ds(pl.multiple_of(first, 16), count)]

    edge = (t == 0) | (t == last)
    near = jnp.where(t == 0, 1, 2)
    side_edge = jnp.where(t == 1, 0, last)

    def along(other):
        return (d, other, h)

    def c_second(i):
        _, _, _, _, p2 = places(i)
        return copy(i, 0, give.at[i], r1.at[i], p2)

    def c_hand(i):
        return copy(i, 1, part(zb, i, jnp.where(t == 0, 16, 0), 48), ra.at[i], along(near))

    def c_near(i):
        return copy(i, 1, part(zb, i, 16 * side_edge, 16), rn.at[i], along(side_edge))

    def c_cross(i):
        return copy(i, 2, part(zc, i, jnp.where(t == 1, 0, 16), 16), rc.at[i], along(last - t))

    def c_far(i):
        return copy(i, 3, part(zc, i, jnp.where(t == 1, 16, 0), 16), rc.at[i], along(last - side_edge))

    def shard(i, owner, count=1):
        s, f1, f2, _, _ = places(i)
        return part(out, s, 128 * f1 + 64 * f2 + 16 * owner, 16 * count)

    def c_shard(i, slot, other):
        return copy(i, slot, shard(i, t), shard(i, t), along(other))

    def c_arrive(i, slot, owner, count=1):
        return copy(i, slot, shard(i, owner, count), shard(i, owner, count), along(owner))

    def c_pass(i):
        here = shard(i, jnp.where(t == 1, 2, 0), 2)
        return copy(i, 5, here, here, along(side_edge))

    def piece(i, flip1, flip2, first, count):
        s, f1, f2, _, _ = places(i)
        g1, g2 = (1 - f1 if flip1 else f1), (1 - f2 if flip2 else f2)
        return part(out, s, 128 * g1 + 64 * g2 + first, count)

    def gather(i, slot, here, which):
        return copy(i, slot, here, here, places(i)[which])

    def c_own2(i):
        return gather(i, 7, piece(i, False, False, 0, 64), 4)

    def c_own1(i):
        return gather(i, 8, piece(i, False, False, 0, 64), 3)

    def c_on1(i):
        return gather(i, 9, piece(i, False, True, 0, 32), 3)

    def c_on2(i):
        return gather(i, 10, piece(i, True, False, 32, 32), 4)

    def c_coreback(i):
        s = places(i)[0]
        return copy(i, 11, out.at[s], out.at[s], core)

    def dec_slab(tap):
        a = tap // 3
        b = tap % 3
        total = None
        for at, ref in ((0, ge), (1, gp)):
            slab = ref[pl.ds(2 - a, 2), pl.ds(2 - b, 8)].reshape(chip, chans)
            term = jnp.dot(ht[:, at * chip : (at + 1) * chip], slab, preferred_element_type=F32)
            total = term if total is None else total + term
        for e in range(3):
            for side in range(2):
                yb[side, e] = total[128 * e : 128 * (e + 1), 128 * side : 128 * (side + 1)]

    def enc_slab(tap):
        a = tap // 3
        b = tap % 3
        total = None
        for at in range(2):
            if at == 0:
                slab = xe[pl.ds(a, 2), pl.ds(b, 8), :, half(ybit)]
            else:
                slab = xp[pl.ds(a, 2), pl.ds(b, 8)]
            term = lax.dot_general(
                slab.reshape(chip, 128),
                ds[at].reshape(chip, 3 * chans),
                (((0,), (0,)), ((), ())),
                preferred_element_type=F32,
            )
            total = term if total is None else total + term
        for e in range(3):
            for side in range(2):
                at = chans * e + 128 * side
                yb[side, e] = total[:, at : at + 128]

    def items(i):
        enc, tap = kind(i, h)

        @pl.when(i == 1)
        def _():
            @pl.when(outer)
            def _():
                gp_halo.wait_recv()
                gp_halo_core.start()
                gp_halo_core.wait_recv()

        @pl.when((i == 2) & inner)
        def _():
            h_later.wait_recv()
            h_halo_core.start()

        @pl.when(i == 2)
        def _():
            d_core.wait_recv()
            spread(de[...].reshape(chip, chans), 0)
            d_pair.wait_recv()
            d_pair_core.start()

        @pl.when(i == 4)
        def _():
            xp_own_core.wait_recv()
            when(inner, lambda: xp_halo_core.wait_recv())
            d_pair_core.wait_recv()
            spread(dp[...].reshape(chip, chans), 1)

        @pl.when(enc == 0)
        def _():
            dec_slab(tap)

        @pl.when(enc == 1)
        def _():
            enc_slab(tap)

    def finish_output():
        @pl.when(inner)
        def _():
            h_halo_core.wait_recv()

        partial_conv(ys, he, wdec, (0, 1, 2), False, True)
        total = joined(ys, False) + xe[2:4, rows].reshape(spots, chans).astype(F32)
        output[0] = total.astype(BF16).reshape(frames, tall, wide, chans)

    def s0(i):
        @pl.when(i % 2 == 0)
        def _():
            items(i // 2)

        _, _, f2, _, _ = places(i)
        side = i % 2
        keep[i] = yb[side, :, pl.ds(pl.multiple_of(64 * f2, 64), 64)]
        give[i] = yb[side, :, pl.ds(pl.multiple_of(64 * (1 - f2), 64), 64)].astype(BF16)
        c_second(i).start()

    def s1(i):
        c_second(i).wait_recv()
        total = keep[i] + r1[i].astype(F32)
        keep[i] = total
        zb[i] = total.astype(BF16)
        when(edge, lambda: c_hand(i).start())
        when(~edge, lambda: c_near(i).start())

    def s2(i):
        @pl.when(~edge)
        def _():
            copy(i, 1, ra.at[i], ra.at[i], along(side_edge)).wait_recv()
            low = jnp.where(t == 1, 16, 0)
            at = pl.ds(pl.multiple_of(low, 16), 48)
            keep[i, :, at] = keep[i, :, at] + ra[i].astype(F32)
            zc[i] = keep[i, :, pl.ds(pl.multiple_of(2 * low, 16), 32)].astype(BF16)
            c_cross(i).start()
            c_far(i).start()

    def s3(i):
        s, f1, f2, _, _ = places(i)
        mine = pl.ds(pl.multiple_of(16 * t, 16), 16)

        @pl.when(edge)
        def _():
            copy(i, 1, rn.at[i], rn.at[i], along(near)).wait_recv()
            copy(i, 3, rc.at[i], rc.at[i], along(last - near)).wait_recv()
            keep[i, :, mine] = keep[i, :, mine] + rn[i].astype(F32)

        @pl.when(~edge)
        def _():
            copy(i, 2, rc.at[i], rc.at[i], along(last - t)).wait_recv()

        total = keep[i, :, mine] + rc[i].astype(F32)
        out[s, :, pl.ds(pl.multiple_of(128 * f1 + 64 * f2 + 16 * t, 16), 16)] = total.astype(BF16)

        @pl.when(edge)
        def _():
            c_shard(i, 5, last - near).start()
            c_shard(i, 4, near).start()

        @pl.when(~edge)
        def _():
            c_shard(i, 6, last - t).start()
            c_shard(i, 4, side_edge).start()

    def s3b(i):
        @pl.when(~edge)
        def _():
            c_arrive(i, 6, last - t).wait_recv()
            c_arrive(i, 5, last - side_edge).wait_recv()
            c_pass(i).start()
            c_arrive(i, 4, side_edge).wait_recv()
            c_own1(i).start()
            c_own2(i).start()

    def s3c(i):
        @pl.when(edge)
        def _():
            c_arrive(i, 4, near).wait_recv()
            c_arrive(i, 5, jnp.where(t == 0, 2, 0), 2).wait_recv()
            c_own1(i).start()
            c_own2(i).start()

    def s4(i):
        c_own2(i).wait_recv()
        c_on1(i).start()
        c_own1(i).wait_recv()
        c_on2(i).start()

    def s5(i):
        c_on1(i).wait_recv()
        c_on2(i).wait_recv()
        c_coreback(i).start()

    def s6(i):
        c_coreback(i).wait_recv()

    stages = [s0, s1, s2, s3, s3b, s3c, s4, s5, s6]

    def body(i, carry):
        for k in ORDER:
            s = i - LAGS[k]

            @pl.when((s >= 0) & (s < STEPS))
            def _(k=k, s=s):
                stages[k](s)

        pl.when(i == STEPS + 1)(finish_output)
        return carry

    lax.fori_loop(0, STEPS + max(LAGS), body, 0)

    def sent_all(slot, ref):
        copy(0, slot, ref, ref, core).wait_send()

    halves = out.at[pl.ds(0, STEPS)]
    sent_all(0, give)
    sent_all(7, give)
    sent_all(8, give)
    sent_all(9, zc)
    sent_all(10, zc)
    sent_all(11, halves)

    @pl.when(edge)
    def _():
        sent_all(1, ra)
        sent_all(4, rn)
        sent_all(5, rn)

    @pl.when(~edge)
    def _():
        sent_all(1, rn)
        sent_all(2, rn)
        sent_all(3, rn)
        sent_all(4, rn)
        sent_all(5, zc)
        sent_all(6, rn)


    for sent in (x_core, g_core, xp_own, xp_own_core, gp_own, gp_own_core, d_core, d_pair, d_pair_core,
                 h_core, h_pair, h_pair_core):
        sent.wait_send()

    @pl.when(inner)
    def _():
        for sent in (g_earlier, x_halo_core, xp_halo, xp_halo_core, gp_halo, h_halo_core):
            sent.wait_send()

    @pl.when(outer)
    def _():
        for sent in (x_later, h_later, g_halo_core, gp_halo_core):
            sent.wait_send()


def widen_kernel(output, sums, output_out, enc_out, dec_out):
    step = pl.program_id(0)

    @pl.when(step == 0)
    def _():
        output_out[...] = output[...]

    taps = enc_out.shape[0] // 3
    for ref, first in ((dec_out, 0), (enc_out, STEPS)):
        for k in range(taps):
            for side in range(2):
                part = sums[first + 2 * (taps * step + k) + side]
                ref[3 * k : 3 * k + 3, :, 128 * side : 128 * (side + 1)] = part.astype(F32)


def whole_step(video, lengths, enc_weight, dec_weight, cotangent):
    vmem, bf = pltpu.VMEM, BF16
    frames, tall, wide, chans = video.shape[1:]
    spots = frames * tall * wide
    ext = (4, 10, wide, chans)
    enc27, dec27 = (w.reshape(27, chans, chans) for w in (enc_weight, dec_weight))
    output, sums = pl.pallas_call(
        step_kernel,
        out_shape=[
            jax.ShapeDtypeStruct(video.shape, bf),
            vmem((2 * STEPS, 3, chans, 128), bf),
        ],
        in_specs=[
            pl.BlockSpec(memory_space=pltpu.SMEM),
            pl.BlockSpec(memory_space=vmem),
            pl.BlockSpec(memory_space=vmem),
            pl.BlockSpec(memory_space=pl.ANY),
            pl.BlockSpec(memory_space=pl.ANY),
        ],
        out_specs=[pl.BlockSpec(memory_space=vmem)] * 2,
        scratch_shapes=[
            vmem((27, chans, chans), bf),
            vmem((27, chans, chans), bf),
            vmem(ext, bf),
            vmem(ext, bf),
            vmem(ext, bf),
            vmem((frames, 8, wide, chans), bf),
            vmem((4, 10, wide, 128), bf),
            vmem(ext, bf),
            vmem((frames, 8, wide, 128), bf),
            vmem((frames, 8, wide, chans), bf),
            vmem((384, 4 * spots), bf),
            vmem((2, frames, 8, wide, 3 * chans), bf),
            vmem((3, spots, chans), F32),
            vmem((3, spots, chans), F32),
            vmem((spots, chans), F32),
            vmem((2, 3, 128, 128), F32),
            vmem((STEPS, 3, 64, 128), F32),
            vmem((STEPS, 3, 64, 128), bf),
            vmem((STEPS, 3, 64, 128), bf),
            vmem((STEPS, 3, 64, 128), bf),
            vmem((STEPS, 3, 32, 128), bf),
            vmem((STEPS, 3, 48, 128), bf),
            vmem((STEPS, 3, 16, 128), bf),
            vmem((STEPS, 3, 16, 128), bf),
            pltpu.SemaphoreType.DMA((2,)),
            pltpu.SemaphoreType.DMA((22,)),
            pltpu.SemaphoreType.DMA((22,)),
            pltpu.SemaphoreType.DMA((12,)),
            pltpu.SemaphoreType.DMA((STEPS, 12)),
        ],
        compiler_params=pltpu.CompilerParams(
            collective_id=0, has_side_effects=True, vmem_limit_bytes=48 * 2**20
        ),
    )(lengths, video, cotangent, enc27, dec27)
    taps = pl.BlockSpec((WIDE, chans, chans), lambda i: (i, 0, 0))
    whole = pl.BlockSpec(video.shape, lambda i: (0,) * 5)
    output, enc_grad, dec_grad = pl.pallas_call(
        widen_kernel,
        grid=(27 // WIDE,),
        in_specs=[whole, pl.BlockSpec(memory_space=vmem)],
        out_specs=[whole, taps, taps],
        out_shape=[jax.ShapeDtypeStruct(video.shape, bf)] + [jax.ShapeDtypeStruct(enc27.shape, F32)] * 2,
        compiler_params=pltpu.CompilerParams(vmem_limit_bytes=40 * 2**20),
    )(output, sums)
    return output, enc_grad.reshape(enc_weight.shape), dec_grad.reshape(dec_weight.shape)


def shards(video, lengths, enc_weight, dec_weight, cotangent):
    sizes = tuple(lax.axis_size(axis) for axis in ("dp", "tm", "height"))
    if sizes == (4, 4, 2) and video.shape[:3] == (1, 2, 4) and video.shape[-1] == 256:
        return whole_step(video, lengths, enc_weight, dec_weight, cotangent)
    frames = video.shape[1]
    first_frame = lax.axis_index("tm") * frames
    tpos = first_frame + jnp.arange(frames, dtype=jnp.int32)
    keep = (tpos[None, :] < lengths[:, None])[:, :, None, None, None]
    masked = jnp.where(keep, video, jnp.zeros_like(video))
    cot_masked = jnp.where(keep, cotangent, jnp.zeros_like(cotangent))
    ext_x = with_earlier(masked)
    pre = apply_taps(ext_x, enc_weight)
    hidden = jax.nn.silu(pre).astype(jnp.bfloat16)
    ext_h = with_earlier(hidden)
    output = (apply_taps(ext_h, dec_weight) + masked.astype(jnp.float32)).astype(jnp.bfloat16)
    ext_g = with_later(cot_masked)
    chans = dec_weight.shape[3]
    flipped = jnp.transpose(dec_weight[::-1, ::-1, ::-1], (0, 1, 3, 2, 4)).reshape(3, 3, chans, -1)
    dec_local = tap_grads(ext_h, cot_masked)
    back = apply_taps(ext_g, flipped, True)
    dpre = (back * dsilu(pre)).astype(jnp.bfloat16)
    enc_local = tap_grads(ext_x, dpre)
    enc_grad, dec_grad = sum_all(enc_local), sum_all(dec_local)
    return (output, enc_grad, dec_grad)


def solution(mesh):
    in_specs = (
        P("dp", "tm", "height", None, None),
        P("dp"),
        P(),
        P(),
        P("dp", "tm", "height", None, None),
    )
    out_specs = (P("dp", "tm", "height", None, None), P(), P())
    return jax.shard_map(shards, mesh=mesh, in_specs=in_specs, out_specs=out_specs, check_vma=False)
```

```python
import jax
import jax.numpy as jnp
from jax import lax
from jax.experimental import pallas as pl
from jax.experimental.pallas import tpu as pltpu
from jax.sharding import PartitionSpec as P

MESH = pl.DeviceIdType.MESH
WIDE = 9
ORDER = (8, 7, 6, 5, 4, 3, 2, 1, 0)
LAGS = (0, 5, 8, 12, 15, 18, 22, 26, 29)


def extended(shard, sides, width):
    for axis, dim in sides:
        devices, length = (lax.axis_size(axis), shard.shape[dim])
        up = [(i, (i + 1) % devices) for i in range(devices - 1)]
        down = [(j, i) for i, j in up]
        last = lax.slice_in_dim(shard, length - width, length, axis=dim)
        leading = lax.slice_in_dim(shard, 0, width, axis=dim)
        before = lax.ppermute(last, axis, up)
        after = lax.ppermute(leading, axis, down)
        shard = jnp.concatenate([before, shard, after], axis=dim)
    return shard


def from_behind(block, axis, distance):
    devices = range(lax.axis_size(axis))
    route = [(i - distance, i) for i in devices if i - distance in devices]
    return lax.ppermute(block, axis, route)


def apply_taps(ext, weight, transposed=False):
    count, frame_pad, row_pad, wide, chans = ext.shape
    frames = frame_pad - 2
    rows = row_pad - 2
    outs = weight.shape[2] if transposed else weight.shape[-1]
    padded = jnp.pad(ext, ((0, 0), (0, 0), (0, 0), (1, 1), (0, 0)))
    stacked = jnp.concatenate([padded[:, :, :, e : e + wide, :] for e in range(3)], axis=-1)
    total = jnp.zeros((count * frames * rows * wide, outs), jnp.float32)
    for a in range(3):
        for b in range(3):
            slab = stacked[:, a : a + frames, b : b + rows].reshape(-1, 3 * chans)
            if transposed:
                total = total + lax.dot_general(
                    slab, weight[a, b], (((1,), (1,)), ((), ())), preferred_element_type=jnp.float32
                )
                continue
            total = total + jnp.dot(
                slab, weight[a, b].reshape(3 * chans, outs), preferred_element_type=jnp.float32
            )
    return total.reshape(count, frames, rows, wide, outs)


def tap_grads(ext, cot):
    count, frame_pad, row_pad, wide, chans = ext.shape
    frames = frame_pad - 2
    rows = row_pad - 2
    outs = cot.shape[-1]
    padded = jnp.pad(ext, ((0, 0), (0, 0), (0, 0), (1, 1), (0, 0)))
    stacked = jnp.concatenate([padded[:, :, :, e : e + wide, :] for e in range(3)], axis=-1)
    flat = cot.reshape(-1, outs)
    result = []
    for a in range(3):
        for b in range(3):
            slab = stacked[:, a : a + frames, b : b + rows].reshape(-1, 3 * chans)
            result.append(
                lax.dot_general(
                    slab, flat, (((0,), (0,)), ((), ())), preferred_element_type=jnp.float32
                )
            )
    return jnp.stack(result).reshape(3, 3, 3, chans, outs)


def dsilu(value):
    sig = jax.nn.sigmoid(value)
    return sig * (1.0 + value * (1.0 - sig))


def row_edges(block):
    return extended(block, (("height", 2),), 1)


def with_earlier(block):
    before = from_behind(block, "tm", 1)
    return row_edges(jnp.concatenate([before, block], axis=1))


def with_later(block):
    after = from_behind(block, "tm", -1)
    return row_edges(jnp.concatenate([block, after], axis=1))


def index_bits(axis):
    size = lax.axis_size(axis)
    bits = []
    step = 1
    while step < size:
        bits.append((axis, step))
        step *= 2
    return bits


def swap(block, axis, step):
    return lax.ppermute(block, axis, [(i, i ^ step) for i in range(lax.axis_size(axis))])


def sum_part(part, order):
    trail = []
    for dim, (axis, step) in order:
        upper = lax.rem(lax.axis_index(axis) // step, 2) == 1
        low, high = jnp.split(part, 2, axis=dim)
        keep, give = jnp.where(upper, high, low), jnp.where(upper, low, high)
        got = swap(give.astype(jnp.bfloat16), axis, step)
        part = keep + got.astype(jnp.float32)
        trail.append((dim, axis, step, upper))
    part = part.astype(jnp.bfloat16)
    for dim, axis, step, upper in trail[::-1]:
        got = swap(part, axis, step)
        part = jnp.concatenate([jnp.where(upper, got, part), jnp.where(upper, part, got)], axis=dim)
    return part.astype(jnp.float32)


def sum_all(grad):
    height, dp, tm = index_bits("height"), index_bits("dp"), index_bits("tm")
    rest = height[1:]
    flat = grad.reshape(27, -1, grad.shape[-1])
    sums = []
    at = 0
    for count, order in ((10, dp + tm + rest), (10, dp[::-1] + tm + rest), (7, tm + dp + rest)):
        part = flat[at : at + count]
        at += count
        sums.append(sum_part(part, [(2, height[0])] + [(1, bit) for bit in order]))
    return jnp.concatenate(sums, axis=0).reshape(grad.shape)

ITEMS = 9
STEPS = 2 * ITEMS
F32 = jnp.float32
BF16 = jnp.bfloat16


def step_kernel(
    lengths, video, cot, enc_hbm, dec_hbm, output, out,
    wenc, wdec, xe, ge, he, de, xp, gp, hp, dp, ht, ds, ys, yg, slope,
    yb, keep, give, r1, zb, zc, ra, rn, rc, wsem, hs, hr, ssem, rsem,
):
    d, t, h = lax.axis_index("dp"), lax.axis_index("tm"), lax.axis_index("height")
    frames, tall, wide, chans = video.shape[1:]
    last = lax.axis_size("tm") - 1
    xbit, ybit = d % 2, d // 2
    core = (d, t, 1 - h)
    xdev = (d + 1 - 2 * xbit, t, h)
    ydev = (d + 2 - 4 * ybit, t, h)
    later = (d, lax.rem(t + 1, last + 1), h)
    earlier = (d, lax.rem(t + last, last + 1), h)
    spots = frames * tall * wide
    base = tall * h

    w_enc = pltpu.make_async_copy(enc_hbm, wenc, wsem.at[0])
    w_dec = pltpu.make_async_copy(dec_hbm, wdec, wsem.at[1])
    w_enc.start()
    w_dec.start()

    barrier = pltpu.get_barrier_semaphore()

    def greet(partner):
        pl.semaphore_signal(barrier, inc=1, device_id=partner, device_id_type=MESH)

    for k in (-2, -1, 1, 2):
        pl.when((t + k >= 0) & (t + k <= last))(lambda k=k: greet((d, t + k, h)))
    for partner in (core, xdev, ydev):
        greet(partner)

    rows = pl.ds(1 + base, tall)
    own_rows = pl.ds(base, tall)

    def half(first):
        return pl.ds(pl.multiple_of(128 * first, 128), 128)

    for f in range(frames):
        live = t * frames + f < lengths[0]
        xe[2 + f, rows] = jnp.where(live, video[0, f], jnp.zeros_like(video[0, f]))
        ge[f, rows] = jnp.where(live, cot[0, f], jnp.zeros_like(cot[0, f]))
    pl.semaphore_wait(barrier, jnp.where((t == 0) | (t == last), 5, 6))

    def message(slot, src, dst, target):
        return pltpu.make_async_remote_copy(
            src_ref=src,
            dst_ref=dst,
            send_sem=hs.at[slot],
            recv_sem=hr.at[slot],
            device_id=target,
            device_id_type=MESH,
        )

    def same(slot, ref, target):
        return message(slot, ref, ref, target)

    own, ahead = pl.ds(2, 2), pl.ds(0, 2)
    x_core = same(0, xe.at[own, rows], core)
    g_core = same(1, ge.at[ahead, rows], core)
    x_later = message(2, xe.at[own, rows], xe.at[ahead, rows], later)
    g_earlier = message(3, ge.at[ahead, rows], ge.at[own, rows], earlier)
    x_halo_core = same(4, xe.at[ahead, rows], core)
    g_halo_core = same(5, ge.at[own, rows], core)
    xp_own = message(6, xe.at[own, rows, :, half(1 - ybit)], xp.at[own, rows], ydev)
    xp_own_core = same(7, xp.at[own, rows], core)
    xp_halo = message(8, xe.at[ahead, rows, :, half(1 - ybit)], xp.at[ahead, rows], ydev)
    xp_halo_core = same(9, xp.at[ahead, rows], core)
    gp_own = message(10, ge.at[ahead, rows], gp.at[ahead, rows], xdev)
    gp_own_core = same(11, gp.at[ahead, rows], core)
    gp_halo = message(12, gp.at[ahead, rows], gp.at[own, rows], earlier)
    gp_halo_core = same(13, gp.at[own, rows], core)
    d_core = same(14, de.at[:, own_rows], core)
    d_pair = message(15, de.at[:, own_rows], dp.at[:, own_rows], ydev)
    d_pair_core = same(16, dp.at[:, own_rows], core)
    h_core = same(17, he.at[own, rows], core)
    h_later = message(18, he.at[own, rows], he.at[ahead, rows], later)
    h_halo_core = same(19, he.at[ahead, rows], core)
    h_pair = message(20, he.at[own, rows, :, half(1 - xbit)], hp.at[:, own_rows], xdev)
    h_pair_core = same(21, hp.at[:, own_rows], core)

    def when(cond, action):
        pl.when(cond)(action)

    inner, outer = t > 0, t < last
    when(outer, lambda: x_later.start())
    when(inner, lambda: g_earlier.start())
    x_core.start()
    g_core.start()
    gp_own.start()
    xp_own.start()

    for ref in (xe, ge, he, xp, gp):
        for edge in (0, 9):
            ref[:, edge] = jnp.zeros((4,) + ref.shape[2:], BF16)

    @pl.when(t == 0)
    def _():
        for ref in (xe, he, xp):
            ref[0:2] = jnp.zeros((2,) + ref.shape[1:], BF16)

    @pl.when(t == last)
    def _():
        for ref in (ge, gp):
            ref[2:4] = jnp.zeros((2,) + ref.shape[1:], BF16)

    def shifted(value, by):
        count = value.shape[0]
        column = lax.broadcasted_iota(jnp.int32, value.shape, 0) % wide
        moved = pltpu.roll(value, by % count, axis=0)
        return jnp.where(column == (0 if by == 1 else wide - 1), 0.0, moved)

    def partial_conv(acc, src, weight, taps, transposed, fresh):
        for e in range(3):
            total = None
            for a in taps:
                first = 2 - a if transposed else a
                for b in range(3):
                    down = 2 - b if transposed else b
                    slab = src[first : first + 2, pl.ds(base + down, tall)].reshape(spots, chans)
                    dims = (((1,), (1 if transposed else 0,)), ((), ()))
                    term = lax.dot_general(slab, weight[9 * a + 3 * b + e], dims, preferred_element_type=F32)
                    total = term if total is None else total + term
            if fresh:
                acc[e] = total
            else:
                acc[e] = acc[e] + total

    def joined(acc, transposed):
        one = -1 if transposed else 1
        return acc[1] + shifted(acc[0], one) + shifted(acc[2], -one)

    w_enc.wait()
    x_core.wait_recv()
    partial_conv(ys, xe, wenc, (2,), False, True)
    w_dec.wait()
    g_core.wait_recv()
    partial_conv(yg, ge, wdec, (2,), True, True)

    @pl.when(inner)
    def _():
        x_later.wait_recv()
        x_halo_core.start()
        xp_halo.start()
        x_halo_core.wait_recv()

    partial_conv(ys, xe, wenc, (1, 0), False, False)
    pre = joined(ys, False)
    sig = jax.nn.sigmoid(pre)
    hidden = (pre * sig).astype(BF16)
    slope[...] = sig * (1.0 + pre * (1.0 - sig))
    he[2:4, rows] = hidden.reshape(frames, tall, wide, chans)
    h_pair.start()
    h_core.start()
    when(outer, lambda: h_later.start())

    gp_own.wait_recv()
    gp_own_core.start()
    when(inner, lambda: gp_halo.start())
    xp_own.wait_recv()
    xp_own_core.start()

    @pl.when(outer)
    def _():
        g_earlier.wait_recv()
        g_halo_core.start()
        g_halo_core.wait_recv()

    partial_conv(yg, ge, wdec, (1, 0), True, False)
    de[:, own_rows] = (joined(yg, True) * slope[...]).astype(BF16).reshape(frames, tall, wide, chans)
    d_pair.start()
    d_core.start()

    chip = 2 * spots

    def turned(value, at):
        value = value.astype(F32)
        for e in range(3):
            moved = value if e == 1 else shifted(value, 1 if e == 0 else -1)
            ht[pl.ds(128 * e, 128), pl.ds(at * chip, chip)] = moved.T.astype(BF16)

    h_core.wait_recv()
    turned(he[2:4, 1:9, :, half(xbit)].reshape(chip, 128), 0)
    h_pair.wait_recv()
    h_pair_core.start()

    @pl.when(inner)
    def _():
        xp_halo.wait_recv()
        xp_halo_core.start()

    h_pair_core.wait_recv()
    turned(hp[...].reshape(chip, 128), 1)
    gp_own_core.wait_recv()

    def spread(value, at):
        value = value.astype(F32)
        for e in range(3):
            moved = value if e == 1 else shifted(value, -1 if e == 0 else 1)
            ds[at, :, :, :, pl.ds(chans * e, chans)] = moved.astype(BF16).reshape(frames, 8, wide, chans)

    def kind(i, hh):
        start = ITEMS // 2 + 1 - hh
        enc = jnp.where(i >= start, 1, 0)
        before = jnp.maximum(i - start, 0)
        tap = jnp.where(enc == 1, 7 + hh - 2 * before, 8 - hh - 2 * (i - before))
        return enc, tap

    def places(i):
        enc, tap = kind(i // 2, h)
        f1 = jnp.where(enc == 1, ybit, xbit)
        f2 = jnp.where(enc == 1, xbit, ybit)
        dx, dy = d + 1 - 2 * xbit, d + 2 - 4 * ybit
        p1 = (jnp.where(enc == 1, dy, dx), t, h)
        p2 = (jnp.where(enc == 1, dx, dy), t, h)
        return 18 * enc + 2 * tap + i % 2, f1, f2, p1, p2

    def copy(i, slot, src, dst, target):
        return pltpu.make_async_remote_copy(
            src_ref=src,
            dst_ref=dst,
            send_sem=ssem.at[slot],
            recv_sem=rsem.at[i, slot - (slot > 2)],
            device_id=target,
            device_id_type=MESH,
        )

    def part(ref, i, first, count):
        return ref.at[i, :, pl.ds(pl.multiple_of(first, 16), count)]

    edge = (t == 0) | (t == last)
    near = jnp.where(t == 0, 1, 2)
    side_edge = jnp.where(t == 1, 0, last)

    def along(other):
        return (d, other, h)

    def c_second(i):
        _, _, _, _, p2 = places(i)
        return copy(i, 0, give.at[i], r1.at[i], p2)

    def c_hand(i):
        return copy(i, 1, part(zb, i, jnp.where(t == 0, 16, 0), 48), ra.at[i], along(near))

    def c_near(i):
        return copy(i, 1, part(zb, i, 16 * side_edge, 16), rn.at[i], along(side_edge))

    def c_cross(i):
        return copy(i, 2, part(zc, i, jnp.where(t == 1, 0, 16), 16), rc.at[i], along(last - t))

    def c_far(i):
        return copy(i, 3, part(zc, i, jnp.where(t == 1, 16, 0), 16), rc.at[i], along(last - side_edge))

    def shard(i, owner, count=1):
        s, f1, f2, _, _ = places(i)
        return part(out, s, 128 * f1 + 64 * f2 + 16 * owner, 16 * count)

    def c_shard(i, slot, other):
        return copy(i, slot, shard(i, t), shard(i, t), along(other))

    def c_arrive(i, slot, owner, count=1):
        return copy(i, slot, shard(i, owner, count), shard(i, owner, count), along(owner))

    def c_pass(i):
        here = shard(i, jnp.where(t == 1, 2, 0), 2)
        return copy(i, 5, here, here, along(side_edge))

    def piece(i, flip1, flip2, first, count):
        s, f1, f2, _, _ = places(i)
        g1, g2 = (1 - f1 if flip1 else f1), (1 - f2 if flip2 else f2)
        return part(out, s, 128 * g1 + 64 * g2 + first, count)

    def gather(i, slot, here, which):
        return copy(i, slot, here, here, places(i)[which])

    def c_own2(i):
        return gather(i, 7, piece(i, False, False, 0, 64), 4)

    def c_own1(i):
        return gather(i, 8, piece(i, False, False, 0, 64), 3)

    def c_on1(i):
        return gather(i, 9, piece(i, False, True, 0, 32), 3)

    def c_on2(i):
        return gather(i, 10, piece(i, True, False, 32, 32), 4)

    def c_coreback(i):
        s = places(i)[0]
        return copy(i, 11, out.at[s], out.at[s], core)

    def dec_slab(tap):
        a = tap // 3
        b = tap % 3
        total = None
        for at, ref in ((0, ge), (1, gp)):
            slab = ref[pl.ds(2 - a, 2), pl.ds(2 - b, 8)].reshape(chip, chans)
            term = jnp.dot(ht[:, at * chip : (at + 1) * chip], slab, preferred_element_type=F32)
            total = term if total is None else total + term
        for e in range(3):
            for side in range(2):
                yb[side, e] = total[128 * e : 128 * (e + 1), 128 * side : 128 * (side + 1)]

    def enc_slab(tap):
        a = tap // 3
        b = tap % 3
        total = None
        for at in range(2):
            if at == 0:
                slab = xe[pl.ds(a, 2), pl.ds(b, 8), :, half(ybit)]
            else:
                slab = xp[pl.ds(a, 2), pl.ds(b, 8)]
            term = lax.dot_general(
                slab.reshape(chip, 128),
                ds[at].reshape(chip, 3 * chans),
                (((0,), (0,)), ((), ())),
                preferred_element_type=F32,
            )
            total = term if total is None else total + term
        for e in range(3):
            for side in range(2):
                at = chans * e + 128 * side
                yb[side, e] = total[:, at : at + 128]

    def items(i):
        enc, tap = kind(i, h)

        @pl.when(i == 1)
        def _():
            @pl.when(outer)
            def _():
                gp_halo.wait_recv()
                gp_halo_core.start()
                gp_halo_core.wait_recv()

        @pl.when((i == 2) & inner)
        def _():
            h_later.wait_recv()
            h_halo_core.start()

        @pl.when(i == 2)
        def _():
            d_core.wait_recv()
            spread(de[...].reshape(chip, chans), 0)
            d_pair.wait_recv()
            d_pair_core.start()

        @pl.when(i == 4)
        def _():
            xp_own_core.wait_recv()
            when(inner, lambda: xp_halo_core.wait_recv())
            d_pair_core.wait_recv()
            spread(dp[...].reshape(chip, chans), 1)

        @pl.when(enc == 0)
        def _():
            dec_slab(tap)

        @pl.when(enc == 1)
        def _():
            enc_slab(tap)

    def finish_output():
        @pl.when(inner)
        def _():
            h_halo_core.wait_recv()

        partial_conv(ys, he, wdec, (0, 1, 2), False, True)
        total = joined(ys, False) + xe[2:4, rows].reshape(spots, chans).astype(F32)
        output[0] = total.astype(BF16).reshape(frames, tall, wide, chans)

    def s0(i):
        @pl.when(i % 2 == 0)
        def _():
            items(i // 2)

        _, _, f2, _, _ = places(i)
        side = i % 2
        keep[i] = yb[side, :, pl.ds(pl.multiple_of(64 * f2, 64), 64)]
        give[i] = yb[side, :, pl.ds(pl.multiple_of(64 * (1 - f2), 64), 64)].astype(BF16)
        c_second(i).start()

    def s1(i):
        c_second(i).wait_recv()
        total = keep[i] + r1[i].astype(F32)
        keep[i] = total
        zb[i] = total.astype(BF16)
        when(edge, lambda: c_hand(i).start())
        when(~edge, lambda: c_near(i).start())

    def s2(i):
        @pl.when(~edge)
        def _():
            copy(i, 1, ra.at[i], ra.at[i], along(side_edge)).wait_recv()
            low = jnp.where(t == 1, 16, 0)
            at = pl.ds(pl.multiple_of(low, 16), 48)
            keep[i, :, at] = keep[i, :, at] + ra[i].astype(F32)
            zc[i] = keep[i, :, pl.ds(pl.multiple_of(2 * low, 16), 32)].astype(BF16)
            c_cross(i).start()
            c_far(i).start()

    def s3(i):
        s, f1, f2, _, _ = places(i)
        mine = pl.ds(pl.multiple_of(16 * t, 16), 16)

        @pl.when(edge)
        def _():
            copy(i, 1, rn.at[i], rn.at[i], along(near)).wait_recv()
            copy(i, 3, rc.at[i], rc.at[i], along(last - near)).wait_recv()
            keep[i, :, mine] = keep[i, :, mine] + rn[i].astype(F32)

        @pl.when(~edge)
        def _():
            copy(i, 2, rc.at[i], rc.at[i], along(last - t)).wait_recv()

        total = keep[i, :, mine] + rc[i].astype(F32)
        out[s, :, pl.ds(pl.multiple_of(128 * f1 + 64 * f2 + 16 * t, 16), 16)] = total.astype(BF16)

        @pl.when(edge)
        def _():
            c_shard(i, 5, last - near).start()
            c_shard(i, 4, near).start()

        @pl.when(~edge)
        def _():
            c_shard(i, 6, last - t).start()
            c_shard(i, 4, side_edge).start()

    def s3b(i):
        @pl.when(~edge)
        def _():
            c_arrive(i, 6, last - t).wait_recv()
            c_arrive(i, 5, last - side_edge).wait_recv()
            c_pass(i).start()
            c_arrive(i, 4, side_edge).wait_recv()
            c_own1(i).start()
            c_own2(i).start()

    def s3c(i):
        @pl.when(edge)
        def _():
            c_arrive(i, 4, near).wait_recv()
            c_arrive(i, 5, jnp.where(t == 0, 2, 0), 2).wait_recv()
            c_own1(i).start()
            c_own2(i).start()

    def s4(i):
        c_own2(i).wait_recv()
        c_on1(i).start()
        c_own1(i).wait_recv()
        c_on2(i).start()

    def s5(i):
        c_on1(i).wait_recv()
        c_on2(i).wait_recv()
        c_coreback(i).start()

    def s6(i):
        c_coreback(i).wait_recv()

    stages = [s0, s1, s2, s3, s3b, s3c, s4, s5, s6]

    def body(i, carry):
        for k in ORDER:
            s = i - LAGS[k]

            @pl.when((s >= 0) & (s < STEPS))
            def _(k=k, s=s):
                stages[k](s)

        pl.when(i == STEPS + 1)(finish_output)
        return carry

    lax.fori_loop(0, STEPS + max(LAGS), body, 0)

    def sent_all(slot, ref):
        copy(0, slot, ref, ref, core).wait_send()

    halves = out.at[pl.ds(0, STEPS)]
    sent_all(0, give)
    sent_all(7, give)
    sent_all(8, give)
    sent_all(9, zc)
    sent_all(10, zc)
    sent_all(11, halves)

    @pl.when(edge)
    def _():
        sent_all(1, ra)
        sent_all(4, rn)
        sent_all(5, rn)

    @pl.when(~edge)
    def _():
        sent_all(1, rn)
        sent_all(2, rn)
        sent_all(3, rn)
        sent_all(4, rn)
        sent_all(5, zc)
        sent_all(6, rn)


    for sent in (x_core, g_core, xp_own, xp_own_core, gp_own, gp_own_core, d_core, d_pair, d_pair_core,
                 h_core, h_pair, h_pair_core):
        sent.wait_send()

    @pl.when(inner)
    def _():
        for sent in (g_earlier, x_halo_core, xp_halo, xp_halo_core, gp_halo, h_halo_core):
            sent.wait_send()

    @pl.when(outer)
    def _():
        for sent in (x_later, h_later, g_halo_core, gp_halo_core):
            sent.wait_send()


def widen_kernel(output, sums, output_out, enc_out, dec_out):
    step = pl.program_id(0)

    @pl.when(step == 0)
    def _():
        output_out[...] = output[...]

    taps = enc_out.shape[0] // 3
    for ref, first in ((dec_out, 0), (enc_out, STEPS)):
        for k in range(taps):
            for side in range(2):
                part = sums[first + 2 * (taps * step + k) + side]
                ref[3 * k : 3 * k + 3, :, 128 * side : 128 * (side + 1)] = part.astype(F32)


def whole_step(video, lengths, enc_weight, dec_weight, cotangent):
    vmem, bf = pltpu.VMEM, BF16
    frames, tall, wide, chans = video.shape[1:]
    spots = frames * tall * wide
    ext = (4, 10, wide, chans)
    enc27, dec27 = (w.reshape(27, chans, chans) for w in (enc_weight, dec_weight))
    output, sums = pl.pallas_call(
        step_kernel,
        out_shape=[
            jax.ShapeDtypeStruct(video.shape, bf),
            vmem((2 * STEPS, 3, chans, 128), bf),
        ],
        in_specs=[
            pl.BlockSpec(memory_space=pltpu.SMEM),
            pl.BlockSpec(memory_space=vmem),
            pl.BlockSpec(memory_space=vmem),
            pl.BlockSpec(memory_space=pl.ANY),
            pl.BlockSpec(memory_space=pl.ANY),
        ],
        out_specs=[pl.BlockSpec(memory_space=vmem)] * 2,
        scratch_shapes=[
            vmem((27, chans, chans), bf),
            vmem((27, chans, chans), bf),
            vmem(ext, bf),
            vmem(ext, bf),
            vmem(ext, bf),
            vmem((frames, 8, wide, chans), bf),
            vmem((4, 10, wide, 128), bf),
            vmem(ext, bf),
            vmem((frames, 8, wide, 128), bf),
            vmem((frames, 8, wide, chans), bf),
            vmem((384, 4 * spots), bf),
            vmem((2, frames, 8, wide, 3 * chans), bf),
            vmem((3, spots, chans), F32),
            vmem((3, spots, chans), F32),
            vmem((spots, chans), F32),
            vmem((2, 3, 128, 128), F32),
            vmem((STEPS, 3, 64, 128), F32),
            vmem((STEPS, 3, 64, 128), bf),
            vmem((STEPS, 3, 64, 128), bf),
            vmem((STEPS, 3, 64, 128), bf),
            vmem((STEPS, 3, 32, 128), bf),
            vmem((STEPS, 3, 48, 128), bf),
            vmem((STEPS, 3, 16, 128), bf),
            vmem((STEPS, 3, 16, 128), bf),
            pltpu.SemaphoreType.DMA((2,)),
            pltpu.SemaphoreType.DMA((22,)),
            pltpu.SemaphoreType.DMA((22,)),
            pltpu.SemaphoreType.DMA((12,)),
            pltpu.SemaphoreType.DMA((STEPS, 11)),
        ],
        compiler_params=pltpu.CompilerParams(
            collective_id=0, has_side_effects=True, vmem_limit_bytes=48 * 2**20
        ),
    )(lengths, video, cotangent, enc27, dec27)
    taps = pl.BlockSpec((WIDE, chans, chans), lambda i: (i, 0, 0))
    whole = pl.BlockSpec(video.shape, lambda i: (0,) * 5)
    output, enc_grad, dec_grad = pl.pallas_call(
        widen_kernel,
        grid=(27 // WIDE,),
        in_specs=[whole, pl.BlockSpec(memory_space=vmem)],
        out_specs=[whole, taps, taps],
        out_shape=[jax.ShapeDtypeStruct(video.shape, bf)] + [jax.ShapeDtypeStruct(enc27.shape, F32)] * 2,
        compiler_params=pltpu.CompilerParams(vmem_limit_bytes=40 * 2**20),
    )(output, sums)
    return output, enc_grad.reshape(enc_weight.shape), dec_grad.reshape(dec_weight.shape)


def shards(video, lengths, enc_weight, dec_weight, cotangent):
    sizes = tuple(lax.axis_size(axis) for axis in ("dp", "tm", "height"))
    if sizes == (4, 4, 2) and video.shape[:3] == (1, 2, 4) and video.shape[-1] == 256:
        return whole_step(video, lengths, enc_weight, dec_weight, cotangent)
    frames = video.shape[1]
    first_frame = lax.axis_index("tm") * frames
    tpos = first_frame + jnp.arange(frames, dtype=jnp.int32)
    keep = (tpos[None, :] < lengths[:, None])[:, :, None, None, None]
    masked = jnp.where(keep, video, jnp.zeros_like(video))
    cot_masked = jnp.where(keep, cotangent, jnp.zeros_like(cotangent))
    ext_x = with_earlier(masked)
    pre = apply_taps(ext_x, enc_weight)
    hidden = jax.nn.silu(pre).astype(jnp.bfloat16)
    ext_h = with_earlier(hidden)
    output = (apply_taps(ext_h, dec_weight) + masked.astype(jnp.float32)).astype(jnp.bfloat16)
    ext_g = with_later(cot_masked)
    chans = dec_weight.shape[3]
    flipped = jnp.transpose(dec_weight[::-1, ::-1, ::-1], (0, 1, 3, 2, 4)).reshape(3, 3, chans, -1)
    dec_local = tap_grads(ext_h, cot_masked)
    back = apply_taps(ext_g, flipped, True)
    dpre = (back * dsilu(pre)).astype(jnp.bfloat16)
    enc_local = tap_grads(ext_x, dpre)
    enc_grad, dec_grad = sum_all(enc_local), sum_all(dec_local)
    return (output, enc_grad, dec_grad)


def solution(mesh):
    in_specs = (
        P("dp", "tm", "height", None, None),
        P("dp"),
        P(),
        P(),
        P("dp", "tm", "height", None, None),
    )
    out_specs = (P("dp", "tm", "height", None, None), P(), P())
    return jax.shard_map(shards, mesh=mesh, in_specs=in_specs, out_specs=out_specs, check_vma=False)
```
